32 devices in a mesh: batch: 2 (over core), seq: 16 (over z, y, x).
Axes of the slice: x: 2, y: 2, z: 4, core: 2. Of those that a mesh axis runs over, the one named last changes fastest.
Arguments:
- tokens: bfloat16 [4, 2048, 768], P('batch', 'seq'), may hold values from -6 to 6
- doc_lengths: int32 [4, 8], P('batch'), may hold values from 0 to 2048, as said below
- query_weight: bfloat16 [768, 768], P(('batch', 'seq')), may hold values from -0.21875 to 0.21875
- query_bias: bfloat16 [768], P(('batch', 'seq')), may hold values from -3 to 3
- key_weight: bfloat16 [768, 768], P(('batch', 'seq')), may hold values from -0.21875 to 0.21875
- value_weight: bfloat16 [768, 768], P(('batch', 'seq')), may hold values from -0.21875 to 0.21875
- value_bias: bfloat16 [768], P(('batch', 'seq')), may hold values from -0.59765625 to 0.59765625
- output_weight: bfloat16 [768, 768], P(('batch', 'seq')), may hold values from -1.75 to 1.75
- output_bias: bfloat16 [768], P(('batch', 'seq')), may hold values from -2 to 2
- attn_gain: bfloat16 [768], P(('batch', 'seq')), may hold values from 0.25 to 1.75
- attn_shift: bfloat16 [768], P(('batch', 'seq')), may hold values from -2 to 2
- up_weight: bfloat16 [768, 3072], P(('batch', 'seq')), may hold values from -0.21875 to 0.21875
- up_bias: bfloat16 [3072], P(('batch', 'seq')), may hold values from -2 to 2
- down_weight: bfloat16 [3072, 768], P(('batch', 'seq')), may hold values from -0.109375 to 0.109375
- down_bias: bfloat16 [768], P(('batch', 'seq')), may hold values from -2 to 2
- ffn_gain: bfloat16 [768], P(('batch', 'seq')), may hold values from 0.25 to 1.75
- ffn_shift: bfloat16 [768], P(('batch', 'seq')), may hold values from -2 to 2
- cotangent: bfloat16 [4, 2048, 768], P('batch', 'seq'), may hold values from -6 to 6
Outputs:
- mixed: bfloat16 [4, 2048, 768], P('batch', 'seq')
- grad_tokens: float32 [4, 2048, 768], P('batch', 'seq')
- grad_query_weight: float32 [768, 768], P(('batch', 'seq'))
- grad_query_bias: float32 [768], P(('batch', 'seq'))
- grad_key_weight: float32 [768, 768], P(('batch', 'seq'))
- grad_value_weight: float32 [768, 768], P(('batch', 'seq'))
- grad_value_bias: float32 [768], P(('batch', 'seq'))
- grad_output_weight: float32 [768, 768], P(('batch', 'seq'))
- grad_output_bias: float32 [768], P(('batch', 'seq'))
- grad_attn_gain: float32 [768], P(('batch', 'seq'))
- grad_attn_shift: float32 [768], P(('batch', 'seq'))
- grad_up_weight: float32 [768, 3072], P(('batch', 'seq'))
- grad_up_bias: float32 [3072], P(('batch', 'seq'))
- grad_down_weight: float32 [3072, 768], P(('batch', 'seq'))
- grad_down_bias: float32 [768], P(('batch', 'seq'))
- grad_ffn_gain: float32 [768], P(('batch', 'seq'))
- grad_ffn_shift: float32 [768], P(('batch', 'seq'))
The draws below stay inside these ranges and needn't reach their ends.
Inputs may be any that keep to these rules, and one draw needn't show every extreme that they name: Each row of doc_lengths sums to 2048; a document may be empty.
All inputs are finite; a program needn't handle non-finite values.
Results may differ from the reference program's by a relative error of at most 0.014.
Values may be sent and summed in bfloat16 or wider, within the bound.
No kernel may reach another device: no remote copies, remote signals or barrier semaphores. Data moves between devices by JAX's collectives and lax.ppermute only.
A program may use at most 192 MiB of HBM per device.

```python
from functools import partial
import jax
import jax.numpy as jnp
from jax import lax

D = 768
HEADS = 12
HEAD_DIM = 64
FF = 3072
DOCS = 8
SEQS_GRP = 2
STRETCH = 128
LENGTH = 2048
SEQS = 4


def draw_doc_lengths(key, part):
    key = jax.random.fold_in(key, 11)
    key_spread, key_head, key_tail, key_pick, key_full = jax.random.split(key, 5)
    spread_cuts = jax.random.randint(key_spread, (SEQS, DOCS - 1), 0, LENGTH + 1)
    head_cuts = jax.random.randint(key_head, (SEQS, DOCS - 1), 0, STRETCH // 2 + 1)
    tail_cuts = LENGTH - jax.random.randint(key_tail, (SEQS, DOCS - 1), 0, STRETCH // 2 + 1)
    early_cut = jnp.arange(DOCS - 1) < (DOCS - 1) // 2
    edge_cuts = jnp.where(early_cut[None, :], head_cuts, tail_cuts)
    chosen = jax.random.randint(key_pick, (SEQS // SEQS_GRP,), 0, SEQS_GRP)
    row_ids = jnp.arange(SEQS)
    spanning = row_ids % SEQS_GRP == chosen[row_ids // SEQS_GRP]
    full_row = jax.random.randint(key_full, (), 0, SEQS)
    cut_points = jnp.where(spanning[:, None], edge_cuts, spread_cuts)
    cut_points = jnp.where((row_ids == full_row)[:, None], jnp.zeros_like(cut_points), cut_points)
    cut_points = jnp.sort(cut_points, axis=1)
    boundaries = jnp.concatenate([jnp.zeros((SEQS, 1), jnp.int32), cut_points.astype(jnp.int32), jnp.full((SEQS, 1), LENGTH, jnp.int32)], axis=1)
    return (boundaries[:, 1:] - boundaries[:, :-1]).astype(jnp.int32)


def shard_levels(stream_key, shape, cuts, smallest, top_value):
    gain = 1.0
    for dim, blocks in cuts:
        steps = jax.random.uniform(jax.random.fold_in(jax.random.fold_in(stream_key, 6), dim), (blocks,), jnp.float32, smallest / len(cuts), top_value / len(cuts))
        gain = gain * jnp.repeat(jnp.exp(steps), shape[dim] // blocks).reshape((-1,) + (1,) * (len(shape) - 1 - dim))
    return gain


def noise(key, extent, scale, most, shards=(), kind=jnp.bfloat16):
    array = jax.random.normal(key, extent, jnp.float32) * scale
    if len(shards) > 0:
        array = shard_levels(key, extent, shards, -0.22, 0.18) * array
    return jnp.clip(array, min=-most, max=most).astype(kind)


def setup_inputs(seed: int = 0) -> dict:
    arg_keys = jax.random.split(jax.random.key(seed), 19)
    tokens = noise(arg_keys[0], (SEQS, LENGTH, D), 1.0, 6.0, ((0, 2), (1, 16)))
    doc_lengths = draw_doc_lengths(jax.random.fold_in(arg_keys[18], 71), 0)
    query_weight = noise(arg_keys[2], (D, D), D ** -0.5, 0.21875, ((0, 32),))
    query_bias = noise(arg_keys[3], (D,), 0.5, 3.0, ((0, 32),))
    key_weight = noise(arg_keys[4], (D, D), D ** -0.5, 0.21875, ((0, 32),))
    value_weight = noise(arg_keys[5], (D, D), D ** -0.5, 0.21875, ((0, 32),))
    value_bias = noise(arg_keys[6], (D,), 0.1, 0.59765625, ((0, 32),))
    output_weight = noise(arg_keys[7], (D, D), (D // 64) ** -0.5, 1.75, ((0, 32),))
    output_bias = noise(arg_keys[8], (D,), 0.3, 2.0, ((0, 32),))
    attn_gain = jnp.clip(1.0 + 0.15 * jax.random.normal(arg_keys[9], (D,), jnp.float32), 0.25, 1.75).astype(jnp.bfloat16)
    attn_shift = noise(arg_keys[10], (D,), 0.3, 2.0, ((0, 32),))
    up_weight = noise(arg_keys[11], (D, FF), D ** -0.5, 0.21875, ((0, 32),))
    up_bias = noise(arg_keys[12], (FF,), 0.3, 2.0, ((0, 32),))
    down_weight = noise(arg_keys[13], (FF, D), FF ** -0.5, 0.109375, ((0, 32),))
    down_bias = noise(arg_keys[14], (D,), 0.3, 2.0, ((0, 32),))
    ffn_gain = jnp.clip(1.0 + 0.15 * jax.random.normal(arg_keys[15], (D,), jnp.float32), 0.25, 1.75).astype(jnp.bfloat16)
    ffn_shift = noise(arg_keys[16], (D,), 0.3, 2.0, ((0, 32),))
    cotangent = noise(arg_keys[17], (SEQS, LENGTH, D), 1.0, 6.0, ((0, 2), (1, 16)))
    return {"tokens": tokens, "doc_lengths": doc_lengths, "query_weight": query_weight, "query_bias": query_bias, "key_weight": key_weight, "value_weight": value_weight, "value_bias": value_bias, "output_weight": output_weight, "output_bias": output_bias, "attn_gain": attn_gain, "attn_shift": attn_shift, "up_weight": up_weight, "up_bias": up_bias, "down_weight": down_weight, "down_bias": down_bias, "ffn_gain": ffn_gain, "ffn_shift": ffn_shift, "cotangent": cotangent}


HIGH = lax.Precision.HIGHEST
NEG = -1e+30
EPS = 1e-12

@jax.custom_vjp
def low(v):
    return lax.optimization_barrier(v.astype(jnp.bfloat16)).astype(jnp.float32)

@jax.custom_vjp
def low_back(v):
    return v

def low_keep(v):
    return (low(v), None)

def low_pass(kept, grad):
    return (grad,)

def back_keep(v):
    return (v, None)

def back_low(kept, grad):
    return (low(grad),)
low.defvjp(low_keep, low_pass)
low_back.defvjp(back_keep, back_low)

def rounded_both(matrix):
    return low(low_back(matrix))

def norm_apply(hidden, gain_vec, shift_vec):
    center = lax.optimization_barrier(jnp.mean(hidden, axis=-1, keepdims=True))
    centered = hidden - center
    spread = lax.optimization_barrier(jnp.mean(centered * centered, axis=-1, keepdims=True))
    return centered * lax.rsqrt(spread + EPS) * gain_vec + shift_vec

def matmul_high(left_op, right_op):
    return jnp.dot(left_op, right_op, precision=HIGH)

def segment_ids(doc_lengths, positions):
    doc_ends = jnp.cumsum(doc_lengths, axis=-1)
    return lax.optimization_barrier(jnp.sum((positions[None, :, None] >= doc_ends[:, None, :]).astype(jnp.int32), axis=-1))

def head_attend(pieces, same_doc):
    query_head, key_head, value_head = pieces
    raw_scores = jnp.einsum('sqd,skd->sqk', query_head, key_head, precision=HIGH)
    scores = low_back(jnp.where(same_doc, HEAD_DIM ** (-0.5) * raw_scores, NEG))
    top_score = lax.optimization_barrier(jnp.max(scores, axis=-1, keepdims=True))
    exponent = jnp.exp(scores - top_score)
    probs = exponent / lax.optimization_barrier(jnp.sum(exponent, axis=-1, keepdims=True))
    return jnp.einsum('sqk,skd->sqd', low(probs), value_head, precision=HIGH)

def layer(params, pieces):
    query_weight, query_bias, key_weight, value_weight, value_bias, output_weight, output_bias, attn_gain, attn_shift, up_weight, up_bias, down_weight, down_bias, ffn_gain, ffn_shift = params
    group_tokens, group_seg = pieces
    group_count = group_tokens.shape[0]
    token_rows = group_tokens.reshape(group_count * LENGTH, D)
    queries = rounded_both(matmul_high(token_rows, query_weight) + query_bias)
    keys_all = rounded_both(matmul_high(token_rows, key_weight))
    values_all = rounded_both(matmul_high(token_rows, value_weight) + value_bias)
    same_doc = group_seg[:, :, None] == group_seg[:, None, :]

    def split_heads(matrix):
        return matrix.reshape(group_count, LENGTH, HEADS, HEAD_DIM).transpose(2, 0, 1, 3)
    attend = partial(jax.checkpoint(head_attend), same_doc=same_doc)
    context = lax.map(attend, (split_heads(queries), split_heads(keys_all), split_heads(values_all)))
    context = rounded_both(context.transpose(1, 2, 0, 3).reshape(group_count * LENGTH, D))
    res_one = token_rows + low_back(matmul_high(context, output_weight) + output_bias)
    normed = norm_apply(res_one, attn_gain, attn_shift)
    up_pre = low_back(matmul_high(low(normed), up_weight) + up_bias)
    activated = low(jax.nn.gelu(up_pre, approximate=False))
    res_two = normed + low_back(matmul_high(activated, down_weight) + down_bias)
    return norm_apply(res_two, ffn_gain, ffn_shift).reshape(group_count, LENGTH, D)

def forward(tokens, params, seg_all):
    grouped = tokens.reshape(SEQS // SEQS_GRP, SEQS_GRP, LENGTH, D)
    seg_grouped = seg_all.reshape(SEQS // SEQS_GRP, SEQS_GRP, LENGTH)
    stepper = partial(jax.checkpoint(layer), params)
    result = lax.map(stepper, (grouped, seg_grouped))
    return result.reshape(SEQS, LENGTH, D)

def reference(tokens, doc_lengths, query_weight, query_bias, key_weight, value_weight, value_bias, output_weight, output_bias, attn_gain, attn_shift, up_weight, up_bias, down_weight, down_bias, ffn_gain, ffn_shift, cotangent):
    params = (query_weight, query_bias, key_weight, value_weight, value_bias, output_weight, output_bias, attn_gain, attn_shift, up_weight, up_bias, down_weight, down_bias, ffn_gain, ffn_shift)
    params = tuple((item.astype(jnp.float32) for item in params))
    seg_all = segment_ids(doc_lengths, jnp.arange(LENGTH, dtype=jnp.int32))
    output, pull = jax.vjp(partial(forward, seg_all=seg_all), tokens.astype(jnp.float32), params)
    grad_input, grads = pull(cotangent.astype(jnp.float32))
    return (output.astype(jnp.bfloat16), grad_input, grads[0], grads[1], grads[2], grads[3], grads[4], grads[5], grads[6], grads[7], grads[8], grads[9], grads[10], grads[11], grads[12], grads[13], grads[14])
```

```python
import jax
import jax.numpy as jnp
from jax import lax
from jax.experimental import pallas as pl
from jax.experimental.pallas import tpu as pltpu
from jax.sharding import PartitionSpec as P

HEADS = 12
HEAD_DIM = 64


SCALE = 0.125
NEG = -1e30
EPS = 1e-12


def norm_apply(hidden, gain_vec, shift_vec):
    center = jnp.mean(hidden, axis=-1, keepdims=True)
    centered = hidden - center
    spread = jnp.mean(centered * centered, axis=-1, keepdims=True)
    return centered * lax.rsqrt(spread + EPS) * gain_vec + shift_vec


def gelu_exact(inputs):
    return jax.nn.gelu(inputs, approximate=False)


def segment_ids(doc_lengths, positions):
    doc_ends = jnp.cumsum(doc_lengths, axis=-1)
    return jnp.sum((positions[None, :, None] >= doc_ends[:, None, :]).astype(jnp.int32), axis=-1)


def matmul_plain(left_op, right_op):
    return jnp.dot(left_op, right_op, preferred_element_type=jnp.float32)


def matmul_right_t(left_op, right_op):
    return lax.dot_general(
        left_op, right_op, (((1,), (1,)), ((), ())), preferred_element_type=jnp.float32
    )


def matmul_left_t(left_op, right_op):
    return lax.dot_general(
        left_op, right_op, (((0,), (0,)), ((), ())), preferred_element_type=jnp.float32
    )


def column_sums(matrix):
    return jnp.sum(matrix.astype(jnp.float32), axis=0)


def head_block(matrix, head_pair):
    pair_width = 2 * HEAD_DIM
    column_block = matrix[..., head_pair * pair_width : (head_pair + 1) * pair_width]
    return column_block.reshape(column_block.shape[:-1] + (2, HEAD_DIM))


def merge_heads(blocks):
    return jnp.concatenate(
        [block_item.reshape(block_item.shape[:2] + (2 * HEAD_DIM,)) for block_item in blocks],
        axis=-1,
    )


def stat_pair(stats, head_pair):
    return stats[:, 2 * head_pair : 2 * head_pair + 2][..., None]


def pair_scores(query_pair, key_pair, same_doc):
    raw_scores = jnp.einsum(
        "sqhd,skhd->shqk", query_pair, key_pair, preferred_element_type=jnp.float32
    )
    return jnp.where(same_doc[:, None], SCALE * raw_scores, NEG)


def attend_forward(queries, key_all, value_all, same_doc):
    outputs, log_sums = ([], [])
    for head_pair in range(HEADS // 2):
        scores = pair_scores(
            head_block(queries, head_pair), head_block(key_all, head_pair), same_doc
        )
        top_score = jnp.max(scores, axis=-1, keepdims=True)
        exponent = jnp.exp(scores - top_score)
        totals = jnp.sum(exponent, axis=-1, keepdims=True)
        probs_low = (exponent / totals).astype(jnp.bfloat16)
        context = jnp.einsum(
            "shqk,skhd->sqhd",
            probs_low,
            head_block(value_all, head_pair),
            preferred_element_type=jnp.float32,
        )
        outputs.append(context)
        log_sums.append((top_score + jnp.log(totals))[..., 0])
    return (merge_heads(outputs), jnp.concatenate(log_sums, axis=1))


def attend_backward(queries, key_all, value_all, same_doc, log_sums, grad_context):
    query_grads, key_grads, value_grads, row_dots = ([], [], [], [])
    for head_pair in range(HEADS // 2):
        query_pair = head_block(queries, head_pair)
        key_pair = head_block(key_all, head_pair)
        grad_pair = head_block(grad_context, head_pair)
        probs = jnp.exp(
            pair_scores(query_pair, key_pair, same_doc) - stat_pair(log_sums, head_pair)
        )
        grad_probs = jnp.einsum(
            "sqhd,skhd->shqk",
            grad_pair,
            head_block(value_all, head_pair),
            preferred_element_type=jnp.float32,
        )
        row_dot = jnp.sum(probs * grad_probs, axis=-1, keepdims=True)
        row_dots.append(row_dot[..., 0])
        grad_scores = (probs * (grad_probs - row_dot)).astype(jnp.bfloat16) * jnp.bfloat16(SCALE)
        query_grads.append(
            jnp.einsum("shqk,skhd->sqhd", grad_scores, key_pair, preferred_element_type=jnp.float32)
        )
    return (merge_heads(query_grads), jnp.concatenate(row_dots, axis=1), None, None)


def key_side_local(query_all, grad_ctx_all, lse_all, rowdot_all, keys_own, values_own, same_doc_t):
    key_grads, value_grads = ([], [])
    for head_pair in range(HEADS // 2):
        query_pair = head_block(query_all, head_pair)
        grad_pair = head_block(grad_ctx_all, head_pair)
        probs = jnp.exp(
            pair_scores(query_pair, head_block(keys_own, head_pair), same_doc_t)
            - stat_pair(lse_all, head_pair)
        )
        grad_probs = jnp.einsum(
            "sqhd,skhd->shqk",
            grad_pair,
            head_block(values_own, head_pair),
            preferred_element_type=jnp.float32,
        )
        grad_scores = (probs * (grad_probs - stat_pair(rowdot_all, head_pair))).astype(
            jnp.bfloat16
        ) * jnp.bfloat16(SCALE)
        key_grads.append(
            jnp.einsum(
                "shqk,sqhd->skhd", grad_scores, query_pair, preferred_element_type=jnp.float32
            )
        )
        value_grads.append(
            jnp.einsum(
                "shqk,sqhd->skhd",
                probs.astype(jnp.bfloat16),
                grad_pair,
                preferred_element_type=jnp.float32,
            )
        )
    return (merge_heads(key_grads), merge_heads(value_grads))


def shards_general(
    tokens,
    doc_lengths,
    query_weight,
    query_bias,
    key_weight,
    value_weight,
    value_bias,
    output_weight,
    output_bias,
    attn_gain,
    attn_shift,
    up_weight,
    up_bias,
    down_weight,
    down_bias,
    ffn_gain,
    ffn_shift,
    cotangent,
):
    gathered = (
        lax.all_gather(query_weight, ("batch", "seq"), axis=0, tiled=True),
        lax.all_gather(query_bias, ("batch", "seq"), axis=0, tiled=True),
        lax.all_gather(key_weight, ("batch", "seq"), axis=0, tiled=True),
        lax.all_gather(value_weight, ("batch", "seq"), axis=0, tiled=True),
        lax.all_gather(value_bias, ("batch", "seq"), axis=0, tiled=True),
        lax.all_gather(output_weight, ("batch", "seq"), axis=0, tiled=True),
        lax.all_gather(output_bias, ("batch", "seq"), axis=0, tiled=True),
        lax.all_gather(attn_gain, ("batch", "seq"), axis=0, tiled=True),
        lax.all_gather(attn_shift, ("batch", "seq"), axis=0, tiled=True),
        lax.all_gather(up_weight, ("batch", "seq"), axis=0, tiled=True),
        lax.all_gather(up_bias, ("batch", "seq"), axis=0, tiled=True),
        lax.all_gather(down_weight, ("batch", "seq"), axis=0, tiled=True),
        lax.all_gather(down_bias, ("batch", "seq"), axis=0, tiled=True),
        lax.all_gather(ffn_gain, ("batch", "seq"), axis=0, tiled=True),
        lax.all_gather(ffn_shift, ("batch", "seq"), axis=0, tiled=True),
    )
    (
        query_full,
        qbias_full,
        key_full,
        value_full,
        vbias_full,
        output_full,
        obias_full,
        again_full,
        ashift_full,
        up_full,
        ubias_full,
        down_full,
        dbias_full,
        fgain_full,
        fshift_full,
    ) = gathered
    seq_groups, stretch_len, width = tokens.shape
    row_count = seq_groups * stretch_len
    token_rows = tokens.reshape(row_count, width)
    positions = lax.axis_index("seq") * stretch_len + jnp.arange(stretch_len, dtype=jnp.int32)
    total_len = stretch_len * lax.axis_size("seq")
    query_seg = segment_ids(doc_lengths, positions)
    key_seg = segment_ids(doc_lengths, jnp.arange(total_len, dtype=jnp.int32))
    same_doc = query_seg[:, :, None] == key_seg[:, None, :]
    queries = (
        (matmul_plain(token_rows, query_full) + qbias_full)
        .astype(jnp.bfloat16)
        .reshape(tokens.shape)
    )
    keys_local = matmul_plain(token_rows, key_full).astype(jnp.bfloat16).reshape(tokens.shape)
    values_local = (
        (matmul_plain(token_rows, value_full) + vbias_full)
        .astype(jnp.bfloat16)
        .reshape(tokens.shape)
    )
    key_all, value_all = (
        lax.all_gather(keys_local, "seq", axis=1, tiled=True),
        lax.all_gather(values_local, "seq", axis=1, tiled=True),
    )
    context, log_sums = attend_forward(queries, key_all, value_all, same_doc)
    context_low = context.reshape(row_count, width).astype(jnp.bfloat16)
    res_one = token_rows.astype(jnp.float32) + matmul_plain(context_low, output_full) + obias_full
    normed, pull_one = jax.vjp(
        norm_apply, res_one, again_full.astype(jnp.float32), ashift_full.astype(jnp.float32)
    )
    normed_low = normed.astype(jnp.bfloat16)
    up_pre = matmul_plain(normed_low, up_full) + ubias_full
    activated, pull_gelu = jax.vjp(gelu_exact, up_pre)
    act_low = activated.astype(jnp.bfloat16)
    res_two = normed + matmul_plain(act_low, down_full) + dbias_full
    output_rows, pull_two = jax.vjp(
        norm_apply, res_two, fgain_full.astype(jnp.float32), fshift_full.astype(jnp.float32)
    )
    mixed = output_rows.astype(jnp.bfloat16).reshape(tokens.shape)
    regathered = (
        lax.all_gather(query_weight, ("batch", "seq"), axis=0, tiled=True),
        lax.all_gather(query_bias, ("batch", "seq"), axis=0, tiled=True),
        lax.all_gather(key_weight, ("batch", "seq"), axis=0, tiled=True),
        lax.all_gather(value_weight, ("batch", "seq"), axis=0, tiled=True),
        lax.all_gather(value_bias, ("batch", "seq"), axis=0, tiled=True),
        lax.all_gather(output_weight, ("batch", "seq"), axis=0, tiled=True),
        lax.all_gather(output_bias, ("batch", "seq"), axis=0, tiled=True),
        lax.all_gather(attn_gain, ("batch", "seq"), axis=0, tiled=True),
        lax.all_gather(attn_shift, ("batch", "seq"), axis=0, tiled=True),
        lax.all_gather(up_weight, ("batch", "seq"), axis=0, tiled=True),
        lax.all_gather(up_bias, ("batch", "seq"), axis=0, tiled=True),
        lax.all_gather(down_weight, ("batch", "seq"), axis=0, tiled=True),
        lax.all_gather(down_bias, ("batch", "seq"), axis=0, tiled=True),
        lax.all_gather(ffn_gain, ("batch", "seq"), axis=0, tiled=True),
        lax.all_gather(ffn_shift, ("batch", "seq"), axis=0, tiled=True),
    )
    query_back = regathered[0]
    key_back = regathered[2]
    value_back = regathered[3]
    output_back = regathered[5]
    up_back = regathered[9]
    down_back = regathered[11]
    grad_out = cotangent.astype(jnp.float32).reshape(row_count, width)
    grad_res_two, grad_ffn_gain, grad_ffn_shift = pull_two(grad_out)
    grad_down_low = grad_res_two.astype(jnp.bfloat16)
    grad_down_weight = matmul_left_t(act_low, grad_down_low)
    grad_down_bias = column_sums(grad_down_low)
    (grad_up_pre,) = pull_gelu(matmul_right_t(grad_down_low, down_back))
    grad_up_low = grad_up_pre.astype(jnp.bfloat16)
    grad_up_weight = matmul_left_t(normed_low, grad_up_low)
    grad_up_bias = column_sums(grad_up_low)
    grad_normed = grad_res_two + matmul_right_t(grad_up_low, up_back)
    grad_res_one, grad_attn_gain, grad_attn_shift = pull_one(grad_normed)
    grad_branch_low = grad_res_one.astype(jnp.bfloat16)
    grad_output_weight = matmul_left_t(context_low, grad_branch_low)
    grad_output_bias = column_sums(grad_branch_low)
    grad_context = (
        matmul_right_t(grad_branch_low, output_back).astype(jnp.bfloat16).reshape(tokens.shape)
    )
    key_again, value_again = (
        lax.all_gather(keys_local, "seq", axis=1, tiled=True),
        lax.all_gather(values_local, "seq", axis=1, tiled=True),
    )
    grad_query, row_dots, unused_key, unused_value = attend_backward(
        queries, key_again, value_again, same_doc, log_sums, grad_context
    )
    query_all, grad_ctx_all = (
        lax.all_gather(queries, "seq", axis=1, tiled=True),
        lax.all_gather(grad_context, "seq", axis=1, tiled=True),
    )
    lse_all, rowdot_all = (
        lax.all_gather(log_sums, "seq", axis=2, tiled=True),
        lax.all_gather(row_dots, "seq", axis=2, tiled=True),
    )
    same_doc_t = key_seg[:, :, None] == query_seg[:, None, :]
    grad_key, grad_value = key_side_local(
        query_all, grad_ctx_all, lse_all, rowdot_all, keys_local, values_local, same_doc_t
    )
    grad_query_low = grad_query.reshape(row_count, width).astype(jnp.bfloat16)
    grad_key_low = grad_key.reshape(row_count, width).astype(jnp.bfloat16)
    grad_value_low = grad_value.reshape(row_count, width).astype(jnp.bfloat16)
    grad_query_weight = matmul_left_t(token_rows, grad_query_low)
    grad_query_bias = column_sums(grad_query_low)
    grad_key_weight = matmul_left_t(token_rows, grad_key_low)
    grad_value_weight = matmul_left_t(token_rows, grad_value_low)
    grad_value_bias = column_sums(grad_value_low)
    grad_tokens = (
        grad_res_one
        + matmul_right_t(grad_query_low, query_back)
        + matmul_right_t(grad_key_low, key_back)
        + matmul_right_t(grad_value_low, value_back)
    )
    summed = (
        lax.psum_scatter(grad_query_weight, ("batch", "seq"), scatter_dimension=0, tiled=True),
        lax.psum_scatter(grad_query_bias, ("batch", "seq"), scatter_dimension=0, tiled=True),
        lax.psum_scatter(grad_key_weight, ("batch", "seq"), scatter_dimension=0, tiled=True),
        lax.psum_scatter(grad_value_weight, ("batch", "seq"), scatter_dimension=0, tiled=True),
        lax.psum_scatter(grad_value_bias, ("batch", "seq"), scatter_dimension=0, tiled=True),
        lax.psum_scatter(grad_output_weight, ("batch", "seq"), scatter_dimension=0, tiled=True),
        lax.psum_scatter(grad_output_bias, ("batch", "seq"), scatter_dimension=0, tiled=True),
        lax.psum_scatter(grad_attn_gain, ("batch", "seq"), scatter_dimension=0, tiled=True),
        lax.psum_scatter(grad_attn_shift, ("batch", "seq"), scatter_dimension=0, tiled=True),
        lax.psum_scatter(grad_up_weight, ("batch", "seq"), scatter_dimension=0, tiled=True),
        lax.psum_scatter(grad_up_bias, ("batch", "seq"), scatter_dimension=0, tiled=True),
        lax.psum_scatter(grad_down_weight, ("batch", "seq"), scatter_dimension=0, tiled=True),
        lax.psum_scatter(grad_down_bias, ("batch", "seq"), scatter_dimension=0, tiled=True),
        lax.psum_scatter(grad_ffn_gain, ("batch", "seq"), scatter_dimension=0, tiled=True),
        lax.psum_scatter(grad_ffn_shift, ("batch", "seq"), scatter_dimension=0, tiled=True),
    )
    return (
        mixed,
        grad_tokens.reshape(tokens.shape),
        summed[0],
        summed[1],
        summed[2],
        summed[3],
        summed[4],
        summed[5],
        summed[6],
        summed[7],
        summed[8],
        summed[9],
        summed[10],
        summed[11],
        summed[12],
        summed[13],
        summed[14],
    )


LOG2E = 1.4426950408889634
GROUP_HEADS = 3
GROUP_COLS = GROUP_HEADS * HEAD_DIM
PACK = 640
VECS = 12
KEY_CHUNK = 512


def dot_nt(left_op, right_op):
    return lax.dot_general(
        left_op, right_op, (((1,), (1,)), ((), ())), preferred_element_type=jnp.float32
    )


def dot_nn(left_op, right_op):
    return lax.dot_general(
        left_op, right_op, (((1,), (0,)), ((), ())), preferred_element_type=jnp.float32
    )


def attend_kernel(
    query_ref, own_ref, other_ref, seg_key_ref, seg_query_ref, ctx_ref, lse_ref, value_t
):
    half = own_ref.shape[0]
    rows = query_ref.shape[0]

    @pl.when(pl.program_id(0) == 0)
    def _():
        value_t[:, :half] = own_ref[:, GROUP_COLS : 2 * GROUP_COLS].T
        value_t[:, half:] = other_ref[:, GROUP_COLS : 2 * GROUP_COLS].T

    seg_query = seg_query_ref[...]
    chunks = [
        (ref, start) for ref in (own_ref, other_ref) for start in range(0, half, KEY_CHUNK)
    ]
    for head in range(GROUP_HEADS):
        cols = slice(head * HEAD_DIM, (head + 1) * HEAD_DIM)
        query = query_ref[:, cols]
        scores = []
        top = None
        for number, (ref, start) in enumerate(chunks):
            raw = dot_nt(ref[start : start + KEY_CHUNK, cols], query)
            seg_key = seg_key_ref[number * KEY_CHUNK : (number + 1) * KEY_CHUNK, :]
            seg_key = jnp.concatenate([seg_key] * (rows // 128), axis=1)
            masked = jnp.where(seg_key == seg_query, raw * (SCALE * LOG2E), NEG)
            scores.append(masked)
            peak = jnp.max(masked, axis=0, keepdims=True)
            top = peak if top is None else jnp.maximum(top, peak)
        total = None
        context_t = None
        for number in range(len(chunks)):
            weight = jnp.exp2(scores[number] - top)
            part = jnp.sum(weight, axis=0, keepdims=True)
            piece = dot_nn(
                value_t[cols, number * KEY_CHUNK : (number + 1) * KEY_CHUNK],
                weight.astype(jnp.bfloat16),
            )
            total = part if total is None else total + part
            context_t = piece if context_t is None else context_t + piece
        ctx_ref[:, cols] = (context_t / total).T
        lse_ref[head : head + 1, :] = top + jnp.log2(total)


def attend(query, own, other, seg_key, seg_query):
    rows = query.shape[0]
    half = own.shape[0]
    block = rows // 4
    return pl.pallas_call(
        attend_kernel,
        grid=(4,),
        in_specs=[
            pl.BlockSpec((block, GROUP_COLS), lambda i: (i, 0)),
            pl.BlockSpec((half, 2 * GROUP_COLS), lambda i: (0, 0)),
            pl.BlockSpec((half, 2 * GROUP_COLS), lambda i: (0, 0)),
            pl.BlockSpec((2 * half, 128), lambda i: (0, 0)),
            pl.BlockSpec((1, block), lambda i: (0, i)),
        ],
        out_specs=[
            pl.BlockSpec((block, GROUP_COLS), lambda i: (i, 0)),
            pl.BlockSpec((8, block), lambda i: (0, i)),
        ],
        out_shape=[
            jax.ShapeDtypeStruct((rows, GROUP_COLS), jnp.float32),
            jax.ShapeDtypeStruct((8, rows), jnp.float32),
        ],
        scratch_shapes=[pltpu.VMEM((GROUP_COLS, 2 * half), jnp.bfloat16)],
        compiler_params=pltpu.CompilerParams(vmem_limit_bytes=48 * 1024 * 1024),
        cost_estimate=pl.CostEstimate(
            flops=16 * rows * half * GROUP_COLS,
            bytes_accessed=4 * 1024 * 1024,
            transcendentals=2 * GROUP_HEADS * rows * half,
        ),
        name="attend",
    )(query, own, other, seg_key, seg_query)


def attend_back_kernel(
    query_ref,
    grad_ref,
    ctx_ref,
    lse_ref,
    own_ref,
    other_ref,
    seg_key_ref,
    seg_query_ref,
    gquery_ref,
    gown_ref,
    gother_ref,
    key_t,
):
    half = own_ref.shape[0]
    rows = query_ref.shape[0]
    first = pl.program_id(0) == 0

    @pl.when(first)
    def _():
        key_t[:, :half] = own_ref[:, :GROUP_COLS].T
        key_t[:, half:] = other_ref[:, :GROUP_COLS].T
        gown_ref[...] = jnp.zeros_like(gown_ref)
        gother_ref[...] = jnp.zeros_like(gother_ref)

    seg_query = seg_query_ref[...]
    chunks = [
        (ref, gref, start)
        for ref, gref in ((own_ref, gown_ref), (other_ref, gother_ref))
        for start in range(0, half, KEY_CHUNK)
    ]
    for head in range(GROUP_HEADS):
        cols = slice(head * HEAD_DIM, (head + 1) * HEAD_DIM)
        vcols = slice(GROUP_COLS + head * HEAD_DIM, GROUP_COLS + (head + 1) * HEAD_DIM)
        query = query_ref[:, cols]
        grad = grad_ref[:, cols]
        lse = lse_ref[head : head + 1, :]
        dots = (grad.astype(jnp.float32) * ctx_ref[:, cols]).T
        row_dot = jnp.sum(dots, axis=0, keepdims=True)
        gquery_t = None
        for number, (ref, gref, start) in enumerate(chunks):
            spot = slice(start, start + KEY_CHUNK)
            raw = dot_nt(ref[spot, cols], query)
            seg_key = seg_key_ref[number * KEY_CHUNK : (number + 1) * KEY_CHUNK, :]
            seg_key = jnp.concatenate([seg_key] * (rows // 128), axis=1)
            masked = jnp.where(seg_key == seg_query, raw * (SCALE * LOG2E), NEG)
            probs = jnp.exp2(masked - lse)
            gprobs = dot_nt(ref[spot, vcols], grad)
            gscores = (probs * (gprobs - row_dot)).astype(jnp.bfloat16)
            gref[spot, vcols] += dot_nn(probs.astype(jnp.bfloat16), grad)
            gref[spot, cols] += dot_nn(gscores, query)
            piece = dot_nn(key_t[cols, number * KEY_CHUNK : (number + 1) * KEY_CHUNK], gscores)
            gquery_t = piece if gquery_t is None else gquery_t + piece
        gquery_ref[:, cols] = (SCALE * gquery_t).T


def attend_back(query, grad, ctx, lse, own, other, seg_key, seg_query):
    rows = query.shape[0]
    half = own.shape[0]
    block = rows // 4
    return pl.pallas_call(
        attend_back_kernel,
        grid=(4,),
        in_specs=[
            pl.BlockSpec((block, GROUP_COLS), lambda i: (i, 0)),
            pl.BlockSpec((block, GROUP_COLS), lambda i: (i, 0)),
            pl.BlockSpec((block, GROUP_COLS), lambda i: (i, 0)),
            pl.BlockSpec((8, block), lambda i: (0, i)),
            pl.BlockSpec((half, 2 * GROUP_COLS), lambda i: (0, 0)),
            pl.BlockSpec((half, 2 * GROUP_COLS), lambda i: (0, 0)),
            pl.BlockSpec((2 * half, 128), lambda i: (0, 0)),
            pl.BlockSpec((1, block), lambda i: (0, i)),
        ],
        out_specs=[
            pl.BlockSpec((block, GROUP_COLS), lambda i: (i, 0)),
            pl.BlockSpec((half, 2 * GROUP_COLS), lambda i: (0, 0)),
            pl.BlockSpec((half, 2 * GROUP_COLS), lambda i: (0, 0)),
        ],
        out_shape=[
            jax.ShapeDtypeStruct((rows, GROUP_COLS), jnp.float32),
            jax.ShapeDtypeStruct((half, 2 * GROUP_COLS), jnp.float32),
            jax.ShapeDtypeStruct((half, 2 * GROUP_COLS), jnp.float32),
        ],
        scratch_shapes=[pltpu.VMEM((GROUP_COLS, 2 * half), jnp.bfloat16)],
        compiler_params=pltpu.CompilerParams(vmem_limit_bytes=48 * 1024 * 1024),
        cost_estimate=pl.CostEstimate(
            flops=40 * rows * half * GROUP_COLS,
            bytes_accessed=10 * 1024 * 1024,
            transcendentals=2 * GROUP_HEADS * rows * half,
        ),
        name="attend_back",
    )(query, grad, ctx, lse, own, other, seg_key, seg_query)


def device_table(mapping):
    pairs = []
    for core in range(2):
        for layer_z in range(4):
            for quad in range(4):
                to_core, to_z, to_quad = mapping(core, layer_z, quad)
                pairs.append((core * 16 + layer_z * 4 + quad, to_core * 16 + to_z * 4 + to_quad))
    return pairs


def hop(value, mapping):
    return lax.ppermute(value, ("batch", "seq"), device_table(mapping))


def hop_quad(value, flip):
    return hop(value, lambda core, layer_z, quad: (core, layer_z, quad ^ flip))


def hop_layer(value, flip):
    return hop(value, lambda core, layer_z, quad: (core, layer_z ^ flip, quad))


def hop_core(value):
    return hop(value, lambda core, layer_z, quad: (1 - core, layer_z, quad))


def to_sequence(value, turn):
    return hop(
        value,
        lambda core, layer_z, quad: (layer_z // 2, 2 * core + (layer_z + turn) % 2, quad),
    )


def to_owner(value, turn):
    return hop(
        value,
        lambda core, layer_z, quad: (layer_z // 2, 2 * core + (layer_z - turn) % 2, quad),
    )


def turned(blocks, quad):
    first, second, third, fourth = blocks
    odd = quad % 2 == 1
    high = quad // 2 == 1
    pairs = (
        jnp.where(odd, second, first),
        jnp.where(odd, first, second),
        jnp.where(odd, fourth, third),
        jnp.where(odd, third, fourth),
    )
    return (
        jnp.where(high, pairs[2], pairs[0]),
        jnp.where(high, pairs[3], pairs[1]),
        jnp.where(high, pairs[0], pairs[2]),
        jnp.where(high, pairs[1], pairs[3]),
    )


def pack_grads(main, vecs):
    coarse = vecs.astype(jnp.bfloat16)
    fine = (vecs - coarse.astype(jnp.float32)).astype(jnp.bfloat16)
    filler = jnp.zeros(main.shape[:-1] + (PACK - main.shape[-1] - 2 * VECS,), jnp.bfloat16)
    return jnp.concatenate([main.astype(jnp.bfloat16), coarse, fine, filler], axis=-1)


def unpack_grads(packed):
    wide = packed.astype(jnp.float32)
    cut = 3 * GROUP_COLS
    return (wide[..., :cut], wide[..., cut : cut + VECS] + wide[..., cut + VECS : cut + 2 * VECS])


def shards_heads(
    tokens,
    doc_lengths,
    query_weight,
    query_bias,
    key_weight,
    value_weight,
    value_bias,
    output_weight,
    output_bias,
    attn_gain,
    attn_shift,
    up_weight,
    up_bias,
    down_weight,
    down_bias,
    ffn_gain,
    ffn_shift,
    cotangent,
):
    groups, stretch, width = tokens.shape
    own_rows = query_weight.shape[0]
    hidden = up_weight.shape[1]
    ratio = hidden // width
    devices = width // own_rows
    bulk_rows = own_rows * (1 + 2 * ratio)
    row_count = groups * stretch
    core = lax.axis_index("batch")
    place = lax.axis_index("seq")
    layer_z = place // 4
    quad = place % 4
    parity = layer_z % 2
    flips = (1, 2, 3)

    with jax.named_scope("tokens_out"):
        arrived = [
            to_sequence(jnp.where((parity + turn) % 2 == 1, tokens[1], tokens[0]), turn)
            for turn in (0, 1)
        ]
        own_block = jnp.concatenate(arrived, axis=0)
        token_half = jnp.concatenate(
            [own_block] + [hop_quad(own_block, flip) for flip in flips], axis=0
        )

    with jax.named_scope("group_weights"):
        coarse_len = (doc_lengths // 64).astype(jnp.bfloat16)
        fine_len = (doc_lengths % 64).astype(jnp.bfloat16)
        digits = jnp.concatenate([coarse_len, fine_len], axis=1)
        digits = jnp.pad(digits, ((0, own_rows - digits.shape[0]), (0, 0)))
        vectors = jnp.stack(
            [
                query_bias,
                value_bias,
                output_bias,
                attn_gain,
                attn_shift,
                down_bias,
                ffn_gain,
                ffn_shift,
            ],
            axis=1,
        )
        extras = jnp.concatenate([vectors, up_bias.reshape(own_rows, ratio), digits], axis=1)
        extras = jnp.pad(extras, ((0, 0), (0, PACK - 3 * GROUP_COLS - extras.shape[1])))
        pieces = [
            jnp.concatenate(
                [
                    item[:, number * GROUP_COLS : (number + 1) * GROUP_COLS]
                    for item in (key_weight, value_weight, query_weight)
                ]
                + [extras],
                axis=1,
            )
            for number in range(4)
        ]
        pieces = turned(pieces, quad)
        quads = turned(
            [pieces[0]] + [hop_quad(pieces[flip], flip) for flip in flips], quad
        )
        quads = jnp.stack(quads, axis=0)
        twin = hop_core(quads)
        cores = jnp.stack([jnp.where(core == 0, quads, twin), jnp.where(core == 0, twin, quads)])
        layers = [cores] + [hop_layer(cores, flip) for flip in flips]
        layers = jnp.stack(turned(layers, layer_z), axis=1)
        packed = layers.reshape(width, PACK)
    group_weight = packed[:, : 3 * GROUP_COLS]
    side = packed[:, 3 * GROUP_COLS :].astype(jnp.float32)
    vector_rows = side[:, :8].T
    up_bias_full = side[:, 8 : 8 + ratio].reshape(1, hidden)
    (
        qbias_full,
        vbias_full,
        obias_full,
        again_full,
        ashift_full,
        dbias_full,
        fgain_full,
        fshift_full,
    ) = [vector_rows[number] for number in range(8)]
    first_digit = 8 + ratio
    docs = doc_lengths.shape[1]
    rows_of_core = side.reshape(2, width // 2, -1)[:, :groups, first_digit : first_digit + 2 * docs]
    lengths_all = (rows_of_core[..., :docs] * 64 + rows_of_core[..., docs:]).astype(jnp.int32)
    lengths = lax.dynamic_index_in_dim(
        lengths_all.reshape(2 * groups, docs), layer_z, axis=0, keepdims=False
    )
    doc_ends = jnp.cumsum(lengths)

    def half_segments(which):
        turn_z = jnp.stack([(layer_z - turn) % 2 for turn in (0, 1)]) + 2 * which
        spot = jnp.stack([quad ^ flip for flip in range(4)])
        start = turn_z[None, :] * (4 * stretch) + spot[:, None] * stretch
        positions = start[:, :, None] + jnp.arange(stretch, dtype=jnp.int32)
        positions = positions.reshape(-1)
        return jnp.sum((positions[:, None] >= doc_ends[None, :]).astype(jnp.int32), axis=-1)

    seg_query = half_segments(core)
    seg_key = jnp.concatenate([seg_query, half_segments(1 - core)])
    seg_key = jnp.broadcast_to(seg_key[:, None], (seg_key.shape[0], 128))
    seg_query = seg_query[None, :]

    bulk = jnp.concatenate(
        [output_weight]
        + [up_weight[:, number * width : (number + 1) * width] for number in range(ratio)]
        + [down_weight],
        axis=0,
    )
    bulk_all = lax.all_gather(bulk, ("batch", "seq"), axis=0, tiled=True)
    bulk_all = bulk_all.reshape(devices, bulk_rows, width)

    with jax.named_scope("projections"):
        column_bias = jnp.concatenate(
            [
                jnp.zeros((GROUP_COLS,), jnp.float32),
                lax.dynamic_slice_in_dim(vbias_full, quad * GROUP_COLS, GROUP_COLS),
                lax.dynamic_slice_in_dim(qbias_full, quad * GROUP_COLS, GROUP_COLS),
            ]
        )
        projected = (matmul_plain(token_half, group_weight) + column_bias).astype(jnp.bfloat16)
        own_pair = projected[:, : 2 * GROUP_COLS]
        queries = projected[:, 2 * GROUP_COLS :]
        other_pair = hop_core(own_pair)
    ctx_wide, lse = attend(queries, own_pair, other_pair, seg_key, seg_query)

    with jax.named_scope("context_home"):
        ctx_blocks = ctx_wide.astype(jnp.bfloat16).reshape(4, row_count, GROUP_COLS)
        ctx_groups = [ctx_blocks[0]] + [hop_quad(ctx_blocks[flip], flip) for flip in flips]
        ctx_merged = jnp.concatenate(turned(ctx_groups, quad), axis=1)
        ctx_turns = [
            to_owner(ctx_merged[turn * stretch : (turn + 1) * stretch], turn) for turn in (0, 1)
        ]
        context_low = jnp.concatenate(
            [
                jnp.where(parity == 0, ctx_turns[0], ctx_turns[1]),
                jnp.where(parity == 0, ctx_turns[1], ctx_turns[0]),
            ],
            axis=0,
        )

    output_full = bulk_all[:, :own_rows].reshape(width, width)
    up_parts = [
        bulk_all[:, (1 + number) * own_rows : (2 + number) * own_rows].reshape(width, width)
        for number in range(ratio)
    ]
    up_full = jnp.concatenate(up_parts, axis=1)
    down_full = bulk_all[:, (1 + ratio) * own_rows :].reshape(hidden, width)

    token_rows = tokens.reshape(row_count, width)
    res_one = token_rows.astype(jnp.float32) + matmul_plain(context_low, output_full) + obias_full
    normed, pull_one = jax.vjp(norm_apply, res_one, again_full, ashift_full)
    normed_low = normed.astype(jnp.bfloat16)
    up_pre = matmul_plain(normed_low, up_full) + up_bias_full
    activated, pull_gelu = jax.vjp(gelu_exact, up_pre)
    act_low = activated.astype(jnp.bfloat16)
    res_two = normed + matmul_plain(act_low, down_full) + dbias_full
    output_rows, pull_two = jax.vjp(norm_apply, res_two, fgain_full, fshift_full)
    mixed = output_rows.astype(jnp.bfloat16).reshape(tokens.shape)
    grad_out = cotangent.astype(jnp.float32).reshape(row_count, width)
    grad_res_two, grad_ffn_gain, grad_ffn_shift = pull_two(grad_out)
    grad_down_low = grad_res_two.astype(jnp.bfloat16)
    (grad_up_pre,) = pull_gelu(matmul_right_t(grad_down_low, down_full))
    grad_up_low = grad_up_pre.astype(jnp.bfloat16)
    grad_normed = grad_res_two + matmul_right_t(grad_up_low, up_full)
    grad_res_one, grad_attn_gain, grad_attn_shift = pull_one(grad_normed)
    grad_branch_low = grad_res_one.astype(jnp.bfloat16)
    grad_context = matmul_right_t(grad_branch_low, output_full).astype(jnp.bfloat16)

    with jax.named_scope("context_grad_out"):
        low_part = grad_context[:stretch]
        high_part = grad_context[stretch:]
        grad_turns = [
            to_sequence(jnp.where((parity + turn) % 2 == 1, high_part, low_part), turn)
            for turn in (0, 1)
        ]
        grad_own = jnp.concatenate(grad_turns, axis=0)
        grad_columns = turned(
            [grad_own[:, n * GROUP_COLS : (n + 1) * GROUP_COLS] for n in range(4)], quad
        )
        grad_ctx = jnp.concatenate(
            [grad_columns[0]] + [hop_quad(grad_columns[flip], flip) for flip in flips], axis=0
        )

    grad_output_weight = matmul_left_t(context_low, grad_branch_low).astype(jnp.bfloat16)
    grad_up_weight = matmul_left_t(normed_low, grad_up_low).astype(jnp.bfloat16)
    grad_down_weight = matmul_left_t(act_low, grad_down_low).astype(jnp.bfloat16)
    bulk_grad = jnp.concatenate(
        [grad_output_weight.reshape(devices, own_rows, width)]
        + [
            grad_up_weight[:, n * width : (n + 1) * width].reshape(devices, own_rows, width)
            for n in range(ratio)
        ]
        + [grad_down_weight.reshape(devices, ratio * own_rows, width)],
        axis=1,
    ).reshape(devices * bulk_rows, width)
    bulk_sum = lax.psum_scatter(
        bulk_grad, ("batch", "seq"), scatter_dimension=0, tiled=True
    ).astype(jnp.float32)
    sum_output = bulk_sum[:own_rows]
    sum_up = jnp.concatenate(
        [bulk_sum[(1 + n) * own_rows : (2 + n) * own_rows] for n in range(ratio)], axis=1
    )
    sum_down = bulk_sum[(1 + ratio) * own_rows :]

    grad_query, grad_own_pair, grad_other_pair = attend_back(
        queries, grad_ctx, ctx_wide, lse, own_pair, other_pair, seg_key, seg_query
    )
    with jax.named_scope("pair_sum"):
        arrived_pair = hop_core(grad_other_pair.astype(jnp.bfloat16)).astype(jnp.float32)
        pair_total = grad_own_pair + arrived_pair
        pair_scale = jnp.where(jnp.arange(2 * GROUP_COLS) < GROUP_COLS, SCALE, 1.0)
        grad_projected = jnp.concatenate([pair_total * pair_scale, grad_query], axis=1).astype(
            jnp.bfloat16
        )

    with jax.named_scope("token_grads"):
        grad_half = matmul_right_t(grad_projected, group_weight)
        half_blocks = grad_half.reshape(4, row_count, width)
        low_blocks = half_blocks.astype(jnp.bfloat16)
        grad_block = half_blocks[0]
        for flip in flips:
            grad_block = grad_block + hop_quad(low_blocks[flip], flip).astype(jnp.float32)
        grad_block = grad_block.astype(jnp.bfloat16)
        home = [
            to_owner(grad_block[turn * stretch : (turn + 1) * stretch], turn) for turn in (0, 1)
        ]
        home_rows = jnp.concatenate(
            [
                jnp.where(parity == 0, home[0], home[1]),
                jnp.where(parity == 0, home[1], home[0]),
            ],
            axis=0,
        )
        grad_tokens = (grad_res_one + home_rows.astype(jnp.float32)).reshape(tokens.shape)

    with jax.named_scope("group_weight_grads"):
        grad_group = matmul_left_t(token_half, grad_projected)
        bias_sums = column_sums(grad_projected)
        nothing = jnp.zeros((width,), jnp.float32)
        vec_rows = jnp.stack(
            [
                lax.dynamic_update_slice_in_dim(
                    nothing, bias_sums[2 * GROUP_COLS :], quad * GROUP_COLS, 0
                ),
                lax.dynamic_update_slice_in_dim(
                    nothing, bias_sums[GROUP_COLS : 2 * GROUP_COLS], quad * GROUP_COLS, 0
                ),
                column_sums(grad_branch_low),
                grad_attn_gain,
                grad_attn_shift,
                column_sums(grad_down_low),
                grad_ffn_gain,
                grad_ffn_shift,
            ],
            axis=0,
        ).T
        vecs = jnp.concatenate([vec_rows, column_sums(grad_up_low).reshape(width, ratio)], axis=1)
        packed_grads = pack_grads(grad_group, vecs).reshape(2, 4, 4 * own_rows, PACK)
        by_layer = turned([packed_grads[:, number] for number in range(4)], layer_z)
        main, vecs = unpack_grads(by_layer[0])
        for flip in flips:
            more, more_vecs = unpack_grads(hop_layer(by_layer[flip], flip))
            main, vecs = (main + more, vecs + more_vecs)
        packed_grads = pack_grads(main, vecs)
        mine = jnp.where(core == 0, packed_grads[0], packed_grads[1])
        theirs = jnp.where(core == 0, packed_grads[1], packed_grads[0])
        main, vecs = unpack_grads(mine)
        more, more_vecs = unpack_grads(hop_core(theirs))
        main, vecs = (main + more, vecs + more_vecs)
        packed_grads = pack_grads(main, vecs).reshape(4, own_rows, PACK)
        by_quad = turned([packed_grads[number] for number in range(4)], quad)
        main, vecs = unpack_grads(by_quad[0])
        quad_parts = [main]
        for flip in flips:
            more, more_vecs = unpack_grads(hop_quad(by_quad[flip], flip))
            quad_parts.append(more)
            vecs = vecs + more_vecs
        quad_parts = turned(quad_parts, quad)
        sum_key, sum_value, sum_query = [
            jnp.concatenate([part[:, n * GROUP_COLS : (n + 1) * GROUP_COLS] for part in quad_parts], axis=1)
            for n in range(3)
        ]
    sum_rows = vecs[:, :8].T
    return (
        mixed,
        grad_tokens,
        sum_query,
        sum_rows[0],
        sum_key,
        sum_value,
        sum_rows[1],
        sum_output,
        sum_rows[2],
        sum_rows[3],
        sum_rows[4],
        sum_up,
        vecs[:, 8:].reshape(up_bias.shape),
        sum_down,
        sum_rows[5],
        sum_rows[6],
        sum_rows[7],
    )


def solution(mesh):
    in_specs = (
        P("batch", "seq", None),
        P("batch", None),
        P(("batch", "seq"), None),
        P(("batch", "seq")),
        P(("batch", "seq"), None),
        P(("batch", "seq"), None),
        P(("batch", "seq")),
        P(("batch", "seq"), None),
        P(("batch", "seq")),
        P(("batch", "seq")),
        P(("batch", "seq")),
        P(("batch", "seq"), None),
        P(("batch", "seq")),
        P(("batch", "seq"), None),
        P(("batch", "seq")),
        P(("batch", "seq")),
        P(("batch", "seq")),
        P("batch", "seq", None),
    )
    out_specs = (
        P("batch", "seq", None),
        P("batch", "seq", None),
        P(("batch", "seq"), None),
        P(("batch", "seq")),
        P(("batch", "seq"), None),
        P(("batch", "seq"), None),
        P(("batch", "seq")),
        P(("batch", "seq"), None),
        P(("batch", "seq")),
        P(("batch", "seq")),
        P(("batch", "seq")),
        P(("batch", "seq"), None),
        P(("batch", "seq")),
        P(("batch", "seq"), None),
        P(("batch", "seq")),
        P(("batch", "seq")),
        P(("batch", "seq")),
    )
    fits = mesh.shape['batch'] == 2 and mesh.shape['seq'] == 16
    body = shards_heads if fits else shards_general
    return jax.shard_map(body, mesh=mesh, in_specs=in_specs, out_specs=out_specs, check_vma=False)
```

```python
import jax
import jax.numpy as jnp
from jax import lax
from jax.experimental import pallas as pl
from jax.experimental.pallas import tpu as pltpu
from jax.sharding import PartitionSpec as P

HEADS = 12
HEAD_DIM = 64


SCALE = 0.125
NEG = -1e30
EPS = 1e-12


def norm_apply(hidden, gain_vec, shift_vec):
    center = jnp.mean(hidden, axis=-1, keepdims=True)
    centered = hidden - center
    spread = jnp.mean(centered * centered, axis=-1, keepdims=True)
    return centered * lax.rsqrt(spread + EPS) * gain_vec + shift_vec


def gelu_exact(inputs):
    return jax.nn.gelu(inputs, approximate=False)


def segment_ids(doc_lengths, positions):
    doc_ends = jnp.cumsum(doc_lengths, axis=-1)
    return jnp.sum((positions[None, :, None] >= doc_ends[:, None, :]).astype(jnp.int32), axis=-1)


def matmul_plain(left_op, right_op):
    return jnp.dot(left_op, right_op, preferred_element_type=jnp.float32)


def matmul_right_t(left_op, right_op):
    return lax.dot_general(
        left_op, right_op, (((1,), (1,)), ((), ())), preferred_element_type=jnp.float32
    )


def matmul_left_t(left_op, right_op):
    return lax.dot_general(
        left_op, right_op, (((0,), (0,)), ((), ())), preferred_element_type=jnp.float32
    )


def column_sums(matrix):
    return jnp.sum(matrix.astype(jnp.float32), axis=0)


def head_block(matrix, head_pair):
    pair_width = 2 * HEAD_DIM
    column_block = matrix[..., head_pair * pair_width : (head_pair + 1) * pair_width]
    return column_block.reshape(column_block.shape[:-1] + (2, HEAD_DIM))


def merge_heads(blocks):
    return jnp.concatenate(
        [block_item.reshape(block_item.shape[:2] + (2 * HEAD_DIM,)) for block_item in blocks],
        axis=-1,
    )


def stat_pair(stats, head_pair):
    return stats[:, 2 * head_pair : 2 * head_pair + 2][..., None]


def pair_scores(query_pair, key_pair, same_doc):
    raw_scores = jnp.einsum(
        "sqhd,skhd->shqk", query_pair, key_pair, preferred_element_type=jnp.float32
    )
    return jnp.where(same_doc[:, None], SCALE * raw_scores, NEG)


def attend_forward(queries, key_all, value_all, same_doc):
    outputs, log_sums = ([], [])
    for head_pair in range(HEADS // 2):
        scores = pair_scores(
            head_block(queries, head_pair), head_block(key_all, head_pair), same_doc
        )
        top_score = jnp.max(scores, axis=-1, keepdims=True)
        exponent = jnp.exp(scores - top_score)
        totals = jnp.sum(exponent, axis=-1, keepdims=True)
        probs_low = (exponent / totals).astype(jnp.bfloat16)
        context = jnp.einsum(
            "shqk,skhd->sqhd",
            probs_low,
            head_block(value_all, head_pair),
            preferred_element_type=jnp.float32,
        )
        outputs.append(context)
        log_sums.append((top_score + jnp.log(totals))[..., 0])
    return (merge_heads(outputs), jnp.concatenate(log_sums, axis=1))


def attend_backward(queries, key_all, value_all, same_doc, log_sums, grad_context):
    query_grads, key_grads, value_grads, row_dots = ([], [], [], [])
    for head_pair in range(HEADS // 2):
        query_pair = head_block(queries, head_pair)
        key_pair = head_block(key_all, head_pair)
        grad_pair = head_block(grad_context, head_pair)
        probs = jnp.exp(
            pair_scores(query_pair, key_pair, same_doc) - stat_pair(log_sums, head_pair)
        )
        grad_probs = jnp.einsum(
            "sqhd,skhd->shqk",
            grad_pair,
            head_block(value_all, head_pair),
            preferred_element_type=jnp.float32,
        )
        row_dot = jnp.sum(probs * grad_probs, axis=-1, keepdims=True)
        row_dots.append(row_dot[..., 0])
        grad_scores = (probs * (grad_probs - row_dot)).astype(jnp.bfloat16) * jnp.bfloat16(SCALE)
        query_grads.append(
            jnp.einsum("shqk,skhd->sqhd", grad_scores, key_pair, preferred_element_type=jnp.float32)
        )
    return (merge_heads(query_grads), jnp.concatenate(row_dots, axis=1), None, None)


def key_side_local(query_all, grad_ctx_all, lse_all, rowdot_all, keys_own, values_own, same_doc_t):
    key_grads, value_grads = ([], [])
    for head_pair in range(HEADS // 2):
        query_pair = head_block(query_all, head_pair)
        grad_pair = head_block(grad_ctx_all, head_pair)
        probs = jnp.exp(
            pair_scores(query_pair, head_block(keys_own, head_pair), same_doc_t)
            - stat_pair(lse_all, head_pair)
        )
        grad_probs = jnp.einsum(
            "sqhd,skhd->shqk",
            grad_pair,
            head_block(values_own, head_pair),
            preferred_element_type=jnp.float32,
        )
        grad_scores = (probs * (grad_probs - stat_pair(rowdot_all, head_pair))).astype(
            jnp.bfloat16
        ) * jnp.bfloat16(SCALE)
        key_grads.append(
            jnp.einsum(
                "shqk,sqhd->skhd", grad_scores, query_pair, preferred_element_type=jnp.float32
            )
        )
        value_grads.append(
            jnp.einsum(
                "shqk,sqhd->skhd",
                probs.astype(jnp.bfloat16),
                grad_pair,
                preferred_element_type=jnp.float32,
            )
        )
    return (merge_heads(key_grads), merge_heads(value_grads))


def shards_general(
    tokens,
    doc_lengths,
    query_weight,
    query_bias,
    key_weight,
    value_weight,
    value_bias,
    output_weight,
    output_bias,
    attn_gain,
    attn_shift,
    up_weight,
    up_bias,
    down_weight,
    down_bias,
    ffn_gain,
    ffn_shift,
    cotangent,
):
    gathered = (
        lax.all_gather(query_weight, ("batch", "seq"), axis=0, tiled=True),
        lax.all_gather(query_bias, ("batch", "seq"), axis=0, tiled=True),
        lax.all_gather(key_weight, ("batch", "seq"), axis=0, tiled=True),
        lax.all_gather(value_weight, ("batch", "seq"), axis=0, tiled=True),
        lax.all_gather(value_bias, ("batch", "seq"), axis=0, tiled=True),
        lax.all_gather(output_weight, ("batch", "seq"), axis=0, tiled=True),
        lax.all_gather(output_bias, ("batch", "seq"), axis=0, tiled=True),
        lax.all_gather(attn_gain, ("batch", "seq"), axis=0, tiled=True),
        lax.all_gather(attn_shift, ("batch", "seq"), axis=0, tiled=True),
        lax.all_gather(up_weight, ("batch", "seq"), axis=0, tiled=True),
        lax.all_gather(up_bias, ("batch", "seq"), axis=0, tiled=True),
        lax.all_gather(down_weight, ("batch", "seq"), axis=0, tiled=True),
        lax.all_gather(down_bias, ("batch", "seq"), axis=0, tiled=True),
        lax.all_gather(ffn_gain, ("batch", "seq"), axis=0, tiled=True),
        lax.all_gather(ffn_shift, ("batch", "seq"), axis=0, tiled=True),
    )
    (
        query_full,
        qbias_full,
        key_full,
        value_full,
        vbias_full,
        output_full,
        obias_full,
        again_full,
        ashift_full,
        up_full,
        ubias_full,
        down_full,
        dbias_full,
        fgain_full,
        fshift_full,
    ) = gathered
    seq_groups, stretch_len, width = tokens.shape
    row_count = seq_groups * stretch_len
    token_rows = tokens.reshape(row_count, width)
    positions = lax.axis_index("seq") * stretch_len + jnp.arange(stretch_len, dtype=jnp.int32)
    total_len = stretch_len * lax.axis_size("seq")
    query_seg = segment_ids(doc_lengths, positions)
    key_seg = segment_ids(doc_lengths, jnp.arange(total_len, dtype=jnp.int32))
    same_doc = query_seg[:, :, None] == key_seg[:, None, :]
    queries = (
        (matmul_plain(token_rows, query_full) + qbias_full)
        .astype(jnp.bfloat16)
        .reshape(tokens.shape)
    )
    keys_local = matmul_plain(token_rows, key_full).astype(jnp.bfloat16).reshape(tokens.shape)
    values_local = (
        (matmul_plain(token_rows, value_full) + vbias_full)
        .astype(jnp.bfloat16)
        .reshape(tokens.shape)
    )
    key_all, value_all = (
        lax.all_gather(keys_local, "seq", axis=1, tiled=True),
        lax.all_gather(values_local, "seq", axis=1, tiled=True),
    )
    context, log_sums = attend_forward(queries, key_all, value_all, same_doc)
    context_low = context.reshape(row_count, width).astype(jnp.bfloat16)
    res_one = token_rows.astype(jnp.float32) + matmul_plain(context_low, output_full) + obias_full
    normed, pull_one = jax.vjp(
        norm_apply, res_one, again_full.astype(jnp.float32), ashift_full.astype(jnp.float32)
    )
    normed_low = normed.astype(jnp.bfloat16)
    up_pre = matmul_plain(normed_low, up_full) + ubias_full
    activated, pull_gelu = jax.vjp(gelu_exact, up_pre)
    act_low = activated.astype(jnp.bfloat16)
    res_two = normed + matmul_plain(act_low, down_full) + dbias_full
    output_rows, pull_two = jax.vjp(
        norm_apply, res_two, fgain_full.astype(jnp.float32), fshift_full.astype(jnp.float32)
    )
    mixed = output_rows.astype(jnp.bfloat16).reshape(tokens.shape)
    regathered = (
        lax.all_gather(query_weight, ("batch", "seq"), axis=0, tiled=True),
        lax.all_gather(query_bias, ("batch", "seq"), axis=0, tiled=True),
        lax.all_gather(key_weight, ("batch", "seq"), axis=0, tiled=True),
        lax.all_gather(value_weight, ("batch", "seq"), axis=0, tiled=True),
        lax.all_gather(value_bias, ("batch", "seq"), axis=0, tiled=True),
        lax.all_gather(output_weight, ("batch", "seq"), axis=0, tiled=True),
        lax.all_gather(output_bias, ("batch", "seq"), axis=0, tiled=True),
        lax.all_gather(attn_gain, ("batch", "seq"), axis=0, tiled=True),
        lax.all_gather(attn_shift, ("batch", "seq"), axis=0, tiled=True),
        lax.all_gather(up_weight, ("batch", "seq"), axis=0, tiled=True),
        lax.all_gather(up_bias, ("batch", "seq"), axis=0, tiled=True),
        lax.all_gather(down_weight, ("batch", "seq"), axis=0, tiled=True),
        lax.all_gather(down_bias, ("batch", "seq"), axis=0, tiled=True),
        lax.all_gather(ffn_gain, ("batch", "seq"), axis=0, tiled=True),
        lax.all_gather(ffn_shift, ("batch", "seq"), axis=0, tiled=True),
    )
    query_back = regathered[0]
    key_back = regathered[2]
    value_back = regathered[3]
    output_back = regathered[5]
    up_back = regathered[9]
    down_back = regathered[11]
    grad_out = cotangent.astype(jnp.float32).reshape(row_count, width)
    grad_res_two, grad_ffn_gain, grad_ffn_shift = pull_two(grad_out)
    grad_down_low = grad_res_two.astype(jnp.bfloat16)
    grad_down_weight = matmul_left_t(act_low, grad_down_low)
    grad_down_bias = column_sums(grad_down_low)
    (grad_up_pre,) = pull_gelu(matmul_right_t(grad_down_low, down_back))
    grad_up_low = grad_up_pre.astype(jnp.bfloat16)
    grad_up_weight = matmul_left_t(normed_low, grad_up_low)
    grad_up_bias = column_sums(grad_up_low)
    grad_normed = grad_res_two + matmul_right_t(grad_up_low, up_back)
    grad_res_one, grad_attn_gain, grad_attn_shift = pull_one(grad_normed)
    grad_branch_low = grad_res_one.astype(jnp.bfloat16)
    grad_output_weight = matmul_left_t(context_low, grad_branch_low)
    grad_output_bias = column_sums(grad_branch_low)
    grad_context = (
        matmul_right_t(grad_branch_low, output_back).astype(jnp.bfloat16).reshape(tokens.shape)
    )
    key_again, value_again = (
        lax.all_gather(keys_local, "seq", axis=1, tiled=True),
        lax.all_gather(values_local, "seq", axis=1, tiled=True),
    )
    grad_query, row_dots, unused_key, unused_value = attend_backward(
        queries, key_again, value_again, same_doc, log_sums, grad_context
    )
    query_all, grad_ctx_all = (
        lax.all_gather(queries, "seq", axis=1, tiled=True),
        lax.all_gather(grad_context, "seq", axis=1, tiled=True),
    )
    lse_all, rowdot_all = (
        lax.all_gather(log_sums, "seq", axis=2, tiled=True),
        lax.all_gather(row_dots, "seq", axis=2, tiled=True),
    )
    same_doc_t = key_seg[:, :, None] == query_seg[:, None, :]
    grad_key, grad_value = key_side_local(
        query_all, grad_ctx_all, lse_all, rowdot_all, keys_local, values_local, same_doc_t
    )
    grad_query_low = grad_query.reshape(row_count, width).astype(jnp.bfloat16)
    grad_key_low = grad_key.reshape(row_count, width).astype(jnp.bfloat16)
    grad_value_low = grad_value.reshape(row_count, width).astype(jnp.bfloat16)
    grad_query_weight = matmul_left_t(token_rows, grad_query_low)
    grad_query_bias = column_sums(grad_query_low)
    grad_key_weight = matmul_left_t(token_rows, grad_key_low)
    grad_value_weight = matmul_left_t(token_rows, grad_value_low)
    grad_value_bias = column_sums(grad_value_low)
    grad_tokens = (
        grad_res_one
        + matmul_right_t(grad_query_low, query_back)
        + matmul_right_t(grad_key_low, key_back)
        + matmul_right_t(grad_value_low, value_back)
    )
    summed = (
        lax.psum_scatter(grad_query_weight, ("batch", "seq"), scatter_dimension=0, tiled=True),
        lax.psum_scatter(grad_query_bias, ("batch", "seq"), scatter_dimension=0, tiled=True),
        lax.psum_scatter(grad_key_weight, ("batch", "seq"), scatter_dimension=0, tiled=True),
        lax.psum_scatter(grad_value_weight, ("batch", "seq"), scatter_dimension=0, tiled=True),
        lax.psum_scatter(grad_value_bias, ("batch", "seq"), scatter_dimension=0, tiled=True),
        lax.psum_scatter(grad_output_weight, ("batch", "seq"), scatter_dimension=0, tiled=True),
        lax.psum_scatter(grad_output_bias, ("batch", "seq"), scatter_dimension=0, tiled=True),
        lax.psum_scatter(grad_attn_gain, ("batch", "seq"), scatter_dimension=0, tiled=True),
        lax.psum_scatter(grad_attn_shift, ("batch", "seq"), scatter_dimension=0, tiled=True),
        lax.psum_scatter(grad_up_weight, ("batch", "seq"), scatter_dimension=0, tiled=True),
        lax.psum_scatter(grad_up_bias, ("batch", "seq"), scatter_dimension=0, tiled=True),
        lax.psum_scatter(grad_down_weight, ("batch", "seq"), scatter_dimension=0, tiled=True),
        lax.psum_scatter(grad_down_bias, ("batch", "seq"), scatter_dimension=0, tiled=True),
        lax.psum_scatter(grad_ffn_gain, ("batch", "seq"), scatter_dimension=0, tiled=True),
        lax.psum_scatter(grad_ffn_shift, ("batch", "seq"), scatter_dimension=0, tiled=True),
    )
    return (
        mixed,
        grad_tokens.reshape(tokens.shape),
        summed[0],
        summed[1],
        summed[2],
        summed[3],
        summed[4],
        summed[5],
        summed[6],
        summed[7],
        summed[8],
        summed[9],
        summed[10],
        summed[11],
        summed[12],
        summed[13],
        summed[14],
    )


LOG2E = 1.4426950408889634
GROUP_HEADS = 3
GROUP_COLS = GROUP_HEADS * HEAD_DIM
PACK = 640
VECS = 12
SIDE = 16
KEY_CHUNK = 512


def dot_nt(left_op, right_op):
    return lax.dot_general(
        left_op, right_op, (((1,), (1,)), ((), ())), preferred_element_type=jnp.float32
    )


def dot_nn(left_op, right_op):
    return lax.dot_general(
        left_op, right_op, (((1,), (0,)), ((), ())), preferred_element_type=jnp.float32
    )


def attend_kernel(
    query_ref, own_ref, other_ref, seg_key_ref, seg_query_ref, ctx_ref, lse_ref, value_t
):
    half = own_ref.shape[0]
    rows = query_ref.shape[0]

    @pl.when(pl.program_id(0) == 0)
    def _():
        value_t[:, :half] = own_ref[:, GROUP_COLS : 2 * GROUP_COLS].T
        value_t[:, half:] = other_ref[:, GROUP_COLS : 2 * GROUP_COLS].T

    seg_query = seg_query_ref[...]
    chunks = [
        (ref, start) for ref in (own_ref, other_ref) for start in range(0, half, KEY_CHUNK)
    ]
    for head in range(GROUP_HEADS):
        cols = slice(head * HEAD_DIM, (head + 1) * HEAD_DIM)
        query = query_ref[:, cols]
        scores = []
        top = None
        for number, (ref, start) in enumerate(chunks):
            raw = dot_nt(ref[start : start + KEY_CHUNK, cols], query)
            seg_key = seg_key_ref[number * KEY_CHUNK : (number + 1) * KEY_CHUNK, :]
            seg_key = jnp.concatenate([seg_key] * (rows // 128), axis=1)
            masked = jnp.where(seg_key == seg_query, raw * (SCALE * LOG2E), NEG)
            scores.append(masked)
            peak = jnp.max(masked, axis=0, keepdims=True)
            top = peak if top is None else jnp.maximum(top, peak)
        total = None
        context_t = None
        for number in range(len(chunks)):
            weight = jnp.exp2(scores[number] - top)
            part = jnp.sum(weight, axis=0, keepdims=True)
            piece = dot_nn(
                value_t[cols, number * KEY_CHUNK : (number + 1) * KEY_CHUNK],
                weight.astype(jnp.bfloat16),
            )
            total = part if total is None else total + part
            context_t = piece if context_t is None else context_t + piece
        ctx_ref[:, cols] = (context_t / total).T
        lse_ref[head : head + 1, :] = top + jnp.log2(total)


def attend(query, own, other, seg_key, seg_query):
    rows = query.shape[0]
    half = own.shape[0]
    block = rows // 4
    return pl.pallas_call(
        attend_kernel,
        grid=(4,),
        in_specs=[
            pl.BlockSpec((block, GROUP_COLS), lambda i: (i, 0)),
            pl.BlockSpec((half, 2 * GROUP_COLS), lambda i: (0, 0)),
            pl.BlockSpec((half, 2 * GROUP_COLS), lambda i: (0, 0)),
            pl.BlockSpec((2 * half, 128), lambda i: (0, 0)),
            pl.BlockSpec((1, block), lambda i: (0, i)),
        ],
        out_specs=[
            pl.BlockSpec((block, GROUP_COLS), lambda i: (i, 0)),
            pl.BlockSpec((8, block), lambda i: (0, i)),
        ],
        out_shape=[
            jax.ShapeDtypeStruct((rows, GROUP_COLS), jnp.float32),
            jax.ShapeDtypeStruct((8, rows), jnp.float32),
        ],
        scratch_shapes=[pltpu.VMEM((GROUP_COLS, 2 * half), jnp.bfloat16)],
        compiler_params=pltpu.CompilerParams(vmem_limit_bytes=48 * 1024 * 1024),
        cost_estimate=pl.CostEstimate(
            flops=16 * rows * half * GROUP_COLS,
            bytes_accessed=4 * 1024 * 1024,
            transcendentals=2 * GROUP_HEADS * rows * half,
        ),
        name="attend",
    )(query, own, other, seg_key, seg_query)


def attend_back_kernel(
    query_ref,
    grad_ref,
    ctx_ref,
    lse_ref,
    own_ref,
    other_ref,
    seg_key_ref,
    seg_query_ref,
    gquery_ref,
    gown_ref,
    gother_ref,
    key_t,
):
    half = own_ref.shape[0]
    rows = query_ref.shape[0]
    first = pl.program_id(0) == 0

    @pl.when(first)
    def _():
        key_t[:, :half] = own_ref[:, :GROUP_COLS].T
        key_t[:, half:] = other_ref[:, :GROUP_COLS].T
        gown_ref[...] = jnp.zeros_like(gown_ref)
        gother_ref[...] = jnp.zeros_like(gother_ref)

    seg_query = seg_query_ref[...]
    chunks = [
        (ref, gref, start)
        for ref, gref in ((own_ref, gown_ref), (other_ref, gother_ref))
        for start in range(0, half, KEY_CHUNK)
    ]
    for head in range(GROUP_HEADS):
        cols = slice(head * HEAD_DIM, (head + 1) * HEAD_DIM)
        vcols = slice(GROUP_COLS + head * HEAD_DIM, GROUP_COLS + (head + 1) * HEAD_DIM)
        query = query_ref[:, cols]
        grad = grad_ref[:, cols]
        lse = lse_ref[head : head + 1, :]
        dots = (grad.astype(jnp.float32) * ctx_ref[:, cols]).T
        row_dot = jnp.sum(dots, axis=0, keepdims=True)
        gquery_t = None
        for number, (ref, gref, start) in enumerate(chunks):
            spot = slice(start, start + KEY_CHUNK)
            raw = dot_nt(ref[spot, cols], query)
            seg_key = seg_key_ref[number * KEY_CHUNK : (number + 1) * KEY_CHUNK, :]
            seg_key = jnp.concatenate([seg_key] * (rows // 128), axis=1)
            masked = jnp.where(seg_key == seg_query, raw * (SCALE * LOG2E), NEG)
            probs = jnp.exp2(masked - lse)
            gprobs = dot_nt(ref[spot, vcols], grad)
            gscores = (probs * (gprobs - row_dot)).astype(jnp.bfloat16)
            gref[spot, vcols] += dot_nn(probs.astype(jnp.bfloat16), grad)
            gref[spot, cols] += dot_nn(gscores, query)
            piece = dot_nn(key_t[cols, number * KEY_CHUNK : (number + 1) * KEY_CHUNK], gscores)
            gquery_t = piece if gquery_t is None else gquery_t + piece
        gquery_ref[:, cols] = (SCALE * gquery_t).T


def attend_back(query, grad, ctx, lse, own, other, seg_key, seg_query):
    rows = query.shape[0]
    half = own.shape[0]
    block = rows // 4
    return pl.pallas_call(
        attend_back_kernel,
        grid=(4,),
        in_specs=[
            pl.BlockSpec((block, GROUP_COLS), lambda i: (i, 0)),
            pl.BlockSpec((block, GROUP_COLS), lambda i: (i, 0)),
            pl.BlockSpec((block, GROUP_COLS), lambda i: (i, 0)),
            pl.BlockSpec((8, block), lambda i: (0, i)),
            pl.BlockSpec((half, 2 * GROUP_COLS), lambda i: (0, 0)),
            pl.BlockSpec((half, 2 * GROUP_COLS), lambda i: (0, 0)),
            pl.BlockSpec((2 * half, 128), lambda i: (0, 0)),
            pl.BlockSpec((1, block), lambda i: (0, i)),
        ],
        out_specs=[
            pl.BlockSpec((block, GROUP_COLS), lambda i: (i, 0)),
            pl.BlockSpec((half, 2 * GROUP_COLS), lambda i: (0, 0)),
            pl.BlockSpec((half, 2 * GROUP_COLS), lambda i: (0, 0)),
        ],
        out_shape=[
            jax.ShapeDtypeStruct((rows, GROUP_COLS), jnp.float32),
            jax.ShapeDtypeStruct((half, 2 * GROUP_COLS), jnp.float32),
            jax.ShapeDtypeStruct((half, 2 * GROUP_COLS), jnp.float32),
        ],
        scratch_shapes=[pltpu.VMEM((GROUP_COLS, 2 * half), jnp.bfloat16)],
        compiler_params=pltpu.CompilerParams(vmem_limit_bytes=48 * 1024 * 1024),
        cost_estimate=pl.CostEstimate(
            flops=40 * rows * half * GROUP_COLS,
            bytes_accessed=10 * 1024 * 1024,
            transcendentals=2 * GROUP_HEADS * rows * half,
        ),
        name="attend_back",
    )(query, grad, ctx, lse, own, other, seg_key, seg_query)


def prepare_kernel(
    tokens_ref,
    lengths_ref,
    key_ref,
    value_ref,
    query_ref,
    qbias_ref,
    vbias_ref,
    obias_ref,
    again_ref,
    ashift_ref,
    dbias_ref,
    fgain_ref,
    fshift_ref,
    ubias_ref,
    first_ref,
    second_ref,
    *piece_refs,
):
    place = lax.axis_index("seq")
    odd = lax.rem(place // 4, 2) == 1
    quad = lax.rem(place, 4)
    first_ref[...] = jnp.where(odd, tokens_ref[1], tokens_ref[0])
    second_ref[...] = jnp.where(odd, tokens_ref[0], tokens_ref[1])
    own_rows = key_ref.shape[0]
    small = (qbias_ref, vbias_ref, obias_ref, again_ref, ashift_ref, dbias_ref, fgain_ref, fshift_ref)
    rows = [ref[...].astype(jnp.float32) for ref in small]
    wide = ubias_ref[...].astype(jnp.float32)
    rows += [wide[:, n * own_rows : (n + 1) * own_rows] for n in range(VECS - len(small))]
    lengths = lengths_ref[...]
    docs = lengths.shape[1]
    flat = jnp.concatenate(
        [lengths[0:1], lengths[1:2], jnp.zeros((1, own_rows - 2 * docs), jnp.int32)], axis=1
    )
    rows += [(flat >> 6).astype(jnp.float32), (flat & 63).astype(jnp.float32)]
    rows += [jnp.zeros_like(rows[0])] * (SIDE - len(rows))
    side = jnp.concatenate(rows, axis=0).T.astype(jnp.bfloat16)
    cut = 3 * GROUP_COLS
    for flip, piece_ref in enumerate(piece_refs):
        piece_ref[...] = jnp.zeros_like(piece_ref)
        piece_ref[:, cut : cut + SIDE] = side
        target = quad ^ flip
        for number in range(4):

            @pl.when(target == number)
            def _():
                cols = slice(number * GROUP_COLS, (number + 1) * GROUP_COLS)
                for spot, ref in enumerate((key_ref, value_ref, query_ref)):
                    piece_ref[:, spot * GROUP_COLS : (spot + 1) * GROUP_COLS] = ref[:, cols]


def prepare(tokens, lengths, key, value, query, vectors, up_bias):
    own_rows = key.shape[0]
    turn_shape = jax.ShapeDtypeStruct(tokens.shape[1:], jnp.bfloat16)
    piece_shape = jax.ShapeDtypeStruct((own_rows, PACK), jnp.bfloat16)
    return pl.pallas_call(
        prepare_kernel,
        out_shape=[turn_shape] * 2 + [piece_shape] * 4,
        name="prepare",
    )(
        tokens,
        lengths,
        key,
        value,
        query,
        *[item.reshape(1, own_rows) for item in vectors],
        up_bias.reshape(1, up_bias.shape[0]),
    )


def scatter_sum(term, rows, core, layer_z, quad):
    theirs = term(1 - core).astype(jnp.bfloat16)
    total = (term(core) + hop_core(theirs).astype(jnp.float32)).astype(jnp.bfloat16)
    blocks = total.reshape(4, 4, rows, total.shape[-1])

    def block(values, index, axis):
        return lax.dynamic_index_in_dim(values, index, axis=axis, keepdims=False)

    part = block(blocks, quad, 1).astype(jnp.float32)
    for flip in (1, 2, 3):
        part = part + hop_quad(block(blocks, quad ^ flip, 1), flip).astype(jnp.float32)
    blocks = part.astype(jnp.bfloat16)
    part = block(part, layer_z, 0)
    for flip in (1, 2, 3):
        part = part + hop_layer(block(blocks, layer_z ^ flip, 0), flip).astype(jnp.float32)
    return part


def device_table(mapping):
    pairs = []
    for core in range(2):
        for layer_z in range(4):
            for quad in range(4):
                to_core, to_z, to_quad = mapping(core, layer_z, quad)
                pairs.append((core * 16 + layer_z * 4 + quad, to_core * 16 + to_z * 4 + to_quad))
    return pairs


def hop(value, mapping):
    return lax.ppermute(value, ("batch", "seq"), device_table(mapping))


def hop_quad(value, flip):
    return hop(value, lambda core, layer_z, quad: (core, layer_z, quad ^ flip))


def hop_layer(value, flip):
    return hop(value, lambda core, layer_z, quad: (core, layer_z ^ flip, quad))


def hop_core(value):
    return hop(value, lambda core, layer_z, quad: (1 - core, layer_z, quad))


def to_sequence(value, turn):
    return hop(
        value,
        lambda core, layer_z, quad: (layer_z // 2, 2 * core + (layer_z + turn) % 2, quad),
    )


def to_owner(value, turn):
    return hop(
        value,
        lambda core, layer_z, quad: (layer_z // 2, 2 * core + (layer_z - turn) % 2, quad),
    )


def turned(blocks, quad):
    first, second, third, fourth = blocks
    odd = quad % 2 == 1
    high = quad // 2 == 1
    pairs = (
        jnp.where(odd, second, first),
        jnp.where(odd, first, second),
        jnp.where(odd, fourth, third),
        jnp.where(odd, third, fourth),
    )
    return (
        jnp.where(high, pairs[2], pairs[0]),
        jnp.where(high, pairs[3], pairs[1]),
        jnp.where(high, pairs[0], pairs[2]),
        jnp.where(high, pairs[1], pairs[3]),
    )


def pack_grads(main, vecs):
    coarse = vecs.astype(jnp.bfloat16)
    fine = (vecs - coarse.astype(jnp.float32)).astype(jnp.bfloat16)
    filler = jnp.zeros(main.shape[:-1] + (PACK - main.shape[-1] - 2 * VECS,), jnp.bfloat16)
    return jnp.concatenate([main.astype(jnp.bfloat16), coarse, fine, filler], axis=-1)


def unpack_grads(packed):
    wide = packed.astype(jnp.float32)
    cut = 3 * GROUP_COLS
    return (wide[..., :cut], wide[..., cut : cut + VECS] + wide[..., cut + VECS : cut + 2 * VECS])


def shards_heads(
    tokens,
    doc_lengths,
    query_weight,
    query_bias,
    key_weight,
    value_weight,
    value_bias,
    output_weight,
    output_bias,
    attn_gain,
    attn_shift,
    up_weight,
    up_bias,
    down_weight,
    down_bias,
    ffn_gain,
    ffn_shift,
    cotangent,
):
    groups, stretch, width = tokens.shape
    own_rows = query_weight.shape[0]
    hidden = up_weight.shape[1]
    ratio = hidden // width
    devices = width // own_rows
    bulk_rows = own_rows * (1 + 2 * ratio)
    row_count = groups * stretch
    core = lax.axis_index("batch")
    place = lax.axis_index("seq")
    layer_z = place // 4
    quad = place % 4
    parity = layer_z % 2
    flips = (1, 2, 3)

    vectors = (
        query_bias,
        value_bias,
        output_bias,
        attn_gain,
        attn_shift,
        down_bias,
        ffn_gain,
        ffn_shift,
    )
    first_turn, second_turn, *pieces = prepare(
        tokens, doc_lengths, key_weight, value_weight, query_weight, vectors, up_bias
    )

    with jax.named_scope("tokens_out"):
        own_block = jnp.concatenate(
            [to_sequence(first_turn, 0), to_sequence(second_turn, 1)], axis=0
        )
        token_half = jnp.concatenate(
            [own_block] + [hop_quad(own_block, flip) for flip in flips], axis=0
        )

    with jax.named_scope("group_weights"):
        quads = turned([pieces[0]] + [hop_quad(pieces[flip], flip) for flip in flips], quad)
        quads = jnp.stack(quads, axis=0)
        layers = [quads] + [hop_layer(quads, flip) for flip in flips]
        layers = jnp.stack(turned(layers, layer_z), axis=0)
        twin = hop_core(layers)
        cores = jnp.stack([jnp.where(core == 0, layers, twin), jnp.where(core == 0, twin, layers)])
        packed = cores.reshape(width, PACK)
    group_weight = packed[:, : 3 * GROUP_COLS]
    side = packed[:, 3 * GROUP_COLS : 3 * GROUP_COLS + SIDE].astype(jnp.float32)
    vector_rows = side[:, :8].T
    up_bias_full = side[:, 8:VECS].reshape(devices, own_rows, ratio)
    up_bias_full = jnp.swapaxes(up_bias_full, 1, 2).reshape(1, hidden)
    (
        qbias_full,
        vbias_full,
        obias_full,
        again_full,
        ashift_full,
        dbias_full,
        fgain_full,
        fshift_full,
    ) = [vector_rows[number] for number in range(8)]
    docs = doc_lengths.shape[1]
    digits = side.reshape(2, width // 2, SIDE)[:, : groups * docs, VECS : VECS + 2]
    lengths_all = (digits[..., 0] * 64 + digits[..., 1]).astype(jnp.int32)
    lengths = lax.dynamic_index_in_dim(
        lengths_all.reshape(2 * groups, docs), layer_z, axis=0, keepdims=False
    )
    doc_ends = jnp.cumsum(lengths)

    def half_segments(which):
        turn_z = jnp.stack([(layer_z - turn) % 2 for turn in (0, 1)]) + 2 * which
        spot = jnp.stack([quad ^ flip for flip in range(4)])
        start = turn_z[None, :] * (4 * stretch) + spot[:, None] * stretch
        positions = start[:, :, None] + jnp.arange(stretch, dtype=jnp.int32)
        positions = positions.reshape(-1)
        return jnp.sum((positions[:, None] >= doc_ends[None, :]).astype(jnp.int32), axis=-1)

    seg_query = half_segments(core)
    seg_key = jnp.concatenate([seg_query, half_segments(1 - core)])
    seg_key = jnp.broadcast_to(seg_key[:, None], (seg_key.shape[0], 128))
    seg_query = seg_query[None, :]

    bulk = jnp.concatenate(
        [output_weight]
        + [up_weight[:, number * width : (number + 1) * width] for number in range(ratio)]
        + [down_weight],
        axis=0,
    )
    bulk_all = lax.all_gather(bulk, ("batch", "seq"), axis=0, tiled=True)
    bulk_all = bulk_all.reshape(devices, bulk_rows, width)

    with jax.named_scope("projections"):
        column_bias = jnp.concatenate(
            [
                jnp.zeros((GROUP_COLS,), jnp.float32),
                lax.dynamic_slice_in_dim(vbias_full, quad * GROUP_COLS, GROUP_COLS),
                lax.dynamic_slice_in_dim(qbias_full, quad * GROUP_COLS, GROUP_COLS),
            ]
        )
        projected = (matmul_plain(token_half, group_weight) + column_bias).astype(jnp.bfloat16)
        own_pair = projected[:, : 2 * GROUP_COLS]
        queries = projected[:, 2 * GROUP_COLS :]
        other_pair = hop_core(own_pair)
    ctx_wide, lse = attend(queries, own_pair, other_pair, seg_key, seg_query)

    with jax.named_scope("context_home"):
        ctx_blocks = ctx_wide.astype(jnp.bfloat16).reshape(4, row_count, GROUP_COLS)
        ctx_groups = [ctx_blocks[0]] + [hop_quad(ctx_blocks[flip], flip) for flip in flips]
        ctx_merged = jnp.concatenate(turned(ctx_groups, quad), axis=1)
        ctx_turns = [
            to_owner(ctx_merged[turn * stretch : (turn + 1) * stretch], turn) for turn in (0, 1)
        ]
        context_low = jnp.concatenate(
            [
                jnp.where(parity == 0, ctx_turns[0], ctx_turns[1]),
                jnp.where(parity == 0, ctx_turns[1], ctx_turns[0]),
            ],
            axis=0,
        )

    output_full = bulk_all[:, :own_rows].reshape(width, width)
    up_parts = [
        bulk_all[:, (1 + number) * own_rows : (2 + number) * own_rows].reshape(width, width)
        for number in range(ratio)
    ]
    up_full = jnp.concatenate(up_parts, axis=1)
    down_full = bulk_all[:, (1 + ratio) * own_rows :].reshape(hidden, width)

    token_rows = tokens.reshape(row_count, width)
    res_one = token_rows.astype(jnp.float32) + matmul_plain(context_low, output_full) + obias_full
    normed, pull_one = jax.vjp(norm_apply, res_one, again_full, ashift_full)
    normed_low = normed.astype(jnp.bfloat16)
    up_pre = matmul_plain(normed_low, up_full) + up_bias_full
    activated, pull_gelu = jax.vjp(gelu_exact, up_pre)
    act_low = activated.astype(jnp.bfloat16)
    res_two = normed + matmul_plain(act_low, down_full) + dbias_full
    output_rows, pull_two = jax.vjp(norm_apply, res_two, fgain_full, fshift_full)
    mixed = output_rows.astype(jnp.bfloat16).reshape(tokens.shape)
    grad_out = cotangent.astype(jnp.float32).reshape(row_count, width)
    grad_res_two, grad_ffn_gain, grad_ffn_shift = pull_two(grad_out)
    grad_down_low = grad_res_two.astype(jnp.bfloat16)
    (grad_up_pre,) = pull_gelu(matmul_right_t(grad_down_low, down_full))
    grad_up_low = grad_up_pre.astype(jnp.bfloat16)
    grad_normed = grad_res_two + matmul_right_t(grad_up_low, up_full)
    grad_res_one, grad_attn_gain, grad_attn_shift = pull_one(grad_normed)
    grad_branch_low = grad_res_one.astype(jnp.bfloat16)
    grad_context = matmul_right_t(grad_branch_low, output_full).astype(jnp.bfloat16)

    with jax.named_scope("context_grad_out"):
        low_part = grad_context[:stretch]
        high_part = grad_context[stretch:]
        grad_turns = [
            to_sequence(jnp.where((parity + turn) % 2 == 1, high_part, low_part), turn)
            for turn in (0, 1)
        ]
        grad_own = jnp.concatenate(grad_turns, axis=0)
        grad_columns = turned(
            [grad_own[:, n * GROUP_COLS : (n + 1) * GROUP_COLS] for n in range(4)], quad
        )
        grad_ctx = jnp.concatenate(
            [grad_columns[0]] + [hop_quad(grad_columns[flip], flip) for flip in flips], axis=0
        )

    def half_columns(matrix, which):
        half = matrix.shape[1] // 2
        return lax.dynamic_slice_in_dim(matrix, which * half, half, axis=1)

    def down_term(which):
        return matmul_left_t(half_columns(act_low, which), grad_down_low)

    def branch_term(which):
        return jnp.concatenate(
            [
                matmul_left_t(half_columns(normed_low, which), grad_up_low),
                matmul_left_t(half_columns(context_low, which), grad_branch_low),
            ],
            axis=1,
        )

    with jax.named_scope("down_grads"):
        sum_down = scatter_sum(down_term, ratio * own_rows, core, layer_z, quad)
    with jax.named_scope("branch_grads"):
        sum_branch = scatter_sum(branch_term, own_rows, core, layer_z, quad)
        sum_up = sum_branch[:, :hidden]
        sum_output = sum_branch[:, hidden:]

    grad_query, grad_own_pair, grad_other_pair = attend_back(
        queries, grad_ctx, ctx_wide, lse, own_pair, other_pair, seg_key, seg_query
    )
    with jax.named_scope("pair_sum"):
        arrived_pair = hop_core(grad_other_pair.astype(jnp.bfloat16)).astype(jnp.float32)
        pair_total = grad_own_pair + arrived_pair
        pair_scale = jnp.where(jnp.arange(2 * GROUP_COLS) < GROUP_COLS, SCALE, 1.0)
        grad_projected = jnp.concatenate([pair_total * pair_scale, grad_query], axis=1).astype(
            jnp.bfloat16
        )

    with jax.named_scope("token_grads"):
        grad_half = matmul_right_t(grad_projected, group_weight)
        half_blocks = grad_half.reshape(4, row_count, width)
        low_blocks = half_blocks.astype(jnp.bfloat16)
        grad_block = half_blocks[0]
        for flip in flips:
            grad_block = grad_block + hop_quad(low_blocks[flip], flip).astype(jnp.float32)
        grad_block = grad_block.astype(jnp.bfloat16)
        home = [
            to_owner(grad_block[turn * stretch : (turn + 1) * stretch], turn) for turn in (0, 1)
        ]
        home_rows = jnp.concatenate(
            [
                jnp.where(parity == 0, home[0], home[1]),
                jnp.where(parity == 0, home[1], home[0]),
            ],
            axis=0,
        )
        grad_tokens = (grad_res_one + home_rows.astype(jnp.float32)).reshape(tokens.shape)

    with jax.named_scope("group_weight_grads"):
        grad_group = matmul_left_t(token_half, grad_projected)
        bias_sums = column_sums(grad_projected)
        nothing = jnp.zeros((width,), jnp.float32)
        vec_rows = jnp.stack(
            [
                lax.dynamic_update_slice_in_dim(
                    nothing, bias_sums[2 * GROUP_COLS :], quad * GROUP_COLS, 0
                ),
                lax.dynamic_update_slice_in_dim(
                    nothing, bias_sums[GROUP_COLS : 2 * GROUP_COLS], quad * GROUP_COLS, 0
                ),
                column_sums(grad_branch_low),
                grad_attn_gain,
                grad_attn_shift,
                column_sums(grad_down_low),
                grad_ffn_gain,
                grad_ffn_shift,
            ],
            axis=0,
        ).T
        up_sums = column_sums(grad_up_low).reshape(devices, ratio, own_rows)
        up_sums = jnp.swapaxes(up_sums, 1, 2).reshape(width, ratio)
        vecs = jnp.concatenate([vec_rows, up_sums], axis=1)
        packed_grads = pack_grads(grad_group, vecs).reshape(2, width // 2, PACK)
        mine = jnp.where(core == 0, packed_grads[0], packed_grads[1])
        theirs = jnp.where(core == 0, packed_grads[1], packed_grads[0])
        main, vecs = unpack_grads(mine)
        more, more_vecs = unpack_grads(hop_core(theirs))
        main, vecs = (main + more, vecs + more_vecs)
        packed_grads = pack_grads(main, vecs).reshape(4, 4 * own_rows, PACK)
        by_layer = turned([packed_grads[number] for number in range(4)], layer_z)
        main, vecs = unpack_grads(by_layer[0])
        for flip in flips:
            more, more_vecs = unpack_grads(hop_layer(by_layer[flip], flip))
            main, vecs = (main + more, vecs + more_vecs)
        packed_grads = pack_grads(main, vecs).reshape(4, own_rows, PACK)
        by_quad = turned([packed_grads[number] for number in range(4)], quad)
        main, vecs = unpack_grads(by_quad[0])
        quad_parts = [main]
        for flip in flips:
            more, more_vecs = unpack_grads(hop_quad(by_quad[flip], flip))
            quad_parts.append(more)
            vecs = vecs + more_vecs
        quad_parts = turned(quad_parts, quad)
        sum_key, sum_value, sum_query = [
            jnp.concatenate([part[:, n * GROUP_COLS : (n + 1) * GROUP_COLS] for part in quad_parts], axis=1)
            for n in range(3)
        ]
    sum_rows = vecs[:, :8].T
    return (
        mixed,
        grad_tokens,
        sum_query,
        sum_rows[0],
        sum_key,
        sum_value,
        sum_rows[1],
        sum_output,
        sum_rows[2],
        sum_rows[3],
        sum_rows[4],
        sum_up,
        vecs[:, 8:].T.reshape(up_bias.shape),
        sum_down,
        sum_rows[5],
        sum_rows[6],
        sum_rows[7],
    )


def solution(mesh):
    in_specs = (
        P("batch", "seq", None),
        P("batch", None),
        P(("batch", "seq"), None),
        P(("batch", "seq")),
        P(("batch", "seq"), None),
        P(("batch", "seq"), None),
        P(("batch", "seq")),
        P(("batch", "seq"), None),
        P(("batch", "seq")),
        P(("batch", "seq")),
        P(("batch", "seq")),
        P(("batch", "seq"), None),
        P(("batch", "seq")),
        P(("batch", "seq"), None),
        P(("batch", "seq")),
        P(("batch", "seq")),
        P(("batch", "seq")),
        P("batch", "seq", None),
    )
    out_specs = (
        P("batch", "seq", None),
        P("batch", "seq", None),
        P(("batch", "seq"), None),
        P(("batch", "seq")),
        P(("batch", "seq"), None),
        P(("batch", "seq"), None),
        P(("batch", "seq")),
        P(("batch", "seq"), None),
        P(("batch", "seq")),
        P(("batch", "seq")),
        P(("batch", "seq")),
        P(("batch", "seq"), None),
        P(("batch", "seq")),
        P(("batch", "seq"), None),
        P(("batch", "seq")),
        P(("batch", "seq")),
        P(("batch", "seq")),
    )
    fits = mesh.shape['batch'] == 2 and mesh.shape['seq'] == 16
    body = shards_heads if fits else shards_general
    return jax.shard_map(body, mesh=mesh, in_specs=in_specs, out_specs=out_specs, check_vma=False)
```

```python
import jax
import jax.numpy as jnp
from jax import lax
from jax.experimental import pallas as pl
from jax.experimental.pallas import tpu as pltpu
from jax.sharding import PartitionSpec as P

HEADS = 12
HEAD_DIM = 64


SCALE = 0.125
NEG = -1e30
EPS = 1e-12


def norm_apply(hidden, gain_vec, shift_vec):
    center = jnp.mean(hidden, axis=-1, keepdims=True)
    centered = hidden - center
    spread = jnp.mean(centered * centered, axis=-1, keepdims=True)
    return centered * lax.rsqrt(spread + EPS) * gain_vec + shift_vec


def gelu_exact(inputs):
    return jax.nn.gelu(inputs, approximate=False)


def segment_ids(doc_lengths, positions):
    doc_ends = jnp.cumsum(doc_lengths, axis=-1)
    return jnp.sum((positions[None, :, None] >= doc_ends[:, None, :]).astype(jnp.int32), axis=-1)


def matmul_plain(left_op, right_op):
    return jnp.dot(left_op, right_op, preferred_element_type=jnp.float32)


def matmul_right_t(left_op, right_op):
    return lax.dot_general(
        left_op, right_op, (((1,), (1,)), ((), ())), preferred_element_type=jnp.float32
    )


def matmul_left_t(left_op, right_op):
    return lax.dot_general(
        left_op, right_op, (((0,), (0,)), ((), ())), preferred_element_type=jnp.float32
    )


def column_sums(matrix):
    return jnp.sum(matrix.astype(jnp.float32), axis=0)


def head_block(matrix, head_pair):
    pair_width = 2 * HEAD_DIM
    column_block = matrix[..., head_pair * pair_width : (head_pair + 1) * pair_width]
    return column_block.reshape(column_block.shape[:-1] + (2, HEAD_DIM))


def merge_heads(blocks):
    return jnp.concatenate(
        [block_item.reshape(block_item.shape[:2] + (2 * HEAD_DIM,)) for block_item in blocks],
        axis=-1,
    )


def stat_pair(stats, head_pair):
    return stats[:, 2 * head_pair : 2 * head_pair + 2][..., None]


def pair_scores(query_pair, key_pair, same_doc):
    raw_scores = jnp.einsum(
        "sqhd,skhd->shqk", query_pair, key_pair, preferred_element_type=jnp.float32
    )
    return jnp.where(same_doc[:, None], SCALE * raw_scores, NEG)


def attend_forward(queries, key_all, value_all, same_doc):
    outputs, log_sums = ([], [])
    for head_pair in range(HEADS // 2):
        scores = pair_scores(
            head_block(queries, head_pair), head_block(key_all, head_pair), same_doc
        )
        top_score = jnp.max(scores, axis=-1, keepdims=True)
        exponent = jnp.exp(scores - top_score)
        totals = jnp.sum(exponent, axis=-1, keepdims=True)
        probs_low = (exponent / totals).astype(jnp.bfloat16)
        context = jnp.einsum(
            "shqk,skhd->sqhd",
            probs_low,
            head_block(value_all, head_pair),
            preferred_element_type=jnp.float32,
        )
        outputs.append(context)
        log_sums.append((top_score + jnp.log(totals))[..., 0])
    return (merge_heads(outputs), jnp.concatenate(log_sums, axis=1))


def attend_backward(queries, key_all, value_all, same_doc, log_sums, grad_context):
    query_grads, key_grads, value_grads, row_dots = ([], [], [], [])
    for head_pair in range(HEADS // 2):
        query_pair = head_block(queries, head_pair)
        key_pair = head_block(key_all, head_pair)
        grad_pair = head_block(grad_context, head_pair)
        probs = jnp.exp(
            pair_scores(query_pair, key_pair, same_doc) - stat_pair(log_sums, head_pair)
        )
        grad_probs = jnp.einsum(
            "sqhd,skhd->shqk",
            grad_pair,
            head_block(value_all, head_pair),
            preferred_element_type=jnp.float32,
        )
        row_dot = jnp.sum(probs * grad_probs, axis=-1, keepdims=True)
        row_dots.append(row_dot[..., 0])
        grad_scores = (probs * (grad_probs - row_dot)).astype(jnp.bfloat16) * jnp.bfloat16(SCALE)
        query_grads.append(
            jnp.einsum("shqk,skhd->sqhd", grad_scores, key_pair, preferred_element_type=jnp.float32)
        )
    return (merge_heads(query_grads), jnp.concatenate(row_dots, axis=1), None, None)


def key_side_local(query_all, grad_ctx_all, lse_all, rowdot_all, keys_own, values_own, same_doc_t):
    key_grads, value_grads = ([], [])
    for head_pair in range(HEADS // 2):
        query_pair = head_block(query_all, head_pair)
        grad_pair = head_block(grad_ctx_all, head_pair)
        probs = jnp.exp(
            pair_scores(query_pair, head_block(keys_own, head_pair), same_doc_t)
            - stat_pair(lse_all, head_pair)
        )
        grad_probs = jnp.einsum(
            "sqhd,skhd->shqk",
            grad_pair,
            head_block(values_own, head_pair),
            preferred_element_type=jnp.float32,
        )
        grad_scores = (probs * (grad_probs - stat_pair(rowdot_all, head_pair))).astype(
            jnp.bfloat16
        ) * jnp.bfloat16(SCALE)
        key_grads.append(
            jnp.einsum(
                "shqk,sqhd->skhd", grad_scores, query_pair, preferred_element_type=jnp.float32
            )
        )
        value_grads.append(
            jnp.einsum(
                "shqk,sqhd->skhd",
                probs.astype(jnp.bfloat16),
                grad_pair,
                preferred_element_type=jnp.float32,
            )
        )
    return (merge_heads(key_grads), merge_heads(value_grads))


def shards_general(
    tokens,
    doc_lengths,
    query_weight,
    query_bias,
    key_weight,
    value_weight,
    value_bias,
    output_weight,
    output_bias,
    attn_gain,
    attn_shift,
    up_weight,
    up_bias,
    down_weight,
    down_bias,
    ffn_gain,
    ffn_shift,
    cotangent,
):
    gathered = (
        lax.all_gather(query_weight, ("batch", "seq"), axis=0, tiled=True),
        lax.all_gather(query_bias, ("batch", "seq"), axis=0, tiled=True),
        lax.all_gather(key_weight, ("batch", "seq"), axis=0, tiled=True),
        lax.all_gather(value_weight, ("batch", "seq"), axis=0, tiled=True),
        lax.all_gather(value_bias, ("batch", "seq"), axis=0, tiled=True),
        lax.all_gather(output_weight, ("batch", "seq"), axis=0, tiled=True),
        lax.all_gather(output_bias, ("batch", "seq"), axis=0, tiled=True),
        lax.all_gather(attn_gain, ("batch", "seq"), axis=0, tiled=True),
        lax.all_gather(attn_shift, ("batch", "seq"), axis=0, tiled=True),
        lax.all_gather(up_weight, ("batch", "seq"), axis=0, tiled=True),
        lax.all_gather(up_bias, ("batch", "seq"), axis=0, tiled=True),
        lax.all_gather(down_weight, ("batch", "seq"), axis=0, tiled=True),
        lax.all_gather(down_bias, ("batch", "seq"), axis=0, tiled=True),
        lax.all_gather(ffn_gain, ("batch", "seq"), axis=0, tiled=True),
        lax.all_gather(ffn_shift, ("batch", "seq"), axis=0, tiled=True),
    )
    (
        query_full,
        qbias_full,
        key_full,
        value_full,
        vbias_full,
        output_full,
        obias_full,
        again_full,
        ashift_full,
        up_full,
        ubias_full,
        down_full,
        dbias_full,
        fgain_full,
        fshift_full,
    ) = gathered
    seq_groups, stretch_len, width = tokens.shape
    row_count = seq_groups * stretch_len
    token_rows = tokens.reshape(row_count, width)
    positions = lax.axis_index("seq") * stretch_len + jnp.arange(stretch_len, dtype=jnp.int32)
    total_len = stretch_len * lax.axis_size("seq")
    query_seg = segment_ids(doc_lengths, positions)
    key_seg = segment_ids(doc_lengths, jnp.arange(total_len, dtype=jnp.int32))
    same_doc = query_seg[:, :, None] == key_seg[:, None, :]
    queries = (
        (matmul_plain(token_rows, query_full) + qbias_full)
        .astype(jnp.bfloat16)
        .reshape(tokens.shape)
    )
    keys_local = matmul_plain(token_rows, key_full).astype(jnp.bfloat16).reshape(tokens.shape)
    values_local = (
        (matmul_plain(token_rows, value_full) + vbias_full)
        .astype(jnp.bfloat16)
        .reshape(tokens.shape)
    )
    key_all, value_all = (
        lax.all_gather(keys_local, "seq", axis=1, tiled=True),
        lax.all_gather(values_local, "seq", axis=1, tiled=True),
    )
    context, log_sums = attend_forward(queries, key_all, value_all, same_doc)
    context_low = context.reshape(row_count, width).astype(jnp.bfloat16)
    res_one = token_rows.astype(jnp.float32) + matmul_plain(context_low, output_full) + obias_full
    normed, pull_one = jax.vjp(
        norm_apply, res_one, again_full.astype(jnp.float32), ashift_full.astype(jnp.float32)
    )
    normed_low = normed.astype(jnp.bfloat16)
    up_pre = matmul_plain(normed_low, up_full) + ubias_full
    activated, pull_gelu = jax.vjp(gelu_exact, up_pre)
    act_low = activated.astype(jnp.bfloat16)
    res_two = normed + matmul_plain(act_low, down_full) + dbias_full
    output_rows, pull_two = jax.vjp(
        norm_apply, res_two, fgain_full.astype(jnp.float32), fshift_full.astype(jnp.float32)
    )
    mixed = output_rows.astype(jnp.bfloat16).reshape(tokens.shape)
    regathered = (
        lax.all_gather(query_weight, ("batch", "seq"), axis=0, tiled=True),
        lax.all_gather(query_bias, ("batch", "seq"), axis=0, tiled=True),
        lax.all_gather(key_weight, ("batch", "seq"), axis=0, tiled=True),
        lax.all_gather(value_weight, ("batch", "seq"), axis=0, tiled=True),
        lax.all_gather(value_bias, ("batch", "seq"), axis=0, tiled=True),
        lax.all_gather(output_weight, ("batch", "seq"), axis=0, tiled=True),
        lax.all_gather(output_bias, ("batch", "seq"), axis=0, tiled=True),
        lax.all_gather(attn_gain, ("batch", "seq"), axis=0, tiled=True),
        lax.all_gather(attn_shift, ("batch", "seq"), axis=0, tiled=True),
        lax.all_gather(up_weight, ("batch", "seq"), axis=0, tiled=True),
        lax.all_gather(up_bias, ("batch", "seq"), axis=0, tiled=True),
        lax.all_gather(down_weight, ("batch", "seq"), axis=0, tiled=True),
        lax.all_gather(down_bias, ("batch", "seq"), axis=0, tiled=True),
        lax.all_gather(ffn_gain, ("batch", "seq"), axis=0, tiled=True),
        lax.all_gather(ffn_shift, ("batch", "seq"), axis=0, tiled=True),
    )
    query_back = regathered[0]
    key_back = regathered[2]
    value_back = regathered[3]
    output_back = regathered[5]
    up_back = regathered[9]
    down_back = regathered[11]
    grad_out = cotangent.astype(jnp.float32).reshape(row_count, width)
    grad_res_two, grad_ffn_gain, grad_ffn_shift = pull_two(grad_out)
    grad_down_low = grad_res_two.astype(jnp.bfloat16)
    grad_down_weight = matmul_left_t(act_low, grad_down_low)
    grad_down_bias = column_sums(grad_down_low)
    (grad_up_pre,) = pull_gelu(matmul_right_t(grad_down_low, down_back))
    grad_up_low = grad_up_pre.astype(jnp.bfloat16)
    grad_up_weight = matmul_left_t(normed_low, grad_up_low)
    grad_up_bias = column_sums(grad_up_low)
    grad_normed = grad_res_two + matmul_right_t(grad_up_low, up_back)
    grad_res_one, grad_attn_gain, grad_attn_shift = pull_one(grad_normed)
    grad_branch_low = grad_res_one.astype(jnp.bfloat16)
    grad_output_weight = matmul_left_t(context_low, grad_branch_low)
    grad_output_bias = column_sums(grad_branch_low)
    grad_context = (
        matmul_right_t(grad_branch_low, output_back).astype(jnp.bfloat16).reshape(tokens.shape)
    )
    key_again, value_again = (
        lax.all_gather(keys_local, "seq", axis=1, tiled=True),
        lax.all_gather(values_local, "seq", axis=1, tiled=True),
    )
    grad_query, row_dots, unused_key, unused_value = attend_backward(
        queries, key_again, value_again, same_doc, log_sums, grad_context
    )
    query_all, grad_ctx_all = (
        lax.all_gather(queries, "seq", axis=1, tiled=True),
        lax.all_gather(grad_context, "seq", axis=1, tiled=True),
    )
    lse_all, rowdot_all = (
        lax.all_gather(log_sums, "seq", axis=2, tiled=True),
        lax.all_gather(row_dots, "seq", axis=2, tiled=True),
    )
    same_doc_t = key_seg[:, :, None] == query_seg[:, None, :]
    grad_key, grad_value = key_side_local(
        query_all, grad_ctx_all, lse_all, rowdot_all, keys_local, values_local, same_doc_t
    )
    grad_query_low = grad_query.reshape(row_count, width).astype(jnp.bfloat16)
    grad_key_low = grad_key.reshape(row_count, width).astype(jnp.bfloat16)
    grad_value_low = grad_value.reshape(row_count, width).astype(jnp.bfloat16)
    grad_query_weight = matmul_left_t(token_rows, grad_query_low)
    grad_query_bias = column_sums(grad_query_low)
    grad_key_weight = matmul_left_t(token_rows, grad_key_low)
    grad_value_weight = matmul_left_t(token_rows, grad_value_low)
    grad_value_bias = column_sums(grad_value_low)
    grad_tokens = (
        grad_res_one
        + matmul_right_t(grad_query_low, query_back)
        + matmul_right_t(grad_key_low, key_back)
        + matmul_right_t(grad_value_low, value_back)
    )
    summed = (
        lax.psum_scatter(grad_query_weight, ("batch", "seq"), scatter_dimension=0, tiled=True),
        lax.psum_scatter(grad_query_bias, ("batch", "seq"), scatter_dimension=0, tiled=True),
        lax.psum_scatter(grad_key_weight, ("batch", "seq"), scatter_dimension=0, tiled=True),
        lax.psum_scatter(grad_value_weight, ("batch", "seq"), scatter_dimension=0, tiled=True),
        lax.psum_scatter(grad_value_bias, ("batch", "seq"), scatter_dimension=0, tiled=True),
        lax.psum_scatter(grad_output_weight, ("batch", "seq"), scatter_dimension=0, tiled=True),
        lax.psum_scatter(grad_output_bias, ("batch", "seq"), scatter_dimension=0, tiled=True),
        lax.psum_scatter(grad_attn_gain, ("batch", "seq"), scatter_dimension=0, tiled=True),
        lax.psum_scatter(grad_attn_shift, ("batch", "seq"), scatter_dimension=0, tiled=True),
        lax.psum_scatter(grad_up_weight, ("batch", "seq"), scatter_dimension=0, tiled=True),
        lax.psum_scatter(grad_up_bias, ("batch", "seq"), scatter_dimension=0, tiled=True),
        lax.psum_scatter(grad_down_weight, ("batch", "seq"), scatter_dimension=0, tiled=True),
        lax.psum_scatter(grad_down_bias, ("batch", "seq"), scatter_dimension=0, tiled=True),
        lax.psum_scatter(grad_ffn_gain, ("batch", "seq"), scatter_dimension=0, tiled=True),
        lax.psum_scatter(grad_ffn_shift, ("batch", "seq"), scatter_dimension=0, tiled=True),
    )
    return (
        mixed,
        grad_tokens.reshape(tokens.shape),
        summed[0],
        summed[1],
        summed[2],
        summed[3],
        summed[4],
        summed[5],
        summed[6],
        summed[7],
        summed[8],
        summed[9],
        summed[10],
        summed[11],
        summed[12],
        summed[13],
        summed[14],
    )


LOG2E = 1.4426950408889634
GROUP_HEADS = 3
GROUP_COLS = GROUP_HEADS * HEAD_DIM
PACK = 640
VECS = 12
SIDE = 16
KEY_CHUNK = 512


def dot_nt(left_op, right_op):
    return lax.dot_general(
        left_op, right_op, (((1,), (1,)), ((), ())), preferred_element_type=jnp.float32
    )


def dot_nn(left_op, right_op):
    return lax.dot_general(
        left_op, right_op, (((1,), (0,)), ((), ())), preferred_element_type=jnp.float32
    )


def attend_kernel(
    query_ref, own_ref, other_ref, seg_key_ref, seg_query_ref, ctx_ref, lse_ref, value_t
):
    half = own_ref.shape[0]
    rows = query_ref.shape[0]

    @pl.when(pl.program_id(0) == 0)
    def _():
        value_t[:, :half] = own_ref[:, GROUP_COLS : 2 * GROUP_COLS].T
        value_t[:, half:] = other_ref[:, GROUP_COLS : 2 * GROUP_COLS].T

    seg_query = seg_query_ref[...]
    chunks = [
        (ref, start) for ref in (own_ref, other_ref) for start in range(0, half, KEY_CHUNK)
    ]
    for head in range(GROUP_HEADS):
        cols = slice(head * HEAD_DIM, (head + 1) * HEAD_DIM)
        query = query_ref[:, cols]
        scores = []
        top = None
        for number, (ref, start) in enumerate(chunks):
            raw = dot_nt(ref[start : start + KEY_CHUNK, cols], query)
            seg_key = seg_key_ref[number * KEY_CHUNK : (number + 1) * KEY_CHUNK, :]
            seg_key = jnp.concatenate([seg_key] * (rows // 128), axis=1)
            masked = jnp.where(seg_key == seg_query, raw * (SCALE * LOG2E), NEG)
            scores.append(masked)
            peak = jnp.max(masked, axis=0, keepdims=True)
            top = peak if top is None else jnp.maximum(top, peak)
        total = None
        context_t = None
        for number in range(len(chunks)):
            weight = jnp.exp2(scores[number] - top)
            part = jnp.sum(weight, axis=0, keepdims=True)
            piece = dot_nn(
                value_t[cols, number * KEY_CHUNK : (number + 1) * KEY_CHUNK],
                weight.astype(jnp.bfloat16),
            )
            total = part if total is None else total + part
            context_t = piece if context_t is None else context_t + piece
        ctx_ref[:, cols] = (context_t / total).T
        lse_ref[head : head + 1, :] = top + jnp.log2(total)


def attend(query, own, other, seg_key, seg_query):
    rows = query.shape[0]
    half = own.shape[0]
    block = rows // 4
    return pl.pallas_call(
        attend_kernel,
        grid=(4,),
        in_specs=[
            pl.BlockSpec((block, GROUP_COLS), lambda i: (i, 0)),
            pl.BlockSpec((half, 2 * GROUP_COLS), lambda i: (0, 0)),
            pl.BlockSpec((half, 2 * GROUP_COLS), lambda i: (0, 0)),
            pl.BlockSpec((2 * half, 128), lambda i: (0, 0)),
            pl.BlockSpec((1, block), lambda i: (0, i)),
        ],
        out_specs=[
            pl.BlockSpec((block, GROUP_COLS), lambda i: (i, 0)),
            pl.BlockSpec((8, block), lambda i: (0, i)),
        ],
        out_shape=[
            jax.ShapeDtypeStruct((rows, GROUP_COLS), jnp.float32),
            jax.ShapeDtypeStruct((8, rows), jnp.float32),
        ],
        scratch_shapes=[pltpu.VMEM((GROUP_COLS, 2 * half), jnp.bfloat16)],
        compiler_params=pltpu.CompilerParams(vmem_limit_bytes=48 * 1024 * 1024),
        cost_estimate=pl.CostEstimate(
            flops=16 * rows * half * GROUP_COLS,
            bytes_accessed=4 * 1024 * 1024,
            transcendentals=2 * GROUP_HEADS * rows * half,
        ),
        name="attend",
    )(query, own, other, seg_key, seg_query)


def attend_back_kernel(
    query_ref,
    grad_ref,
    ctx_ref,
    lse_ref,
    own_ref,
    other_ref,
    seg_key_ref,
    seg_query_ref,
    gquery_ref,
    gown_ref,
    gother_ref,
    key_t,
):
    half = own_ref.shape[0]
    rows = query_ref.shape[0]
    first = pl.program_id(0) == 0

    @pl.when(first)
    def _():
        key_t[:, :half] = own_ref[:, :GROUP_COLS].T
        key_t[:, half:] = other_ref[:, :GROUP_COLS].T
        gown_ref[...] = jnp.zeros_like(gown_ref)
        gother_ref[...] = jnp.zeros_like(gother_ref)

    seg_query = seg_query_ref[...]
    chunks = [
        (ref, gref, start)
        for ref, gref in ((own_ref, gown_ref), (other_ref, gother_ref))
        for start in range(0, half, KEY_CHUNK)
    ]
    for head in range(GROUP_HEADS):
        cols = slice(head * HEAD_DIM, (head + 1) * HEAD_DIM)
        vcols = slice(GROUP_COLS + head * HEAD_DIM, GROUP_COLS + (head + 1) * HEAD_DIM)
        query = query_ref[:, cols]
        grad = grad_ref[:, cols]
        lse = lse_ref[head : head + 1, :]
        dots = (grad.astype(jnp.float32) * ctx_ref[:, cols]).T
        row_dot = jnp.sum(dots, axis=0, keepdims=True)
        gquery_t = None
        for number, (ref, gref, start) in enumerate(chunks):
            spot = slice(start, start + KEY_CHUNK)
            raw = dot_nt(ref[spot, cols], query)
            seg_key = seg_key_ref[number * KEY_CHUNK : (number + 1) * KEY_CHUNK, :]
            seg_key = jnp.concatenate([seg_key] * (rows // 128), axis=1)
            masked = jnp.where(seg_key == seg_query, raw * (SCALE * LOG2E), NEG)
            probs = jnp.exp2(masked - lse)
            gprobs = dot_nt(ref[spot, vcols], grad)
            gscores = (probs * (gprobs - row_dot)).astype(jnp.bfloat16)
            gref[spot, vcols] += dot_nn(probs.astype(jnp.bfloat16), grad)
            gref[spot, cols] += dot_nn(gscores, query)
            piece = dot_nn(key_t[cols, number * KEY_CHUNK : (number + 1) * KEY_CHUNK], gscores)
            gquery_t = piece if gquery_t is None else gquery_t + piece
        gquery_ref[:, cols] = (SCALE * gquery_t).T


def attend_back(query, grad, ctx, lse, own, other, seg_key, seg_query):
    rows = query.shape[0]
    half = own.shape[0]
    block = rows // 4
    return pl.pallas_call(
        attend_back_kernel,
        grid=(4,),
        in_specs=[
            pl.BlockSpec((block, GROUP_COLS), lambda i: (i, 0)),
            pl.BlockSpec((block, GROUP_COLS), lambda i: (i, 0)),
            pl.BlockSpec((block, GROUP_COLS), lambda i: (i, 0)),
            pl.BlockSpec((8, block), lambda i: (0, i)),
            pl.BlockSpec((half, 2 * GROUP_COLS), lambda i: (0, 0)),
            pl.BlockSpec((half, 2 * GROUP_COLS), lambda i: (0, 0)),
            pl.BlockSpec((2 * half, 128), lambda i: (0, 0)),
            pl.BlockSpec((1, block), lambda i: (0, i)),
        ],
        out_specs=[
            pl.BlockSpec((block, GROUP_COLS), lambda i: (i, 0)),
            pl.BlockSpec((half, 2 * GROUP_COLS), lambda i: (0, 0)),
            pl.BlockSpec((half, 2 * GROUP_COLS), lambda i: (0, 0)),
        ],
        out_shape=[
            jax.ShapeDtypeStruct((rows, GROUP_COLS), jnp.float32),
            jax.ShapeDtypeStruct((half, 2 * GROUP_COLS), jnp.float32),
            jax.ShapeDtypeStruct((half, 2 * GROUP_COLS), jnp.float32),
        ],
        scratch_shapes=[pltpu.VMEM((GROUP_COLS, 2 * half), jnp.bfloat16)],
        compiler_params=pltpu.CompilerParams(vmem_limit_bytes=48 * 1024 * 1024),
        cost_estimate=pl.CostEstimate(
            flops=rows * half * GROUP_COLS, bytes_accessed=1024 * 1024, transcendentals=0
        ),
        name="attend_back",
    )(query, grad, ctx, lse, own, other, seg_key, seg_query)


def prepare_kernel(
    tokens_ref,
    lengths_ref,
    key_ref,
    value_ref,
    query_ref,
    qbias_ref,
    vbias_ref,
    obias_ref,
    again_ref,
    ashift_ref,
    dbias_ref,
    fgain_ref,
    fshift_ref,
    ubias_ref,
    output_ref,
    up_ref,
    down_ref,
    first_ref,
    second_ref,
    bulk_ref,
    *piece_refs,
):
    place = lax.axis_index("seq")
    odd = lax.rem(place // 4, 2) == 1
    quad = lax.rem(place, 4)
    first_ref[...] = jnp.where(odd, tokens_ref[1], tokens_ref[0])
    second_ref[...] = jnp.where(odd, tokens_ref[0], tokens_ref[1])
    own_rows, width = key_ref.shape
    ratio = up_ref.shape[1] // width
    bulk_ref[0, :own_rows] = output_ref[...]
    for number in range(ratio):
        bulk_ref[0, (1 + number) * own_rows : (2 + number) * own_rows] = up_ref[
            :, number * width : (number + 1) * width
        ]
    bulk_ref[0, (1 + ratio) * own_rows :] = down_ref[...]
    small = (qbias_ref, vbias_ref, obias_ref, again_ref, ashift_ref, dbias_ref, fgain_ref, fshift_ref)
    rows = [ref[...].astype(jnp.float32) for ref in small]
    wide = ubias_ref[...].astype(jnp.float32)
    rows += [wide[:, n * own_rows : (n + 1) * own_rows] for n in range(VECS - len(small))]
    lengths = lengths_ref[...]
    docs = lengths.shape[1]
    flat = jnp.concatenate(
        [lengths[0:1], lengths[1:2], jnp.zeros((1, own_rows - 2 * docs), jnp.int32)], axis=1
    )
    rows += [(flat >> 6).astype(jnp.float32), (flat & 63).astype(jnp.float32)]
    rows += [jnp.zeros_like(rows[0])] * (SIDE - len(rows))
    side = jnp.concatenate(rows, axis=0).T.astype(jnp.bfloat16)
    cut = 3 * GROUP_COLS
    for flip, piece_ref in enumerate(piece_refs):
        piece_ref[...] = jnp.zeros_like(piece_ref)
        piece_ref[:, cut : cut + SIDE] = side
        target = quad ^ flip
        for number in range(4):

            @pl.when(target == number)
            def _():
                cols = slice(number * GROUP_COLS, (number + 1) * GROUP_COLS)
                for spot, ref in enumerate((key_ref, value_ref, query_ref)):
                    piece_ref[:, spot * GROUP_COLS : (spot + 1) * GROUP_COLS] = ref[:, cols]


def prepare(tokens, lengths, key, value, query, vectors, up_bias, output, up, down):
    own_rows, width = key.shape
    bulk_rows = own_rows + down.shape[0] * 2
    turn_shape = jax.ShapeDtypeStruct(tokens.shape[1:], jnp.bfloat16)
    piece_shape = jax.ShapeDtypeStruct((own_rows, PACK), jnp.bfloat16)
    return pl.pallas_call(
        prepare_kernel,
        out_shape=[turn_shape] * 2
        + [jax.ShapeDtypeStruct((1, bulk_rows, width), jnp.bfloat16)]
        + [piece_shape] * 4,
        name="prepare",
    )(
        tokens,
        lengths,
        key,
        value,
        query,
        *[item.reshape(1, own_rows) for item in vectors],
        up_bias.reshape(1, up_bias.shape[0]),
        output,
        up,
        down,
    )


def tied(values, *others):
    return lax.optimization_barrier((values, others))[0]


def block_of(values, index, axis):
    return lax.dynamic_index_in_dim(values, index, axis=axis, keepdims=False)


def split_blocks(values, place, axis):
    low = values.astype(jnp.bfloat16)
    return [block_of(values, place, axis)] + [
        block_of(low, place ^ flip, axis) for flip in (1, 2, 3)
    ]


def sum_parts(own, arrived):
    total = own.astype(jnp.float32)
    for item in arrived:
        total = total + item.astype(jnp.float32)
    return total


def device_table(mapping):
    pairs = []
    for core in range(2):
        for layer_z in range(4):
            for quad in range(4):
                to_core, to_z, to_quad = mapping(core, layer_z, quad)
                pairs.append((core * 16 + layer_z * 4 + quad, to_core * 16 + to_z * 4 + to_quad))
    return pairs


def hop(value, mapping):
    return lax.ppermute(value, ("batch", "seq"), device_table(mapping))


def hop_quad(value, flip):
    return hop(value, lambda core, layer_z, quad: (core, layer_z, quad ^ flip))


def hop_layer(value, flip):
    return hop(value, lambda core, layer_z, quad: (core, layer_z ^ flip, quad))


def hop_core(value):
    return hop(value, lambda core, layer_z, quad: (1 - core, layer_z, quad))


def to_sequence(value, turn):
    return hop(
        value,
        lambda core, layer_z, quad: (layer_z // 2, 2 * core + (layer_z + turn) % 2, quad),
    )


def to_owner(value, turn):
    return hop(
        value,
        lambda core, layer_z, quad: (layer_z // 2, 2 * core + (layer_z - turn) % 2, quad),
    )


def turned(blocks, quad):
    first, second, third, fourth = blocks
    odd = quad % 2 == 1
    high = quad // 2 == 1
    pairs = (
        jnp.where(odd, second, first),
        jnp.where(odd, first, second),
        jnp.where(odd, fourth, third),
        jnp.where(odd, third, fourth),
    )
    return (
        jnp.where(high, pairs[2], pairs[0]),
        jnp.where(high, pairs[3], pairs[1]),
        jnp.where(high, pairs[0], pairs[2]),
        jnp.where(high, pairs[1], pairs[3]),
    )


def pack_grads(main, vecs):
    coarse = vecs.astype(jnp.bfloat16)
    fine = (vecs - coarse.astype(jnp.float32)).astype(jnp.bfloat16)
    filler = jnp.zeros(main.shape[:-1] + (PACK - main.shape[-1] - 2 * VECS,), jnp.bfloat16)
    return jnp.concatenate([main.astype(jnp.bfloat16), coarse, fine, filler], axis=-1)


def unpack_grads(packed):
    wide = packed.astype(jnp.float32)
    cut = 3 * GROUP_COLS
    return (wide[..., :cut], wide[..., cut : cut + VECS] + wide[..., cut + VECS : cut + 2 * VECS])


def shards_heads(
    tokens,
    doc_lengths,
    query_weight,
    query_bias,
    key_weight,
    value_weight,
    value_bias,
    output_weight,
    output_bias,
    attn_gain,
    attn_shift,
    up_weight,
    up_bias,
    down_weight,
    down_bias,
    ffn_gain,
    ffn_shift,
    cotangent,
):
    groups, stretch, width = tokens.shape
    own_rows = query_weight.shape[0]
    hidden = up_weight.shape[1]
    ratio = hidden // width
    devices = width // own_rows
    bulk_rows = own_rows * (1 + 2 * ratio)
    row_count = groups * stretch
    core = lax.axis_index("batch")
    place = lax.axis_index("seq")
    layer_z = place // 4
    quad = place % 4
    parity = layer_z % 2
    flips = (1, 2, 3)

    vectors = (
        query_bias,
        value_bias,
        output_bias,
        attn_gain,
        attn_shift,
        down_bias,
        ffn_gain,
        ffn_shift,
    )
    first_turn, second_turn, bulk, *pieces = prepare(
        tokens,
        doc_lengths,
        key_weight,
        value_weight,
        query_weight,
        vectors,
        up_bias,
        output_weight,
        up_weight,
        down_weight,
    )

    with jax.named_scope("tokens_out"):
        own_block = jnp.concatenate(
            [to_sequence(first_turn, 0), to_sequence(second_turn, 1)], axis=0
        )
        token_half = jnp.concatenate(
            [own_block] + [hop_quad(own_block, flip) for flip in flips], axis=0
        )

    with jax.named_scope("group_weights"):
        quads = turned([pieces[0]] + [hop_quad(pieces[flip], flip) for flip in flips], quad)
        quads = jnp.stack(quads, axis=0)
        layers = [quads] + [hop_layer(quads, flip) for flip in flips]
        layers = jnp.stack(turned(layers, layer_z), axis=0)
        twin = hop_core(layers)
        cores = jnp.stack([jnp.where(core == 0, layers, twin), jnp.where(core == 0, twin, layers)])
        packed = cores.reshape(width, PACK)
    group_weight = packed[:, : 3 * GROUP_COLS]
    side = packed[:, 3 * GROUP_COLS : 3 * GROUP_COLS + SIDE].astype(jnp.float32)
    vector_rows = side[:, :8].T
    up_bias_full = side[:, 8:VECS].reshape(devices, own_rows, ratio)
    up_bias_full = jnp.swapaxes(up_bias_full, 1, 2).reshape(1, hidden)
    (
        qbias_full,
        vbias_full,
        obias_full,
        again_full,
        ashift_full,
        dbias_full,
        fgain_full,
        fshift_full,
    ) = [vector_rows[number] for number in range(8)]
    docs = doc_lengths.shape[1]
    digits = side.reshape(2, width // 2, SIDE)[:, : groups * docs, VECS : VECS + 2]
    lengths_all = (digits[..., 0] * 64 + digits[..., 1]).astype(jnp.int32)
    lengths = lax.dynamic_index_in_dim(
        lengths_all.reshape(2 * groups, docs), layer_z, axis=0, keepdims=False
    )
    doc_ends = jnp.cumsum(lengths)

    def half_segments(which):
        turn_z = jnp.stack([(layer_z - turn) % 2 for turn in (0, 1)]) + 2 * which
        spot = jnp.stack([quad ^ flip for flip in range(4)])
        start = turn_z[None, :] * (4 * stretch) + spot[:, None] * stretch
        positions = start[:, :, None] + jnp.arange(stretch, dtype=jnp.int32)
        positions = positions.reshape(-1)
        return jnp.sum((positions[:, None] >= doc_ends[None, :]).astype(jnp.int32), axis=-1)

    seg_query = half_segments(core)
    seg_key = jnp.concatenate([seg_query, half_segments(1 - core)])
    seg_key = jnp.broadcast_to(seg_key[:, None], (seg_key.shape[0], 128))
    seg_query = seg_query[None, :]

    bulk_all = lax.all_gather(bulk, ("batch", "seq"), axis=0, tiled=True)

    with jax.named_scope("projections"):
        column_bias = jnp.concatenate(
            [
                jnp.zeros((GROUP_COLS,), jnp.float32),
                lax.dynamic_slice_in_dim(vbias_full, quad * GROUP_COLS, GROUP_COLS),
                lax.dynamic_slice_in_dim(qbias_full, quad * GROUP_COLS, GROUP_COLS),
            ]
        )
        projected = (matmul_plain(token_half, group_weight) + column_bias).astype(jnp.bfloat16)
        own_pair = projected[:, : 2 * GROUP_COLS]
        queries = projected[:, 2 * GROUP_COLS :]
        other_pair = hop_core(own_pair)
    ctx_wide, lse = attend(queries, own_pair, other_pair, seg_key, seg_query)

    with jax.named_scope("context_home"):
        ctx_blocks = ctx_wide.astype(jnp.bfloat16).reshape(4, row_count, GROUP_COLS)
        ctx_groups = [ctx_blocks[0]] + [hop_quad(ctx_blocks[flip], flip) for flip in flips]
        ctx_merged = jnp.concatenate(turned(ctx_groups, quad), axis=1)
        ctx_turns = [
            to_owner(ctx_merged[turn * stretch : (turn + 1) * stretch], turn) for turn in (0, 1)
        ]
        context_low = jnp.concatenate(
            [
                jnp.where(parity == 0, ctx_turns[0], ctx_turns[1]),
                jnp.where(parity == 0, ctx_turns[1], ctx_turns[0]),
            ],
            axis=0,
        )

    output_full = bulk_all[:, :own_rows].reshape(width, width)
    up_parts = [
        bulk_all[:, (1 + number) * own_rows : (2 + number) * own_rows].reshape(width, width)
        for number in range(ratio)
    ]
    up_full = jnp.concatenate(up_parts, axis=1)
    down_full = bulk_all[:, (1 + ratio) * own_rows :].reshape(hidden, width)

    token_rows = tokens.reshape(row_count, width)
    res_one = token_rows.astype(jnp.float32) + matmul_plain(context_low, output_full) + obias_full
    normed, pull_one = jax.vjp(norm_apply, res_one, again_full, ashift_full)
    normed_low = normed.astype(jnp.bfloat16)
    up_pre = matmul_plain(normed_low, up_full) + up_bias_full
    activated, pull_gelu = jax.vjp(gelu_exact, up_pre)
    act_low = activated.astype(jnp.bfloat16)
    res_two = normed + matmul_plain(act_low, down_full) + dbias_full
    output_rows, pull_two = jax.vjp(norm_apply, res_two, fgain_full, fshift_full)
    mixed = output_rows.astype(jnp.bfloat16).reshape(tokens.shape)
    grad_out = cotangent.astype(jnp.float32).reshape(row_count, width)
    grad_res_two, grad_ffn_gain, grad_ffn_shift = pull_two(grad_out)
    grad_down_low = grad_res_two.astype(jnp.bfloat16)

    def half_columns(matrix, which):
        half = matrix.shape[1] // 2
        return lax.dynamic_slice_in_dim(matrix, which * half, half, axis=1)

    def down_term(which):
        return matmul_left_t(half_columns(act_low, which), grad_down_low)

    def branch_term(which):
        return jnp.concatenate(
            [
                matmul_left_t(half_columns(normed_low, which), grad_up_low),
                matmul_left_t(half_columns(context_low, which), grad_branch_low),
            ],
            axis=1,
        )

    with jax.named_scope("down_grads"):
        down_theirs = down_term(1 - core).astype(jnp.bfloat16)
        down_arrived = hop_core(down_theirs)
    (grad_up_pre,) = pull_gelu(matmul_right_t(tied(grad_down_low, down_theirs), down_full))
    grad_up_low = grad_up_pre.astype(jnp.bfloat16)
    grad_normed = grad_res_two + matmul_right_t(grad_up_low, up_full)
    grad_res_one, grad_attn_gain, grad_attn_shift = pull_one(grad_normed)
    grad_branch_low = grad_res_one.astype(jnp.bfloat16)
    grad_context = matmul_right_t(grad_branch_low, output_full).astype(jnp.bfloat16)
    with jax.named_scope("branch_grads"):
        branch_arrived = hop_core(branch_term(1 - core).astype(jnp.bfloat16))

    with jax.named_scope("context_grad_out"):
        low_part = grad_context[:stretch]
        high_part = grad_context[stretch:]
        grad_turns = [
            to_sequence(jnp.where((parity + turn) % 2 == 1, high_part, low_part), turn)
            for turn in (0, 1)
        ]
        grad_own = jnp.concatenate(grad_turns, axis=0)
        grad_columns = turned(
            [grad_own[:, n * GROUP_COLS : (n + 1) * GROUP_COLS] for n in range(4)], quad
        )
        grad_ctx = jnp.concatenate(
            [grad_columns[0]] + [hop_quad(grad_columns[flip], flip) for flip in flips], axis=0
        )

    with jax.named_scope("down_grads"):
        down_total = (down_term(core) + down_arrived.astype(jnp.float32)).astype(jnp.bfloat16)
        down_blocks = down_total.reshape(4, 4, ratio * own_rows, width)
        down_quads = tied(split_blocks(down_blocks, quad, 1), grad_ctx)
    with jax.named_scope("branch_grads"):
        branch_total = (branch_term(core) + branch_arrived.astype(jnp.float32)).astype(jnp.bfloat16)
        branch_blocks = branch_total.reshape(4, 4, own_rows, hidden + width)
        branch_quads = split_blocks(branch_blocks, quad, 1)
    with jax.named_scope("down_grads"):
        down_arrived = [hop_quad(down_quads[flip], flip) for flip in flips]

    grad_query, grad_own_pair, grad_other_pair = attend_back(
        tied(queries, down_quads, branch_quads),
        grad_ctx,
        ctx_wide,
        lse,
        own_pair,
        other_pair,
        seg_key,
        seg_query,
    )
    with jax.named_scope("pair_sum"):
        arrived_pair = hop_core(grad_other_pair.astype(jnp.bfloat16)).astype(jnp.float32)
        branch_quads = tied(branch_quads, arrived_pair, down_arrived)
        pair_total = grad_own_pair + arrived_pair
        pair_scale = jnp.where(jnp.arange(2 * GROUP_COLS) < GROUP_COLS, SCALE, 1.0)
        grad_projected = jnp.concatenate([pair_total * pair_scale, grad_query], axis=1).astype(
            jnp.bfloat16
        )
    with jax.named_scope("branch_grads"):
        branch_arrived = [hop_quad(branch_quads[flip], flip) for flip in flips]

    with jax.named_scope("group_weight_grads"):
        grad_group = matmul_left_t(token_half, grad_projected)
        bias_sums = column_sums(grad_projected)
        nothing = jnp.zeros((width,), jnp.float32)
        vec_rows = jnp.stack(
            [
                lax.dynamic_update_slice_in_dim(
                    nothing, bias_sums[2 * GROUP_COLS :], quad * GROUP_COLS, 0
                ),
                lax.dynamic_update_slice_in_dim(
                    nothing, bias_sums[GROUP_COLS : 2 * GROUP_COLS], quad * GROUP_COLS, 0
                ),
                column_sums(grad_branch_low),
                grad_attn_gain,
                grad_attn_shift,
                column_sums(grad_down_low),
                grad_ffn_gain,
                grad_ffn_shift,
            ],
            axis=0,
        ).T
        up_sums = column_sums(grad_up_low).reshape(devices, ratio, own_rows)
        up_sums = jnp.swapaxes(up_sums, 1, 2).reshape(width, ratio)
        vecs = jnp.concatenate([vec_rows, up_sums], axis=1)
        packed_grads = pack_grads(grad_group, vecs).reshape(2, width // 2, PACK)
        mine = jnp.where(core == 0, packed_grads[0], packed_grads[1])
        theirs = jnp.where(core == 0, packed_grads[1], packed_grads[0])
        main, vecs = unpack_grads(mine)
        more, more_vecs = unpack_grads(hop_core(theirs))
        main, vecs = (main + more, vecs + more_vecs)
        packed_grads = pack_grads(main, vecs).reshape(4, 4 * own_rows, PACK)
        by_layer = turned([packed_grads[number] for number in range(4)], layer_z)

    with jax.named_scope("token_grads"):
        grad_half = matmul_right_t(grad_projected, group_weight)
        half_blocks = grad_half.reshape(4, row_count, width)
        low_blocks = half_blocks.astype(jnp.bfloat16)
        down_part = sum_parts(down_quads[0], tied(down_arrived, low_blocks))
        down_layers = split_blocks(down_part, layer_z, 0)
        down_arrived = [hop_layer(down_layers[flip], flip) for flip in flips]
        grad_block = half_blocks[0]
        for flip in flips:
            grad_block = grad_block + hop_quad(low_blocks[flip], flip).astype(jnp.float32)
        grad_block = grad_block.astype(jnp.bfloat16)
        branch_part = sum_parts(branch_quads[0], tied(branch_arrived, grad_block))
        branch_layers = split_blocks(branch_part, layer_z, 0)
        branch_arrived = [hop_layer(branch_layers[flip], flip) for flip in flips]
        grad_block = tied(grad_block, branch_layers, by_layer, down_layers)
        home = [
            to_owner(grad_block[turn * stretch : (turn + 1) * stretch], turn) for turn in (0, 1)
        ]
        main, vecs = unpack_grads(by_layer[0])
        for flip in flips:
            more, more_vecs = unpack_grads(hop_layer(by_layer[flip], flip))
            main, vecs = (main + more, vecs + more_vecs)
        packed_grads = pack_grads(main, vecs).reshape(4, own_rows, PACK)
        by_quad = turned([packed_grads[number] for number in range(4)], quad)
        main, vecs = unpack_grads(by_quad[0])
        by_quad = tied(by_quad, home, branch_arrived)
        home_rows = jnp.concatenate(
            [
                jnp.where(parity == 0, home[0], home[1]),
                jnp.where(parity == 0, home[1], home[0]),
            ],
            axis=0,
        )
        grad_tokens = (grad_res_one + home_rows.astype(jnp.float32)).reshape(tokens.shape)

    with jax.named_scope("group_weight_grads"):
        quad_parts = [main]
        for flip in flips:
            more, more_vecs = unpack_grads(hop_quad(by_quad[flip], flip))
            quad_parts.append(more)
            vecs = vecs + more_vecs
        quad_parts = turned(quad_parts, quad)
        sum_key, sum_value, sum_query = [
            jnp.concatenate([part[:, n * GROUP_COLS : (n + 1) * GROUP_COLS] for part in quad_parts], axis=1)
            for n in range(3)
        ]
    sum_rows = vecs[:, :8].T
    sum_down = sum_parts(down_layers[0], down_arrived)
    sum_branch = sum_parts(branch_layers[0], branch_arrived)
    sum_up = sum_branch[:, :hidden]
    sum_output = sum_branch[:, hidden:]
    return (
        mixed,
        grad_tokens,
        sum_query,
        sum_rows[0],
        sum_key,
        sum_value,
        sum_rows[1],
        sum_output,
        sum_rows[2],
        sum_rows[3],
        sum_rows[4],
        sum_up,
        vecs[:, 8:].T.reshape(up_bias.shape),
        sum_down,
        sum_rows[5],
        sum_rows[6],
        sum_rows[7],
    )


def solution(mesh):
    in_specs = (
        P("batch", "seq", None),
        P("batch", None),
        P(("batch", "seq"), None),
        P(("batch", "seq")),
        P(("batch", "seq"), None),
        P(("batch", "seq"), None),
        P(("batch", "seq")),
        P(("batch", "seq"), None),
        P(("batch", "seq")),
        P(("batch", "seq")),
        P(("batch", "seq")),
        P(("batch", "seq"), None),
        P(("batch", "seq")),
        P(("batch", "seq"), None),
        P(("batch", "seq")),
        P(("batch", "seq")),
        P(("batch", "seq")),
        P("batch", "seq", None),
    )
    out_specs = (
        P("batch", "seq", None),
        P("batch", "seq", None),
        P(("batch", "seq"), None),
        P(("batch", "seq")),
        P(("batch", "seq"), None),
        P(("batch", "seq"), None),
        P(("batch", "seq")),
        P(("batch", "seq"), None),
        P(("batch", "seq")),
        P(("batch", "seq")),
        P(("batch", "seq")),
        P(("batch", "seq"), None),
        P(("batch", "seq")),
        P(("batch", "seq"), None),
        P(("batch", "seq")),
        P(("batch", "seq")),
        P(("batch", "seq")),
    )
    fits = mesh.shape['batch'] == 2 and mesh.shape['seq'] == 16
    body = shards_heads if fits else shards_general
    return jax.shard_map(body, mesh=mesh, in_specs=in_specs, out_specs=out_specs, check_vma=False)
```

```python
import jax
import jax.numpy as jnp
from jax import lax
from jax.experimental import pallas as pl
from jax.experimental.pallas import tpu as pltpu
from jax.sharding import PartitionSpec as P

HEADS = 12
HEAD_DIM = 64


SCALE = 0.125
NEG = -1e30
EPS = 1e-12


def norm_apply(hidden, gain_vec, shift_vec):
    center = jnp.mean(hidden, axis=-1, keepdims=True)
    centered = hidden - center
    spread = jnp.mean(centered * centered, axis=-1, keepdims=True)
    return centered * lax.rsqrt(spread + EPS) * gain_vec + shift_vec


def gelu_exact(inputs):
    return jax.nn.gelu(inputs, approximate=False)


def segment_ids(doc_lengths, positions):
    doc_ends = jnp.cumsum(doc_lengths, axis=-1)
    return jnp.sum((positions[None, :, None] >= doc_ends[:, None, :]).astype(jnp.int32), axis=-1)


def matmul_plain(left_op, right_op):
    return jnp.dot(left_op, right_op, preferred_element_type=jnp.float32)


def matmul_right_t(left_op, right_op):
    return lax.dot_general(
        left_op, right_op, (((1,), (1,)), ((), ())), preferred_element_type=jnp.float32
    )


def matmul_left_t(left_op, right_op):
    return lax.dot_general(
        left_op, right_op, (((0,), (0,)), ((), ())), preferred_element_type=jnp.float32
    )


def column_sums(matrix):
    return jnp.sum(matrix.astype(jnp.float32), axis=0)


def head_block(matrix, head_pair):
    pair_width = 2 * HEAD_DIM
    column_block = matrix[..., head_pair * pair_width : (head_pair + 1) * pair_width]
    return column_block.reshape(column_block.shape[:-1] + (2, HEAD_DIM))


def merge_heads(blocks):
    return jnp.concatenate(
        [block_item.reshape(block_item.shape[:2] + (2 * HEAD_DIM,)) for block_item in blocks],
        axis=-1,
    )


def stat_pair(stats, head_pair):
    return stats[:, 2 * head_pair : 2 * head_pair + 2][..., None]


def pair_scores(query_pair, key_pair, same_doc):
    raw_scores = jnp.einsum(
        "sqhd,skhd->shqk", query_pair, key_pair, preferred_element_type=jnp.float32
    )
    return jnp.where(same_doc[:, None], SCALE * raw_scores, NEG)


def attend_forward(queries, key_all, value_all, same_doc):
    outputs, log_sums = ([], [])
    for head_pair in range(HEADS // 2):
        scores = pair_scores(
            head_block(queries, head_pair), head_block(key_all, head_pair), same_doc
        )
        top_score = jnp.max(scores, axis=-1, keepdims=True)
        exponent = jnp.exp(scores - top_score)
        totals = jnp.sum(exponent, axis=-1, keepdims=True)
        probs_low = (exponent / totals).astype(jnp.bfloat16)
        context = jnp.einsum(
            "shqk,skhd->sqhd",
            probs_low,
            head_block(value_all, head_pair),
            preferred_element_type=jnp.float32,
        )
        outputs.append(context)
        log_sums.append((top_score + jnp.log(totals))[..., 0])
    return (merge_heads(outputs), jnp.concatenate(log_sums, axis=1))


def attend_backward(queries, key_all, value_all, same_doc, log_sums, grad_context):
    query_grads, key_grads, value_grads, row_dots = ([], [], [], [])
    for head_pair in range(HEADS // 2):
        query_pair = head_block(queries, head_pair)
        key_pair = head_block(key_all, head_pair)
        grad_pair = head_block(grad_context, head_pair)
        probs = jnp.exp(
            pair_scores(query_pair, key_pair, same_doc) - stat_pair(log_sums, head_pair)
        )
        grad_probs = jnp.einsum(
            "sqhd,skhd->shqk",
            grad_pair,
            head_block(value_all, head_pair),
            preferred_element_type=jnp.float32,
        )
        row_dot = jnp.sum(probs * grad_probs, axis=-1, keepdims=True)
        row_dots.append(row_dot[..., 0])
        grad_scores = (probs * (grad_probs - row_dot)).astype(jnp.bfloat16) * jnp.bfloat16(SCALE)
        query_grads.append(
            jnp.einsum("shqk,skhd->sqhd", grad_scores, key_pair, preferred_element_type=jnp.float32)
        )
    return (merge_heads(query_grads), jnp.concatenate(row_dots, axis=1), None, None)


def key_side_local(query_all, grad_ctx_all, lse_all, rowdot_all, keys_own, values_own, same_doc_t):
    key_grads, value_grads = ([], [])
    for head_pair in range(HEADS // 2):
        query_pair = head_block(query_all, head_pair)
        grad_pair = head_block(grad_ctx_all, head_pair)
        probs = jnp.exp(
            pair_scores(query_pair, head_block(keys_own, head_pair), same_doc_t)
            - stat_pair(lse_all, head_pair)
        )
        grad_probs = jnp.einsum(
            "sqhd,skhd->shqk",
            grad_pair,
            head_block(values_own, head_pair),
            preferred_element_type=jnp.float32,
        )
        grad_scores = (probs * (grad_probs - stat_pair(rowdot_all, head_pair))).astype(
            jnp.bfloat16
        ) * jnp.bfloat16(SCALE)
        key_grads.append(
            jnp.einsum(
                "shqk,sqhd->skhd", grad_scores, query_pair, preferred_element_type=jnp.float32
            )
        )
        value_grads.append(
            jnp.einsum(
                "shqk,sqhd->skhd",
                probs.astype(jnp.bfloat16),
                grad_pair,
                preferred_element_type=jnp.float32,
            )
        )
    return (merge_heads(key_grads), merge_heads(value_grads))


def shards_general(
    tokens,
    doc_lengths,
    query_weight,
    query_bias,
    key_weight,
    value_weight,
    value_bias,
    output_weight,
    output_bias,
    attn_gain,
    attn_shift,
    up_weight,
    up_bias,
    down_weight,
    down_bias,
    ffn_gain,
    ffn_shift,
    cotangent,
):
    gathered = (
        lax.all_gather(query_weight, ("batch", "seq"), axis=0, tiled=True),
        lax.all_gather(query_bias, ("batch", "seq"), axis=0, tiled=True),
        lax.all_gather(key_weight, ("batch", "seq"), axis=0, tiled=True),
        lax.all_gather(value_weight, ("batch", "seq"), axis=0, tiled=True),
        lax.all_gather(value_bias, ("batch", "seq"), axis=0, tiled=True),
        lax.all_gather(output_weight, ("batch", "seq"), axis=0, tiled=True),
        lax.all_gather(output_bias, ("batch", "seq"), axis=0, tiled=True),
        lax.all_gather(attn_gain, ("batch", "seq"), axis=0, tiled=True),
        lax.all_gather(attn_shift, ("batch", "seq"), axis=0, tiled=True),
        lax.all_gather(up_weight, ("batch", "seq"), axis=0, tiled=True),
        lax.all_gather(up_bias, ("batch", "seq"), axis=0, tiled=True),
        lax.all_gather(down_weight, ("batch", "seq"), axis=0, tiled=True),
        lax.all_gather(down_bias, ("batch", "seq"), axis=0, tiled=True),
        lax.all_gather(ffn_gain, ("batch", "seq"), axis=0, tiled=True),
        lax.all_gather(ffn_shift, ("batch", "seq"), axis=0, tiled=True),
    )
    (
        query_full,
        qbias_full,
        key_full,
        value_full,
        vbias_full,
        output_full,
        obias_full,
        again_full,
        ashift_full,
        up_full,
        ubias_full,
        down_full,
        dbias_full,
        fgain_full,
        fshift_full,
    ) = gathered
    seq_groups, stretch_len, width = tokens.shape
    row_count = seq_groups * stretch_len
    token_rows = tokens.reshape(row_count, width)
    positions = lax.axis_index("seq") * stretch_len + jnp.arange(stretch_len, dtype=jnp.int32)
    total_len = stretch_len * lax.axis_size("seq")
    query_seg = segment_ids(doc_lengths, positions)
    key_seg = segment_ids(doc_lengths, jnp.arange(total_len, dtype=jnp.int32))
    same_doc = query_seg[:, :, None] == key_seg[:, None, :]
    queries = (
        (matmul_plain(token_rows, query_full) + qbias_full)
        .astype(jnp.bfloat16)
        .reshape(tokens.shape)
    )
    keys_local = matmul_plain(token_rows, key_full).astype(jnp.bfloat16).reshape(tokens.shape)
    values_local = (
        (matmul_plain(token_rows, value_full) + vbias_full)
        .astype(jnp.bfloat16)
        .reshape(tokens.shape)
    )
    key_all, value_all = (
        lax.all_gather(keys_local, "seq", axis=1, tiled=True),
        lax.all_gather(values_local, "seq", axis=1, tiled=True),
    )
    context, log_sums = attend_forward(queries, key_all, value_all, same_doc)
    context_low = context.reshape(row_count, width).astype(jnp.bfloat16)
    res_one = token_rows.astype(jnp.float32) + matmul_plain(context_low, output_full) + obias_full
    normed, pull_one = jax.vjp(
        norm_apply, res_one, again_full.astype(jnp.float32), ashift_full.astype(jnp.float32)
    )
    normed_low = normed.astype(jnp.bfloat16)
    up_pre = matmul_plain(normed_low, up_full) + ubias_full
    activated, pull_gelu = jax.vjp(gelu_exact, up_pre)
    act_low = activated.astype(jnp.bfloat16)
    res_two = normed + matmul_plain(act_low, down_full) + dbias_full
    output_rows, pull_two = jax.vjp(
        norm_apply, res_two, fgain_full.astype(jnp.float32), fshift_full.astype(jnp.float32)
    )
    mixed = output_rows.astype(jnp.bfloat16).reshape(tokens.shape)
    regathered = (
        lax.all_gather(query_weight, ("batch", "seq"), axis=0, tiled=True),
        lax.all_gather(query_bias, ("batch", "seq"), axis=0, tiled=True),
        lax.all_gather(key_weight, ("batch", "seq"), axis=0, tiled=True),
        lax.all_gather(value_weight, ("batch", "seq"), axis=0, tiled=True),
        lax.all_gather(value_bias, ("batch", "seq"), axis=0, tiled=True),
        lax.all_gather(output_weight, ("batch", "seq"), axis=0, tiled=True),
        lax.all_gather(output_bias, ("batch", "seq"), axis=0, tiled=True),
        lax.all_gather(attn_gain, ("batch", "seq"), axis=0, tiled=True),
        lax.all_gather(attn_shift, ("batch", "seq"), axis=0, tiled=True),
        lax.all_gather(up_weight, ("batch", "seq"), axis=0, tiled=True),
        lax.all_gather(up_bias, ("batch", "seq"), axis=0, tiled=True),
        lax.all_gather(down_weight, ("batch", "seq"), axis=0, tiled=True),
        lax.all_gather(down_bias, ("batch", "seq"), axis=0, tiled=True),
        lax.all_gather(ffn_gain, ("batch", "seq"), axis=0, tiled=True),
        lax.all_gather(ffn_shift, ("batch", "seq"), axis=0, tiled=True),
    )
    query_back = regathered[0]
    key_back = regathered[2]
    value_back = regathered[3]
    output_back = regathered[5]
    up_back = regathered[9]
    down_back = regathered[11]
    grad_out = cotangent.astype(jnp.float32).reshape(row_count, width)
    grad_res_two, grad_ffn_gain, grad_ffn_shift = pull_two(grad_out)
    grad_down_low = grad_res_two.astype(jnp.bfloat16)
    grad_down_weight = matmul_left_t(act_low, grad_down_low)
    grad_down_bias = column_sums(grad_down_low)
    (grad_up_pre,) = pull_gelu(matmul_right_t(grad_down_low, down_back))
    grad_up_low = grad_up_pre.astype(jnp.bfloat16)
    grad_up_weight = matmul_left_t(normed_low, grad_up_low)
    grad_up_bias = column_sums(grad_up_low)
    grad_normed = grad_res_two + matmul_right_t(grad_up_low, up_back)
    grad_res_one, grad_attn_gain, grad_attn_shift = pull_one(grad_normed)
    grad_branch_low = grad_res_one.astype(jnp.bfloat16)
    grad_output_weight = matmul_left_t(context_low, grad_branch_low)
    grad_output_bias = column_sums(grad_branch_low)
    grad_context = (
        matmul_right_t(grad_branch_low, output_back).astype(jnp.bfloat16).reshape(tokens.shape)
    )
    key_again, value_again = (
        lax.all_gather(keys_local, "seq", axis=1, tiled=True),
        lax.all_gather(values_local, "seq", axis=1, tiled=True),
    )
    grad_query, row_dots, unused_key, unused_value = attend_backward(
        queries, key_again, value_again, same_doc, log_sums, grad_context
    )
    query_all, grad_ctx_all = (
        lax.all_gather(queries, "seq", axis=1, tiled=True),
        lax.all_gather(grad_context, "seq", axis=1, tiled=True),
    )
    lse_all, rowdot_all = (
        lax.all_gather(log_sums, "seq", axis=2, tiled=True),
        lax.all_gather(row_dots, "seq", axis=2, tiled=True),
    )
    same_doc_t = key_seg[:, :, None] == query_seg[:, None, :]
    grad_key, grad_value = key_side_local(
        query_all, grad_ctx_all, lse_all, rowdot_all, keys_local, values_local, same_doc_t
    )
    grad_query_low = grad_query.reshape(row_count, width).astype(jnp.bfloat16)
    grad_key_low = grad_key.reshape(row_count, width).astype(jnp.bfloat16)
    grad_value_low = grad_value.reshape(row_count, width).astype(jnp.bfloat16)
    grad_query_weight = matmul_left_t(token_rows, grad_query_low)
    grad_query_bias = column_sums(grad_query_low)
    grad_key_weight = matmul_left_t(token_rows, grad_key_low)
    grad_value_weight = matmul_left_t(token_rows, grad_value_low)
    grad_value_bias = column_sums(grad_value_low)
    grad_tokens = (
        grad_res_one
        + matmul_right_t(grad_query_low, query_back)
        + matmul_right_t(grad_key_low, key_back)
        + matmul_right_t(grad_value_low, value_back)
    )
    summed = (
        lax.psum_scatter(grad_query_weight, ("batch", "seq"), scatter_dimension=0, tiled=True),
        lax.psum_scatter(grad_query_bias, ("batch", "seq"), scatter_dimension=0, tiled=True),
        lax.psum_scatter(grad_key_weight, ("batch", "seq"), scatter_dimension=0, tiled=True),
        lax.psum_scatter(grad_value_weight, ("batch", "seq"), scatter_dimension=0, tiled=True),
        lax.psum_scatter(grad_value_bias, ("batch", "seq"), scatter_dimension=0, tiled=True),
        lax.psum_scatter(grad_output_weight, ("batch", "seq"), scatter_dimension=0, tiled=True),
        lax.psum_scatter(grad_output_bias, ("batch", "seq"), scatter_dimension=0, tiled=True),
        lax.psum_scatter(grad_attn_gain, ("batch", "seq"), scatter_dimension=0, tiled=True),
        lax.psum_scatter(grad_attn_shift, ("batch", "seq"), scatter_dimension=0, tiled=True),
        lax.psum_scatter(grad_up_weight, ("batch", "seq"), scatter_dimension=0, tiled=True),
        lax.psum_scatter(grad_up_bias, ("batch", "seq"), scatter_dimension=0, tiled=True),
        lax.psum_scatter(grad_down_weight, ("batch", "seq"), scatter_dimension=0, tiled=True),
        lax.psum_scatter(grad_down_bias, ("batch", "seq"), scatter_dimension=0, tiled=True),
        lax.psum_scatter(grad_ffn_gain, ("batch", "seq"), scatter_dimension=0, tiled=True),
        lax.psum_scatter(grad_ffn_shift, ("batch", "seq"), scatter_dimension=0, tiled=True),
    )
    return (
        mixed,
        grad_tokens.reshape(tokens.shape),
        summed[0],
        summed[1],
        summed[2],
        summed[3],
        summed[4],
        summed[5],
        summed[6],
        summed[7],
        summed[8],
        summed[9],
        summed[10],
        summed[11],
        summed[12],
        summed[13],
        summed[14],
    )


LOG2E = 1.4426950408889634
GROUP_HEADS = 3
GROUP_COLS = GROUP_HEADS * HEAD_DIM
PACK = 640
VECS = 12
SIDE = 16
KEY_CHUNK = 512


def dot_nt(left_op, right_op):
    return lax.dot_general(
        left_op, right_op, (((1,), (1,)), ((), ())), preferred_element_type=jnp.float32
    )


def dot_nn(left_op, right_op):
    return lax.dot_general(
        left_op, right_op, (((1,), (0,)), ((), ())), preferred_element_type=jnp.float32
    )


def attend_kernel(
    query_ref, own_ref, other_ref, seg_key_ref, seg_query_ref, ctx_ref, lse_ref, value_t
):
    half = own_ref.shape[0]
    rows = query_ref.shape[0]

    @pl.when(pl.program_id(0) == 0)
    def _():
        value_t[:, :half] = own_ref[:, GROUP_COLS : 2 * GROUP_COLS].T
        value_t[:, half:] = other_ref[:, GROUP_COLS : 2 * GROUP_COLS].T

    seg_query = seg_query_ref[...]
    chunks = [
        (ref, start) for ref in (own_ref, other_ref) for start in range(0, half, KEY_CHUNK)
    ]
    for head in range(GROUP_HEADS):
        cols = slice(head * HEAD_DIM, (head + 1) * HEAD_DIM)
        query = query_ref[:, cols]
        scores = []
        top = None
        for number, (ref, start) in enumerate(chunks):
            raw = dot_nt(ref[start : start + KEY_CHUNK, cols], query)
            seg_key = seg_key_ref[number * KEY_CHUNK : (number + 1) * KEY_CHUNK, :]
            seg_key = jnp.concatenate([seg_key] * (rows // 128), axis=1)
            masked = jnp.where(seg_key == seg_query, raw * (SCALE * LOG2E), NEG)
            scores.append(masked)
            peak = jnp.max(masked, axis=0, keepdims=True)
            top = peak if top is None else jnp.maximum(top, peak)
        total = None
        context_t = None
        for number in range(len(chunks)):
            weight = jnp.exp2(scores[number] - top)
            part = jnp.sum(weight, axis=0, keepdims=True)
            piece = dot_nn(
                value_t[cols, number * KEY_CHUNK : (number + 1) * KEY_CHUNK],
                weight.astype(jnp.bfloat16),
            )
            total = part if total is None else total + part
            context_t = piece if context_t is None else context_t + piece
        ctx_ref[:, cols] = (context_t / total).T
        lse_ref[head : head + 1, :] = top + jnp.log2(total)


def attend(query, own, other, seg_key, seg_query):
    rows = query.shape[0]
    half = own.shape[0]
    block = rows // 4
    return pl.pallas_call(
        attend_kernel,
        grid=(4,),
        in_specs=[
            pl.BlockSpec((block, GROUP_COLS), lambda i: (i, 0)),
            pl.BlockSpec((half, 2 * GROUP_COLS), lambda i: (0, 0)),
            pl.BlockSpec((half, 2 * GROUP_COLS), lambda i: (0, 0)),
            pl.BlockSpec((2 * half, 128), lambda i: (0, 0)),
            pl.BlockSpec((1, block), lambda i: (0, i)),
        ],
        out_specs=[
            pl.BlockSpec((block, GROUP_COLS), lambda i: (i, 0)),
            pl.BlockSpec((8, block), lambda i: (0, i)),
        ],
        out_shape=[
            jax.ShapeDtypeStruct((rows, GROUP_COLS), jnp.float32),
            jax.ShapeDtypeStruct((8, rows), jnp.float32),
        ],
        scratch_shapes=[pltpu.VMEM((GROUP_COLS, 2 * half), jnp.bfloat16)],
        compiler_params=pltpu.CompilerParams(vmem_limit_bytes=48 * 1024 * 1024),
        cost_estimate=pl.CostEstimate(
            flops=70 * rows * half * GROUP_COLS, bytes_accessed=1024 * 1024, transcendentals=0
        ),
        name="attend",
    )(query, own, other, seg_key, seg_query)


def attend_back_kernel(
    query_ref,
    grad_ref,
    ctx_ref,
    lse_ref,
    own_ref,
    other_ref,
    seg_key_ref,
    seg_query_ref,
    gquery_ref,
    gown_ref,
    gother_ref,
    key_t,
    gother_sum,
):
    half = own_ref.shape[0]
    rows = query_ref.shape[0]
    first = pl.program_id(0) == 0

    @pl.when(first)
    def _():
        key_t[:, :half] = own_ref[:, :GROUP_COLS].T
        key_t[:, half:] = other_ref[:, :GROUP_COLS].T
        gown_ref[...] = jnp.zeros_like(gown_ref)
        gother_sum[...] = jnp.zeros_like(gother_sum)

    seg_query = seg_query_ref[...]
    chunks = [
        (ref, gref, start)
        for ref, gref in ((own_ref, gown_ref), (other_ref, gother_sum))
        for start in range(0, half, KEY_CHUNK)
    ]
    for head in range(GROUP_HEADS):
        cols = slice(head * HEAD_DIM, (head + 1) * HEAD_DIM)
        vcols = slice(GROUP_COLS + head * HEAD_DIM, GROUP_COLS + (head + 1) * HEAD_DIM)
        query = query_ref[:, cols]
        grad = grad_ref[:, cols]
        lse = lse_ref[head : head + 1, :]
        dots = (grad.astype(jnp.float32) * ctx_ref[:, cols]).T
        row_dot = jnp.sum(dots, axis=0, keepdims=True)
        gquery_t = None
        for number, (ref, gref, start) in enumerate(chunks):
            spot = slice(start, start + KEY_CHUNK)
            raw = dot_nt(ref[spot, cols], query)
            seg_key = seg_key_ref[number * KEY_CHUNK : (number + 1) * KEY_CHUNK, :]
            seg_key = jnp.concatenate([seg_key] * (rows // 128), axis=1)
            masked = jnp.where(seg_key == seg_query, raw * (SCALE * LOG2E), NEG)
            probs = jnp.exp2(masked - lse)
            gprobs = dot_nt(ref[spot, vcols], grad)
            gscores = (probs * (gprobs - row_dot)).astype(jnp.bfloat16)
            gref[spot, vcols] += dot_nn(probs.astype(jnp.bfloat16), grad)
            gref[spot, cols] += dot_nn(gscores, query)
            piece = dot_nn(key_t[cols, number * KEY_CHUNK : (number + 1) * KEY_CHUNK], gscores)
            gquery_t = piece if gquery_t is None else gquery_t + piece
        gquery_ref[:, cols] = (SCALE * gquery_t).T.astype(jnp.bfloat16)

    @pl.when(pl.program_id(0) == pl.num_programs(0) - 1)
    def _():
        gother_ref[...] = gother_sum[...].astype(jnp.bfloat16)


def attend_back(query, grad, ctx, lse, own, other, seg_key, seg_query):
    rows = query.shape[0]
    half = own.shape[0]
    block = rows // 4
    return pl.pallas_call(
        attend_back_kernel,
        grid=(4,),
        in_specs=[
            pl.BlockSpec((block, GROUP_COLS), lambda i: (i, 0)),
            pl.BlockSpec((block, GROUP_COLS), lambda i: (i, 0)),
            pl.BlockSpec((block, GROUP_COLS), lambda i: (i, 0)),
            pl.BlockSpec((8, block), lambda i: (0, i)),
            pl.BlockSpec((half, 2 * GROUP_COLS), lambda i: (0, 0)),
            pl.BlockSpec((half, 2 * GROUP_COLS), lambda i: (0, 0)),
            pl.BlockSpec((2 * half, 128), lambda i: (0, 0)),
            pl.BlockSpec((1, block), lambda i: (0, i)),
        ],
        out_specs=[
            pl.BlockSpec((block, GROUP_COLS), lambda i: (i, 0)),
            pl.BlockSpec((half, 2 * GROUP_COLS), lambda i: (0, 0)),
            pl.BlockSpec((half, 2 * GROUP_COLS), lambda i: (0, 0)),
        ],
        out_shape=[
            jax.ShapeDtypeStruct((rows, GROUP_COLS), jnp.bfloat16),
            jax.ShapeDtypeStruct((half, 2 * GROUP_COLS), jnp.float32),
            jax.ShapeDtypeStruct((half, 2 * GROUP_COLS), jnp.bfloat16),
        ],
        scratch_shapes=[
            pltpu.VMEM((GROUP_COLS, 2 * half), jnp.bfloat16),
            pltpu.VMEM((half, 2 * GROUP_COLS), jnp.float32),
        ],
        compiler_params=pltpu.CompilerParams(vmem_limit_bytes=48 * 1024 * 1024),
        cost_estimate=pl.CostEstimate(
            flops=100 * rows * half * GROUP_COLS, bytes_accessed=1024 * 1024, transcendentals=0
        ),
        name="attend_back",
    )(query, grad, ctx, lse, own, other, seg_key, seg_query)


def prepare_kernel(
    tokens_ref,
    lengths_ref,
    key_ref,
    value_ref,
    query_ref,
    qbias_ref,
    vbias_ref,
    obias_ref,
    again_ref,
    ashift_ref,
    dbias_ref,
    fgain_ref,
    fshift_ref,
    ubias_ref,
    output_ref,
    up_ref,
    down_ref,
    first_ref,
    second_ref,
    bulk_ref,
    *piece_refs,
):
    place = lax.axis_index("seq")
    odd = lax.rem(place // 4, 2) == 1
    quad = lax.rem(place, 4)
    first_ref[...] = jnp.where(odd, tokens_ref[1], tokens_ref[0])
    second_ref[...] = jnp.where(odd, tokens_ref[0], tokens_ref[1])
    own_rows, width = key_ref.shape
    ratio = up_ref.shape[1] // width
    bulk_ref[0, :own_rows] = output_ref[...]
    for number in range(ratio):
        bulk_ref[0, (1 + number) * own_rows : (2 + number) * own_rows] = up_ref[
            :, number * width : (number + 1) * width
        ]
    bulk_ref[0, (1 + ratio) * own_rows :] = down_ref[...]
    small = (qbias_ref, vbias_ref, obias_ref, again_ref, ashift_ref, dbias_ref, fgain_ref, fshift_ref)
    rows = [ref[...].astype(jnp.float32) for ref in small]
    wide = ubias_ref[...].astype(jnp.float32)
    rows += [wide[:, n * own_rows : (n + 1) * own_rows] for n in range(VECS - len(small))]
    lengths = lengths_ref[...]
    docs = lengths.shape[1]
    flat = jnp.concatenate(
        [lengths[0:1], lengths[1:2], jnp.zeros((1, own_rows - 2 * docs), jnp.int32)], axis=1
    )
    rows += [(flat >> 6).astype(jnp.float32), (flat & 63).astype(jnp.float32)]
    rows += [jnp.zeros_like(rows[0])] * (SIDE - len(rows))
    side = jnp.concatenate(rows, axis=0).T.astype(jnp.bfloat16)
    cut = 3 * GROUP_COLS
    for flip, piece_ref in enumerate(piece_refs):
        piece_ref[...] = jnp.zeros_like(piece_ref)
        piece_ref[:, cut : cut + SIDE] = side
        target = quad ^ flip
        for number in range(4):

            @pl.when(target == number)
            def _():
                cols = slice(number * GROUP_COLS, (number + 1) * GROUP_COLS)
                for spot, ref in enumerate((key_ref, value_ref, query_ref)):
                    piece_ref[:, spot * GROUP_COLS : (spot + 1) * GROUP_COLS] = ref[:, cols]


def prepare(tokens, lengths, key, value, query, vectors, up_bias, output, up, down):
    own_rows, width = key.shape
    bulk_rows = own_rows + down.shape[0] * 2
    turn_shape = jax.ShapeDtypeStruct(tokens.shape[1:], jnp.bfloat16)
    piece_shape = jax.ShapeDtypeStruct((own_rows, PACK), jnp.bfloat16)
    return pl.pallas_call(
        prepare_kernel,
        out_shape=[turn_shape] * 2
        + [jax.ShapeDtypeStruct((1, bulk_rows, width), jnp.bfloat16)]
        + [piece_shape] * 4,
        name="prepare",
    )(
        tokens,
        lengths,
        key,
        value,
        query,
        *[item.reshape(1, own_rows) for item in vectors],
        up_bias.reshape(1, up_bias.shape[0]),
        output,
        up,
        down,
    )


def tied(values, *others):
    return lax.optimization_barrier((values, others))[0]


def block_of(values, index, axis):
    return lax.dynamic_index_in_dim(values, index, axis=axis, keepdims=False)


def split_blocks(values, place, axis):
    low = values.astype(jnp.bfloat16)
    return [block_of(values, place, axis)] + [
        block_of(low, place ^ flip, axis) for flip in (1, 2, 3)
    ]


def sum_parts(own, arrived):
    total = own.astype(jnp.float32)
    for item in arrived:
        total = total + item.astype(jnp.float32)
    return total


def device_table(mapping):
    pairs = []
    for core in range(2):
        for layer_z in range(4):
            for quad in range(4):
                to_core, to_z, to_quad = mapping(core, layer_z, quad)
                pairs.append((core * 16 + layer_z * 4 + quad, to_core * 16 + to_z * 4 + to_quad))
    return pairs


def hop(value, mapping):
    return lax.ppermute(value, ("batch", "seq"), device_table(mapping))


def hop_quad(value, flip):
    return hop(value, lambda core, layer_z, quad: (core, layer_z, quad ^ flip))


def hop_layer(value, flip):
    return hop(value, lambda core, layer_z, quad: (core, layer_z ^ flip, quad))


def hop_core(value):
    return hop(value, lambda core, layer_z, quad: (1 - core, layer_z, quad))


def to_sequence(value, turn):
    return hop(
        value,
        lambda core, layer_z, quad: (layer_z // 2, 2 * core + (layer_z + turn) % 2, quad),
    )


def to_owner(value, turn):
    return hop(
        value,
        lambda core, layer_z, quad: (layer_z // 2, 2 * core + (layer_z - turn) % 2, quad),
    )


def turned(blocks, quad):
    first, second, third, fourth = blocks
    odd = quad % 2 == 1
    high = quad // 2 == 1
    pairs = (
        jnp.where(odd, second, first),
        jnp.where(odd, first, second),
        jnp.where(odd, fourth, third),
        jnp.where(odd, third, fourth),
    )
    return (
        jnp.where(high, pairs[2], pairs[0]),
        jnp.where(high, pairs[3], pairs[1]),
        jnp.where(high, pairs[0], pairs[2]),
        jnp.where(high, pairs[1], pairs[3]),
    )


def pack_grads(main, vecs):
    coarse = vecs.astype(jnp.bfloat16)
    fine = (vecs - coarse.astype(jnp.float32)).astype(jnp.bfloat16)
    filler = jnp.zeros(main.shape[:-1] + (PACK - main.shape[-1] - 2 * VECS,), jnp.bfloat16)
    return jnp.concatenate([main.astype(jnp.bfloat16), coarse, fine, filler], axis=-1)


def unpack_grads(packed):
    wide = packed.astype(jnp.float32)
    cut = 3 * GROUP_COLS
    return (wide[..., :cut], wide[..., cut : cut + VECS] + wide[..., cut + VECS : cut + 2 * VECS])


def shards_heads(
    tokens,
    doc_lengths,
    query_weight,
    query_bias,
    key_weight,
    value_weight,
    value_bias,
    output_weight,
    output_bias,
    attn_gain,
    attn_shift,
    up_weight,
    up_bias,
    down_weight,
    down_bias,
    ffn_gain,
    ffn_shift,
    cotangent,
):
    groups, stretch, width = tokens.shape
    own_rows = query_weight.shape[0]
    hidden = up_weight.shape[1]
    ratio = hidden // width
    devices = width // own_rows
    bulk_rows = own_rows * (1 + 2 * ratio)
    row_count = groups * stretch
    core = lax.axis_index("batch")
    place = lax.axis_index("seq")
    layer_z = place // 4
    quad = place % 4
    parity = layer_z % 2
    flips = (1, 2, 3)

    vectors = (
        query_bias,
        value_bias,
        output_bias,
        attn_gain,
        attn_shift,
        down_bias,
        ffn_gain,
        ffn_shift,
    )
    first_turn, second_turn, bulk, *pieces = prepare(
        tokens,
        doc_lengths,
        key_weight,
        value_weight,
        query_weight,
        vectors,
        up_bias,
        output_weight,
        up_weight,
        down_weight,
    )

    with jax.named_scope("tokens_out"):
        own_block = jnp.concatenate(
            [to_sequence(first_turn, 0), to_sequence(second_turn, 1)], axis=0
        )
        token_half = jnp.concatenate(
            [own_block] + [hop_quad(own_block, flip) for flip in flips], axis=0
        )

    with jax.named_scope("group_weights"):
        quads = turned([pieces[0]] + [hop_quad(pieces[flip], flip) for flip in flips], quad)
        quads = jnp.stack(quads, axis=0)
        layers = [quads] + [hop_layer(quads, flip) for flip in flips]
        layers = jnp.stack(turned(layers, layer_z), axis=0)
        twin = hop_core(layers)
        cores = jnp.stack([jnp.where(core == 0, layers, twin), jnp.where(core == 0, twin, layers)])
        packed = cores.reshape(width, PACK)
    group_weight = packed[:, : 3 * GROUP_COLS]
    side = packed[:, 3 * GROUP_COLS : 3 * GROUP_COLS + SIDE].astype(jnp.float32)
    vector_rows = side[:, :8].T
    up_bias_full = side[:, 8:VECS].reshape(devices, own_rows, ratio)
    up_bias_full = jnp.swapaxes(up_bias_full, 1, 2).reshape(1, hidden)
    (
        qbias_full,
        vbias_full,
        obias_full,
        again_full,
        ashift_full,
        dbias_full,
        fgain_full,
        fshift_full,
    ) = [vector_rows[number] for number in range(8)]
    docs = doc_lengths.shape[1]
    digits = side.reshape(2, width // 2, SIDE)[:, : groups * docs, VECS : VECS + 2]
    lengths_all = (digits[..., 0] * 64 + digits[..., 1]).astype(jnp.int32)
    lengths = lax.dynamic_index_in_dim(
        lengths_all.reshape(2 * groups, docs), layer_z, axis=0, keepdims=False
    )
    doc_ends = jnp.cumsum(lengths)

    def half_segments(which):
        turn_z = jnp.stack([(layer_z - turn) % 2 for turn in (0, 1)]) + 2 * which
        spot = jnp.stack([quad ^ flip for flip in range(4)])
        start = turn_z[None, :] * (4 * stretch) + spot[:, None] * stretch
        positions = start[:, :, None] + jnp.arange(stretch, dtype=jnp.int32)
        positions = positions.reshape(-1)
        return jnp.sum((positions[:, None] >= doc_ends[None, :]).astype(jnp.int32), axis=-1)

    seg_query = half_segments(core)
    seg_key = jnp.concatenate([seg_query, half_segments(1 - core)])
    seg_key = jnp.broadcast_to(seg_key[:, None], (seg_key.shape[0], 128))
    seg_query = seg_query[None, :]

    bulk_all = lax.all_gather(bulk, ("batch", "seq"), axis=0, tiled=True)

    with jax.named_scope("projections"):
        column_bias = jnp.concatenate(
            [
                jnp.zeros((GROUP_COLS,), jnp.float32),
                lax.dynamic_slice_in_dim(vbias_full, quad * GROUP_COLS, GROUP_COLS),
                lax.dynamic_slice_in_dim(qbias_full, quad * GROUP_COLS, GROUP_COLS),
            ]
        )
        projected = (matmul_plain(token_half, group_weight) + column_bias).astype(jnp.bfloat16)
        own_pair = projected[:, : 2 * GROUP_COLS]
        queries = projected[:, 2 * GROUP_COLS :]
        other_pair = hop_core(own_pair)
    ctx_wide, lse = attend(queries, own_pair, other_pair, seg_key, seg_query)

    with jax.named_scope("context_home"):
        ctx_blocks = ctx_wide.astype(jnp.bfloat16).reshape(4, row_count, GROUP_COLS)
        ctx_groups = [ctx_blocks[0]] + [hop_quad(ctx_blocks[flip], flip) for flip in flips]
        ctx_merged = jnp.concatenate(turned(ctx_groups, quad), axis=1)
        ctx_turns = [
            to_owner(ctx_merged[turn * stretch : (turn + 1) * stretch], turn) for turn in (0, 1)
        ]
        context_low = jnp.concatenate(
            [
                jnp.where(parity == 0, ctx_turns[0], ctx_turns[1]),
                jnp.where(parity == 0, ctx_turns[1], ctx_turns[0]),
            ],
            axis=0,
        )

    output_full = bulk_all[:, :own_rows].reshape(width, width)
    up_parts = [
        bulk_all[:, (1 + number) * own_rows : (2 + number) * own_rows].reshape(width, width)
        for number in range(ratio)
    ]
    up_full = jnp.concatenate(up_parts, axis=1)
    down_full = bulk_all[:, (1 + ratio) * own_rows :].reshape(hidden, width)

    token_rows = tokens.reshape(row_count, width)
    res_one = token_rows.astype(jnp.float32) + matmul_plain(context_low, output_full) + obias_full
    normed, pull_one = jax.vjp(norm_apply, res_one, again_full, ashift_full)
    normed_low = normed.astype(jnp.bfloat16)
    up_pre = matmul_plain(normed_low, up_full) + up_bias_full
    activated, pull_gelu = jax.vjp(gelu_exact, up_pre)
    act_low = activated.astype(jnp.bfloat16)
    res_two = normed + matmul_plain(act_low, down_full) + dbias_full
    output_rows, pull_two = jax.vjp(norm_apply, res_two, fgain_full, fshift_full)
    mixed = output_rows.astype(jnp.bfloat16).reshape(tokens.shape)
    grad_out = cotangent.astype(jnp.float32).reshape(row_count, width)
    grad_res_two, grad_ffn_gain, grad_ffn_shift = pull_two(grad_out)
    grad_down_low = grad_res_two.astype(jnp.bfloat16)

    def half_columns(matrix, which):
        half = matrix.shape[1] // 2
        return lax.dynamic_slice_in_dim(matrix, which * half, half, axis=1)

    def down_term(which):
        return matmul_left_t(half_columns(act_low, which), grad_down_low)

    def branch_term(which):
        return jnp.concatenate(
            [
                matmul_left_t(half_columns(normed_low, which), grad_up_low),
                matmul_left_t(half_columns(context_low, which), grad_branch_low),
            ],
            axis=1,
        )

    with jax.named_scope("down_grads"):
        down_theirs = down_term(1 - core).astype(jnp.bfloat16)
        down_arrived = hop_core(down_theirs)
    (grad_up_pre,) = pull_gelu(matmul_right_t(tied(grad_down_low, down_theirs), down_full))
    grad_up_low = grad_up_pre.astype(jnp.bfloat16)
    grad_normed = grad_res_two + matmul_right_t(grad_up_low, up_full)
    grad_res_one, grad_attn_gain, grad_attn_shift = pull_one(grad_normed)
    grad_branch_low = grad_res_one.astype(jnp.bfloat16)
    grad_context = matmul_right_t(grad_branch_low, output_full).astype(jnp.bfloat16)
    with jax.named_scope("branch_grads"):
        branch_arrived = hop_core(branch_term(1 - core).astype(jnp.bfloat16))

    with jax.named_scope("context_grad_out"):
        low_part = grad_context[:stretch]
        high_part = grad_context[stretch:]
        grad_turns = [
            to_sequence(jnp.where((parity + turn) % 2 == 1, high_part, low_part), turn)
            for turn in (0, 1)
        ]
        grad_own = jnp.concatenate(grad_turns, axis=0)
        grad_columns = turned(
            [grad_own[:, n * GROUP_COLS : (n + 1) * GROUP_COLS] for n in range(4)], quad
        )
        grad_ctx = jnp.concatenate(
            [grad_columns[0]] + [hop_quad(grad_columns[flip], flip) for flip in flips], axis=0
        )

    with jax.named_scope("down_grads"):
        down_total = (down_term(core) + down_arrived.astype(jnp.float32)).astype(jnp.bfloat16)
        down_blocks = down_total.reshape(4, 4, ratio * own_rows, width)
        down_quads = tied(split_blocks(down_blocks, quad, 1), grad_ctx)
    with jax.named_scope("branch_grads"):
        branch_total = (branch_term(core) + branch_arrived.astype(jnp.float32)).astype(jnp.bfloat16)
        branch_blocks = branch_total.reshape(4, 4, own_rows, hidden + width)
        branch_quads = split_blocks(branch_blocks, quad, 1)
    with jax.named_scope("down_grads"):
        down_arrived = [hop_quad(down_quads[flip], flip) for flip in flips]

    grad_query, grad_own_pair, grad_other_pair = attend_back(
        tied(queries, down_quads, branch_quads),
        grad_ctx,
        ctx_wide,
        lse,
        own_pair,
        other_pair,
        seg_key,
        seg_query,
    )
    with jax.named_scope("branch_grads"):
        branch_quads = tied(branch_quads, grad_other_pair)
        branch_arrived = [hop_quad(branch_quads[flip], flip) for flip in flips]
    with jax.named_scope("pair_sum"):
        pair_total = grad_own_pair + hop_core(grad_other_pair).astype(jnp.float32)
        pair_scale = jnp.where(jnp.arange(2 * GROUP_COLS) < GROUP_COLS, SCALE, 1.0)
        grad_projected = jnp.concatenate(
            [(pair_total * pair_scale).astype(jnp.bfloat16), grad_query], axis=1
        )
        grad_projected = tied(grad_projected, down_arrived)
    with jax.named_scope("token_grads"):
        grad_half = matmul_right_t(grad_projected, group_weight)
        half_blocks = grad_half.reshape(4, row_count, width)
        low_blocks = half_blocks.astype(jnp.bfloat16)
    with jax.named_scope("down_grads"):
        down_part = sum_parts(down_quads[0], down_arrived)
        down_layers = split_blocks(down_part, layer_z, 0)
        down_arrived = [hop_layer(down_layers[flip], flip) for flip in flips]
    with jax.named_scope("token_grads"):
        down_arrived = tied(down_arrived, low_blocks)
        low_blocks = tied(low_blocks, branch_arrived, down_arrived)
        token_arrived = [hop_quad(low_blocks[flip], flip) for flip in flips]
    with jax.named_scope("branch_grads"):
        branch_part = sum_parts(branch_quads[0], tied(branch_arrived, low_blocks))
        branch_layers = split_blocks(branch_part, layer_z, 0)
        branch_arrived = [hop_layer(branch_layers[flip], flip) for flip in flips]
    up_sums, out_sums, down_sums, again_sums, ashift_sums, fgain_sums, fshift_sums = tied(
        (
            column_sums(grad_up_low),
            column_sums(grad_branch_low),
            column_sums(grad_down_low),
            grad_attn_gain,
            grad_attn_shift,
            grad_ffn_gain,
            grad_ffn_shift,
        ),
        low_blocks,
    )

    with jax.named_scope("group_weight_grads"):
        grad_group = matmul_left_t(token_half, grad_projected)
        bias_sums = column_sums(grad_projected)
        nothing = jnp.zeros((width,), jnp.float32)
        vec_rows = jnp.stack(
            [
                lax.dynamic_update_slice_in_dim(
                    nothing, bias_sums[2 * GROUP_COLS :], quad * GROUP_COLS, 0
                ),
                lax.dynamic_update_slice_in_dim(
                    nothing, bias_sums[GROUP_COLS : 2 * GROUP_COLS], quad * GROUP_COLS, 0
                ),
                out_sums,
                again_sums,
                ashift_sums,
                down_sums,
                fgain_sums,
                fshift_sums,
            ],
            axis=0,
        ).T
        up_sums = up_sums.reshape(devices, ratio, own_rows)
        up_sums = jnp.swapaxes(up_sums, 1, 2).reshape(width, ratio)
        vecs = jnp.concatenate([vec_rows, up_sums], axis=1)
        packed_grads = pack_grads(grad_group, vecs).reshape(2, width // 2, PACK)
        mine = jnp.where(core == 0, packed_grads[0], packed_grads[1])
        theirs = jnp.where(core == 0, packed_grads[1], packed_grads[0])
        main, vecs = unpack_grads(mine)
        more, more_vecs = unpack_grads(hop_core(theirs))
        main, vecs = (main + more, vecs + more_vecs)
        packed_grads = pack_grads(main, vecs).reshape(4, 4 * own_rows, PACK)
        by_layer = turned([packed_grads[number] for number in range(4)], layer_z)

    with jax.named_scope("token_grads"):
        grad_block = sum_parts(half_blocks[0], token_arrived).astype(jnp.bfloat16)
        branch_arrived = tied(branch_arrived, grad_block)
        grad_block = tied(grad_block, branch_layers, by_layer)
        home = [
            to_owner(grad_block[turn * stretch : (turn + 1) * stretch], turn) for turn in (0, 1)
        ]
        main, vecs = unpack_grads(by_layer[0])
        for flip in flips:
            more, more_vecs = unpack_grads(hop_layer(by_layer[flip], flip))
            main, vecs = (main + more, vecs + more_vecs)
        packed_grads = pack_grads(main, vecs).reshape(4, own_rows, PACK)
        by_quad = turned([packed_grads[number] for number in range(4)], quad)
        main, vecs = unpack_grads(by_quad[0])
        by_quad = tied(by_quad, home, branch_arrived)
        home_rows = jnp.concatenate(
            [
                jnp.where(parity == 0, home[0], home[1]),
                jnp.where(parity == 0, home[1], home[0]),
            ],
            axis=0,
        )
        grad_tokens = (grad_res_one + home_rows.astype(jnp.float32)).reshape(tokens.shape)

    with jax.named_scope("group_weight_grads"):
        quad_parts = [main]
        for flip in flips:
            more, more_vecs = unpack_grads(hop_quad(by_quad[flip], flip))
            quad_parts.append(more)
            vecs = vecs + more_vecs
        quad_parts = turned(quad_parts, quad)
        sum_key, sum_value, sum_query = [
            jnp.concatenate([part[:, n * GROUP_COLS : (n + 1) * GROUP_COLS] for part in quad_parts], axis=1)
            for n in range(3)
        ]
    sum_rows = vecs[:, :8].T
    sum_down = sum_parts(down_layers[0], down_arrived)
    sum_branch = sum_parts(branch_layers[0], branch_arrived)
    sum_up = sum_branch[:, :hidden]
    sum_output = sum_branch[:, hidden:]
    return (
        mixed,
        grad_tokens,
        sum_query,
        sum_rows[0],
        sum_key,
        sum_value,
        sum_rows[1],
        sum_output,
        sum_rows[2],
        sum_rows[3],
        sum_rows[4],
        sum_up,
        vecs[:, 8:].T.reshape(up_bias.shape),
        sum_down,
        sum_rows[5],
        sum_rows[6],
        sum_rows[7],
    )


def solution(mesh):
    in_specs = (
        P("batch", "seq", None),
        P("batch", None),
        P(("batch", "seq"), None),
        P(("batch", "seq")),
        P(("batch", "seq"), None),
        P(("batch", "seq"), None),
        P(("batch", "seq")),
        P(("batch", "seq"), None),
        P(("batch", "seq")),
        P(("batch", "seq")),
        P(("batch", "seq")),
        P(("batch", "seq"), None),
        P(("batch", "seq")),
        P(("batch", "seq"), None),
        P(("batch", "seq")),
        P(("batch", "seq")),
        P(("batch", "seq")),
        P("batch", "seq", None),
    )
    out_specs = (
        P("batch", "seq", None),
        P("batch", "seq", None),
        P(("batch", "seq"), None),
        P(("batch", "seq")),
        P(("batch", "seq"), None),
        P(("batch", "seq"), None),
        P(("batch", "seq")),
        P(("batch", "seq"), None),
        P(("batch", "seq")),
        P(("batch", "seq")),
        P(("batch", "seq")),
        P(("batch", "seq"), None),
        P(("batch", "seq")),
        P(("batch", "seq"), None),
        P(("batch", "seq")),
        P(("batch", "seq")),
        P(("batch", "seq")),
    )
    fits = mesh.shape['batch'] == 2 and mesh.shape['seq'] == 16
    body = shards_heads if fits else shards_general
    return jax.shard_map(body, mesh=mesh, in_specs=in_specs, out_specs=out_specs, check_vma=False)
```

```python
import jax
import jax.numpy as jnp
from jax import lax
from jax.experimental import pallas as pl
from jax.experimental.pallas import tpu as pltpu
from jax.sharding import PartitionSpec as P

BATCH = "batch"
SEQ = "seq"
BOTH = (BATCH, SEQ)
HEADS = 12
HEAD_DIM = 64


SCALE = 0.125
NEG = -1e30
EPS = 1e-12


def norm_apply(hidden, gain_vec, shift_vec):
    center = jnp.mean(hidden, axis=-1, keepdims=True)
    centered = hidden - center
    spread = jnp.mean(centered * centered, axis=-1, keepdims=True)
    return centered * lax.rsqrt(spread + EPS) * gain_vec + shift_vec


def gelu_exact(inputs):
    return jax.nn.gelu(inputs, approximate=False)


def segment_ids(doc_lengths, positions):
    doc_ends = jnp.cumsum(doc_lengths, axis=-1)
    return jnp.sum((positions[None, :, None] >= doc_ends[:, None, :]).astype(jnp.int32), axis=-1)


def matmul_plain(left_op, right_op):
    return jnp.dot(left_op, right_op, preferred_element_type=jnp.float32)


def matmul_right_t(left_op, right_op):
    return lax.dot_general(
        left_op, right_op, (((1,), (1,)), ((), ())), preferred_element_type=jnp.float32
    )


def matmul_left_t(left_op, right_op):
    return lax.dot_general(
        left_op, right_op, (((0,), (0,)), ((), ())), preferred_element_type=jnp.float32
    )


def column_sums(matrix):
    return jnp.sum(matrix.astype(jnp.float32), axis=0)


def head_block(matrix, head_pair):
    pair_width = 2 * HEAD_DIM
    column_block = matrix[..., head_pair * pair_width : (head_pair + 1) * pair_width]
    return column_block.reshape(column_block.shape[:-1] + (2, HEAD_DIM))


def merge_heads(blocks):
    return jnp.concatenate(
        [block_item.reshape(block_item.shape[:2] + (2 * HEAD_DIM,)) for block_item in blocks],
        axis=-1,
    )


def stat_pair(stats, head_pair):
    return stats[:, 2 * head_pair : 2 * head_pair + 2][..., None]


def pair_scores(query_pair, key_pair, same_doc):
    raw_scores = jnp.einsum(
        "sqhd,skhd->shqk", query_pair, key_pair, preferred_element_type=jnp.float32
    )
    return jnp.where(same_doc[:, None], SCALE * raw_scores, NEG)


def attend_forward(queries, key_all, value_all, same_doc):
    outputs, log_sums = ([], [])
    for head_pair in range(HEADS // 2):
        scores = pair_scores(
            head_block(queries, head_pair), head_block(key_all, head_pair), same_doc
        )
        top_score = jnp.max(scores, axis=-1, keepdims=True)
        exponent = jnp.exp(scores - top_score)
        totals = jnp.sum(exponent, axis=-1, keepdims=True)
        probs_low = (exponent / totals).astype(jnp.bfloat16)
        context = jnp.einsum(
            "shqk,skhd->sqhd",
            probs_low,
            head_block(value_all, head_pair),
            preferred_element_type=jnp.float32,
        )
        outputs.append(context)
        log_sums.append((top_score + jnp.log(totals))[..., 0])
    return (merge_heads(outputs), jnp.concatenate(log_sums, axis=1))


def attend_backward(queries, key_all, value_all, same_doc, log_sums, grad_context):
    query_grads, key_grads, value_grads, row_dots = ([], [], [], [])
    for head_pair in range(HEADS // 2):
        query_pair = head_block(queries, head_pair)
        key_pair = head_block(key_all, head_pair)
        grad_pair = head_block(grad_context, head_pair)
        probs = jnp.exp(
            pair_scores(query_pair, key_pair, same_doc) - stat_pair(log_sums, head_pair)
        )
        grad_probs = jnp.einsum(
            "sqhd,skhd->shqk",
            grad_pair,
            head_block(value_all, head_pair),
            preferred_element_type=jnp.float32,
        )
        row_dot = jnp.sum(probs * grad_probs, axis=-1, keepdims=True)
        row_dots.append(row_dot[..., 0])
        grad_scores = (probs * (grad_probs - row_dot)).astype(jnp.bfloat16) * jnp.bfloat16(SCALE)
        query_grads.append(
            jnp.einsum("shqk,skhd->sqhd", grad_scores, key_pair, preferred_element_type=jnp.float32)
        )
    return (merge_heads(query_grads), jnp.concatenate(row_dots, axis=1), None, None)


def key_side_local(query_all, grad_ctx_all, lse_all, rowdot_all, keys_own, values_own, same_doc_t):
    key_grads, value_grads = ([], [])
    for head_pair in range(HEADS // 2):
        query_pair = head_block(query_all, head_pair)
        grad_pair = head_block(grad_ctx_all, head_pair)
        probs = jnp.exp(
            pair_scores(query_pair, head_block(keys_own, head_pair), same_doc_t)
            - stat_pair(lse_all, head_pair)
        )
        grad_probs = jnp.einsum(
            "sqhd,skhd->shqk",
            grad_pair,
            head_block(values_own, head_pair),
            preferred_element_type=jnp.float32,
        )
        grad_scores = (probs * (grad_probs - stat_pair(rowdot_all, head_pair))).astype(
            jnp.bfloat16
        ) * jnp.bfloat16(SCALE)
        key_grads.append(
            jnp.einsum(
                "shqk,sqhd->skhd", grad_scores, query_pair, preferred_element_type=jnp.float32
            )
        )
        value_grads.append(
            jnp.einsum(
                "shqk,sqhd->skhd",
                probs.astype(jnp.bfloat16),
                grad_pair,
                preferred_element_type=jnp.float32,
            )
        )
    return (merge_heads(key_grads), merge_heads(value_grads))


def shards_general(
    tokens,
    doc_lengths,
    query_weight,
    query_bias,
    key_weight,
    value_weight,
    value_bias,
    output_weight,
    output_bias,
    attn_gain,
    attn_shift,
    up_weight,
    up_bias,
    down_weight,
    down_bias,
    ffn_gain,
    ffn_shift,
    cotangent,
):
    gathered = (
        lax.all_gather(query_weight, BOTH, axis=0, tiled=True),
        lax.all_gather(query_bias, BOTH, axis=0, tiled=True),
        lax.all_gather(key_weight, BOTH, axis=0, tiled=True),
        lax.all_gather(value_weight, BOTH, axis=0, tiled=True),
        lax.all_gather(value_bias, BOTH, axis=0, tiled=True),
        lax.all_gather(output_weight, BOTH, axis=0, tiled=True),
        lax.all_gather(output_bias, BOTH, axis=0, tiled=True),
        lax.all_gather(attn_gain, BOTH, axis=0, tiled=True),
        lax.all_gather(attn_shift, BOTH, axis=0, tiled=True),
        lax.all_gather(up_weight, BOTH, axis=0, tiled=True),
        lax.all_gather(up_bias, BOTH, axis=0, tiled=True),
        lax.all_gather(down_weight, BOTH, axis=0, tiled=True),
        lax.all_gather(down_bias, BOTH, axis=0, tiled=True),
        lax.all_gather(ffn_gain, BOTH, axis=0, tiled=True),
        lax.all_gather(ffn_shift, BOTH, axis=0, tiled=True),
    )
    (
        query_full,
        qbias_full,
        key_full,
        value_full,
        vbias_full,
        output_full,
        obias_full,
        again_full,
        ashift_full,
        up_full,
        ubias_full,
        down_full,
        dbias_full,
        fgain_full,
        fshift_full,
    ) = gathered
    seq_groups, stretch_len, width = tokens.shape
    row_count = seq_groups * stretch_len
    token_rows = tokens.reshape(row_count, width)
    positions = lax.axis_index(SEQ) * stretch_len + jnp.arange(stretch_len, dtype=jnp.int32)
    total_len = stretch_len * lax.axis_size(SEQ)
    query_seg = segment_ids(doc_lengths, positions)
    key_seg = segment_ids(doc_lengths, jnp.arange(total_len, dtype=jnp.int32))
    same_doc = query_seg[:, :, None] == key_seg[:, None, :]
    queries = (
        (matmul_plain(token_rows, query_full) + qbias_full)
        .astype(jnp.bfloat16)
        .reshape(tokens.shape)
    )
    keys_local = matmul_plain(token_rows, key_full).astype(jnp.bfloat16).reshape(tokens.shape)
    values_local = (
        (matmul_plain(token_rows, value_full) + vbias_full)
        .astype(jnp.bfloat16)
        .reshape(tokens.shape)
    )
    key_all, value_all = (
        lax.all_gather(keys_local, SEQ, axis=1, tiled=True),
        lax.all_gather(values_local, SEQ, axis=1, tiled=True),
    )
    context, log_sums = attend_forward(queries, key_all, value_all, same_doc)
    context_low = context.reshape(row_count, width).astype(jnp.bfloat16)
    res_one = token_rows.astype(jnp.float32) + matmul_plain(context_low, output_full) + obias_full
    normed, pull_one = jax.vjp(
        norm_apply, res_one, again_full.astype(jnp.float32), ashift_full.astype(jnp.float32)
    )
    normed_low = normed.astype(jnp.bfloat16)
    up_pre = matmul_plain(normed_low, up_full) + ubias_full
    activated, pull_gelu = jax.vjp(gelu_exact, up_pre)
    act_low = activated.astype(jnp.bfloat16)
    res_two = normed + matmul_plain(act_low, down_full) + dbias_full
    output_rows, pull_two = jax.vjp(
        norm_apply, res_two, fgain_full.astype(jnp.float32), fshift_full.astype(jnp.float32)
    )
    mixed = output_rows.astype(jnp.bfloat16).reshape(tokens.shape)
    regathered = (
        lax.all_gather(query_weight, BOTH, axis=0, tiled=True),
        lax.all_gather(query_bias, BOTH, axis=0, tiled=True),
        lax.all_gather(key_weight, BOTH, axis=0, tiled=True),
        lax.all_gather(value_weight, BOTH, axis=0, tiled=True),
        lax.all_gather(value_bias, BOTH, axis=0, tiled=True),
        lax.all_gather(output_weight, BOTH, axis=0, tiled=True),
        lax.all_gather(output_bias, BOTH, axis=0, tiled=True),
        lax.all_gather(attn_gain, BOTH, axis=0, tiled=True),
        lax.all_gather(attn_shift, BOTH, axis=0, tiled=True),
        lax.all_gather(up_weight, BOTH, axis=0, tiled=True),
        lax.all_gather(up_bias, BOTH, axis=0, tiled=True),
        lax.all_gather(down_weight, BOTH, axis=0, tiled=True),
        lax.all_gather(down_bias, BOTH, axis=0, tiled=True),
        lax.all_gather(ffn_gain, BOTH, axis=0, tiled=True),
        lax.all_gather(ffn_shift, BOTH, axis=0, tiled=True),
    )
    query_back = regathered[0]
    key_back = regathered[2]
    value_back = regathered[3]
    output_back = regathered[5]
    up_back = regathered[9]
    down_back = regathered[11]
    grad_out = cotangent.astype(jnp.float32).reshape(row_count, width)
    grad_res_two, grad_ffn_gain, grad_ffn_shift = pull_two(grad_out)
    grad_down_low = grad_res_two.astype(jnp.bfloat16)
    grad_down_weight = matmul_left_t(act_low, grad_down_low)
    grad_down_bias = column_sums(grad_down_low)
    (grad_up_pre,) = pull_gelu(matmul_right_t(grad_down_low, down_back))
    grad_up_low = grad_up_pre.astype(jnp.bfloat16)
    grad_up_weight = matmul_left_t(normed_low, grad_up_low)
    grad_up_bias = column_sums(grad_up_low)
    grad_normed = grad_res_two + matmul_right_t(grad_up_low, up_back)
    grad_res_one, grad_attn_gain, grad_attn_shift = pull_one(grad_normed)
    grad_branch_low = grad_res_one.astype(jnp.bfloat16)
    grad_output_weight = matmul_left_t(context_low, grad_branch_low)
    grad_output_bias = column_sums(grad_branch_low)
    grad_context = (
        matmul_right_t(grad_branch_low, output_back).astype(jnp.bfloat16).reshape(tokens.shape)
    )
    key_again, value_again = (
        lax.all_gather(keys_local, SEQ, axis=1, tiled=True),
        lax.all_gather(values_local, SEQ, axis=1, tiled=True),
    )
    grad_query, row_dots, unused_key, unused_value = attend_backward(
        queries, key_again, value_again, same_doc, log_sums, grad_context
    )
    query_all, grad_ctx_all = (
        lax.all_gather(queries, SEQ, axis=1, tiled=True),
        lax.all_gather(grad_context, SEQ, axis=1, tiled=True),
    )
    lse_all, rowdot_all = (
        lax.all_gather(log_sums, SEQ, axis=2, tiled=True),
        lax.all_gather(row_dots, SEQ, axis=2, tiled=True),
    )
    same_doc_t = key_seg[:, :, None] == query_seg[:, None, :]
    grad_key, grad_value = key_side_local(
        query_all, grad_ctx_all, lse_all, rowdot_all, keys_local, values_local, same_doc_t
    )
    grad_query_low = grad_query.reshape(row_count, width).astype(jnp.bfloat16)
    grad_key_low = grad_key.reshape(row_count, width).astype(jnp.bfloat16)
    grad_value_low = grad_value.reshape(row_count, width).astype(jnp.bfloat16)
    grad_query_weight = matmul_left_t(token_rows, grad_query_low)
    grad_query_bias = column_sums(grad_query_low)
    grad_key_weight = matmul_left_t(token_rows, grad_key_low)
    grad_value_weight = matmul_left_t(token_rows, grad_value_low)
    grad_value_bias = column_sums(grad_value_low)
    grad_tokens = (
        grad_res_one
        + matmul_right_t(grad_query_low, query_back)
        + matmul_right_t(grad_key_low, key_back)
        + matmul_right_t(grad_value_low, value_back)
    )
    summed = (
        lax.psum_scatter(grad_query_weight, BOTH, scatter_dimension=0, tiled=True),
        lax.psum_scatter(grad_query_bias, BOTH, scatter_dimension=0, tiled=True),
        lax.psum_scatter(grad_key_weight, BOTH, scatter_dimension=0, tiled=True),
        lax.psum_scatter(grad_value_weight, BOTH, scatter_dimension=0, tiled=True),
        lax.psum_scatter(grad_value_bias, BOTH, scatter_dimension=0, tiled=True),
        lax.psum_scatter(grad_output_weight, BOTH, scatter_dimension=0, tiled=True),
        lax.psum_scatter(grad_output_bias, BOTH, scatter_dimension=0, tiled=True),
        lax.psum_scatter(grad_attn_gain, BOTH, scatter_dimension=0, tiled=True),
        lax.psum_scatter(grad_attn_shift, BOTH, scatter_dimension=0, tiled=True),
        lax.psum_scatter(grad_up_weight, BOTH, scatter_dimension=0, tiled=True),
        lax.psum_scatter(grad_up_bias, BOTH, scatter_dimension=0, tiled=True),
        lax.psum_scatter(grad_down_weight, BOTH, scatter_dimension=0, tiled=True),
        lax.psum_scatter(grad_down_bias, BOTH, scatter_dimension=0, tiled=True),
        lax.psum_scatter(grad_ffn_gain, BOTH, scatter_dimension=0, tiled=True),
        lax.psum_scatter(grad_ffn_shift, BOTH, scatter_dimension=0, tiled=True),
    )
    return (
        mixed,
        grad_tokens.reshape(tokens.shape),
        summed[0],
        summed[1],
        summed[2],
        summed[3],
        summed[4],
        summed[5],
        summed[6],
        summed[7],
        summed[8],
        summed[9],
        summed[10],
        summed[11],
        summed[12],
        summed[13],
        summed[14],
    )


LOG2E = 1.4426950408889634
GROUP_HEADS = 3
GROUP_COLS = GROUP_HEADS * HEAD_DIM
PACK = 640
VECS = 12
SIDE = 16
KEY_CHUNK = 512


def dot_nt(left_op, right_op):
    return lax.dot_general(
        left_op, right_op, (((1,), (1,)), ((), ())), preferred_element_type=jnp.float32
    )


def dot_nn(left_op, right_op):
    return lax.dot_general(
        left_op, right_op, (((1,), (0,)), ((), ())), preferred_element_type=jnp.float32
    )


def attend_kernel(
    query_ref, own_ref, other_ref, seg_key_ref, seg_query_ref, ctx_ref, lse_ref, value_t
):
    half = own_ref.shape[0]
    rows = query_ref.shape[0]

    @pl.when(pl.program_id(0) == 0)
    def _():
        value_t[:, :half] = own_ref[:, GROUP_COLS : 2 * GROUP_COLS].T
        value_t[:, half:] = other_ref[:, GROUP_COLS : 2 * GROUP_COLS].T

    seg_query = seg_query_ref[...]
    chunks = [
        (ref, start) for ref in (own_ref, other_ref) for start in range(0, half, KEY_CHUNK)
    ]
    for head in range(GROUP_HEADS):
        cols = slice(head * HEAD_DIM, (head + 1) * HEAD_DIM)
        query = query_ref[:, cols]
        scores = []
        top = None
        for number, (ref, start) in enumerate(chunks):
            raw = dot_nt(ref[start : start + KEY_CHUNK, cols], query)
            seg_key = seg_key_ref[number * KEY_CHUNK : (number + 1) * KEY_CHUNK, :]
            seg_key = jnp.concatenate([seg_key] * (rows // 128), axis=1)
            masked = jnp.where(seg_key == seg_query, raw * (SCALE * LOG2E), NEG)
            scores.append(masked)
            peak = jnp.max(masked, axis=0, keepdims=True)
            top = peak if top is None else jnp.maximum(top, peak)
        total = None
        context_t = None
        for number in range(len(chunks)):
            weight = jnp.exp2(scores[number] - top)
            part = jnp.sum(weight, axis=0, keepdims=True)
            piece = dot_nn(
                value_t[cols, number * KEY_CHUNK : (number + 1) * KEY_CHUNK],
                weight.astype(jnp.bfloat16),
            )
            total = part if total is None else total + part
            context_t = piece if context_t is None else context_t + piece
        ctx_ref[:, cols] = (context_t / total).T
        lse_ref[head : head + 1, :] = top + jnp.log2(total)


def attend(query, own, other, seg_key, seg_query):
    rows = query.shape[0]
    half = own.shape[0]
    block = rows // 4
    return pl.pallas_call(
        attend_kernel,
        grid=(4,),
        in_specs=[
            pl.BlockSpec((block, GROUP_COLS), lambda i: (i, 0)),
            pl.BlockSpec((half, 2 * GROUP_COLS), lambda i: (0, 0)),
            pl.BlockSpec((half, 2 * GROUP_COLS), lambda i: (0, 0)),
            pl.BlockSpec((2 * half, 128), lambda i: (0, 0)),
            pl.BlockSpec((1, block), lambda i: (0, i)),
        ],
        out_specs=[
            pl.BlockSpec((block, GROUP_COLS), lambda i: (i, 0)),
            pl.BlockSpec((8, block), lambda i: (0, i)),
        ],
        out_shape=[
            jax.ShapeDtypeStruct((rows, GROUP_COLS), jnp.float32),
            jax.ShapeDtypeStruct((8, rows), jnp.float32),
        ],
        scratch_shapes=[pltpu.VMEM((GROUP_COLS, 2 * half), jnp.bfloat16)],
        compiler_params=pltpu.CompilerParams(vmem_limit_bytes=48 * 1024 * 1024),
        cost_estimate=pl.CostEstimate(
            flops=70 * rows * half * GROUP_COLS, bytes_accessed=1024 * 1024, transcendentals=0
        ),
        name="attend",
    )(query, own, other, seg_key, seg_query)


def attend_back_kernel(
    query_ref,
    grad_ref,
    ctx_ref,
    lse_ref,
    own_ref,
    other_ref,
    seg_key_ref,
    seg_query_ref,
    gquery_ref,
    gown_ref,
    gother_ref,
    key_t,
    gother_sum,
):
    half = own_ref.shape[0]
    rows = query_ref.shape[0]
    first = pl.program_id(0) == 0

    @pl.when(first)
    def _():
        key_t[:, :half] = own_ref[:, :GROUP_COLS].T
        key_t[:, half:] = other_ref[:, :GROUP_COLS].T
        gown_ref[...] = jnp.zeros_like(gown_ref)
        gother_sum[...] = jnp.zeros_like(gother_sum)

    seg_query = seg_query_ref[...]
    chunks = [
        (ref, gref, start)
        for ref, gref in ((own_ref, gown_ref), (other_ref, gother_sum))
        for start in range(0, half, KEY_CHUNK)
    ]
    for head in range(GROUP_HEADS):
        cols = slice(head * HEAD_DIM, (head + 1) * HEAD_DIM)
        vcols = slice(GROUP_COLS + head * HEAD_DIM, GROUP_COLS + (head + 1) * HEAD_DIM)
        query = query_ref[:, cols]
        grad = grad_ref[:, cols]
        lse = lse_ref[head : head + 1, :]
        dots = (grad.astype(jnp.float32) * ctx_ref[:, cols]).T
        row_dot = jnp.sum(dots, axis=0, keepdims=True)
        gquery_t = None
        for number, (ref, gref, start) in enumerate(chunks):
            spot = slice(start, start + KEY_CHUNK)
            raw = dot_nt(ref[spot, cols], query)
            seg_key = seg_key_ref[number * KEY_CHUNK : (number + 1) * KEY_CHUNK, :]
            seg_key = jnp.concatenate([seg_key] * (rows // 128), axis=1)
            masked = jnp.where(seg_key == seg_query, raw * (SCALE * LOG2E), NEG)
            probs = jnp.exp2(masked - lse)
            gprobs = dot_nt(ref[spot, vcols], grad)
            gscores = (probs * (gprobs - row_dot)).astype(jnp.bfloat16)
            gref[spot, vcols] += dot_nn(probs.astype(jnp.bfloat16), grad)
            gref[spot, cols] += dot_nn(gscores, query)
            piece = dot_nn(key_t[cols, number * KEY_CHUNK : (number + 1) * KEY_CHUNK], gscores)
            gquery_t = piece if gquery_t is None else gquery_t + piece
        gquery_ref[:, cols] = (SCALE * gquery_t).T.astype(jnp.bfloat16)

    @pl.when(pl.program_id(0) == pl.num_programs(0) - 1)
    def _():
        gother_ref[...] = gother_sum[...].astype(jnp.bfloat16)


def attend_back(query, grad, ctx, lse, own, other, seg_key, seg_query):
    rows = query.shape[0]
    half = own.shape[0]
    block = rows // 4
    return pl.pallas_call(
        attend_back_kernel,
        grid=(4,),
        in_specs=[
            pl.BlockSpec((block, GROUP_COLS), lambda i: (i, 0)),
            pl.BlockSpec((block, GROUP_COLS), lambda i: (i, 0)),
            pl.BlockSpec((block, GROUP_COLS), lambda i: (i, 0)),
            pl.BlockSpec((8, block), lambda i: (0, i)),
            pl.BlockSpec((half, 2 * GROUP_COLS), lambda i: (0, 0)),
            pl.BlockSpec((half, 2 * GROUP_COLS), lambda i: (0, 0)),
            pl.BlockSpec((2 * half, 128), lambda i: (0, 0)),
            pl.BlockSpec((1, block), lambda i: (0, i)),
        ],
        out_specs=[
            pl.BlockSpec((block, GROUP_COLS), lambda i: (i, 0)),
            pl.BlockSpec((half, 2 * GROUP_COLS), lambda i: (0, 0)),
            pl.BlockSpec((half, 2 * GROUP_COLS), lambda i: (0, 0)),
        ],
        out_shape=[
            jax.ShapeDtypeStruct((rows, GROUP_COLS), jnp.bfloat16),
            jax.ShapeDtypeStruct((half, 2 * GROUP_COLS), jnp.float32),
            jax.ShapeDtypeStruct((half, 2 * GROUP_COLS), jnp.bfloat16),
        ],
        scratch_shapes=[
            pltpu.VMEM((GROUP_COLS, 2 * half), jnp.bfloat16),
            pltpu.VMEM((half, 2 * GROUP_COLS), jnp.float32),
        ],
        compiler_params=pltpu.CompilerParams(vmem_limit_bytes=48 * 1024 * 1024),
        cost_estimate=pl.CostEstimate(
            flops=100 * rows * half * GROUP_COLS, bytes_accessed=1024 * 1024, transcendentals=0
        ),
        name="attend_back",
    )(query, grad, ctx, lse, own, other, seg_key, seg_query)


def prepare_kernel(
    tokens_ref,
    lengths_ref,
    key_ref,
    value_ref,
    query_ref,
    qbias_ref,
    vbias_ref,
    obias_ref,
    again_ref,
    ashift_ref,
    dbias_ref,
    fgain_ref,
    fshift_ref,
    ubias_ref,
    output_ref,
    up_ref,
    down_ref,
    first_ref,
    second_ref,
    bulk_ref,
    *piece_refs,
):
    place = lax.axis_index(SEQ)
    odd = lax.rem(place // 4, 2) == 1
    quad = lax.rem(place, 4)
    first_ref[...] = jnp.where(odd, tokens_ref[1], tokens_ref[0])
    second_ref[...] = jnp.where(odd, tokens_ref[0], tokens_ref[1])
    own_rows, width = key_ref.shape
    ratio = up_ref.shape[1] // width
    bulk_ref[0, :own_rows] = output_ref[...]
    for number in range(ratio):
        bulk_ref[0, (1 + number) * own_rows : (2 + number) * own_rows] = up_ref[
            :, number * width : (number + 1) * width
        ]
    bulk_ref[0, (1 + ratio) * own_rows :] = down_ref[...]
    small = (qbias_ref, vbias_ref, obias_ref, again_ref, ashift_ref, dbias_ref, fgain_ref, fshift_ref)
    rows = [ref[...].astype(jnp.float32) for ref in small]
    wide = ubias_ref[...].astype(jnp.float32)
    rows += [wide[:, n * own_rows : (n + 1) * own_rows] for n in range(VECS - len(small))]
    lengths = lengths_ref[...]
    docs = lengths.shape[1]
    flat = jnp.concatenate(
        [lengths[0:1], lengths[1:2], jnp.zeros((1, own_rows - 2 * docs), jnp.int32)], axis=1
    )
    rows += [(flat >> 6).astype(jnp.float32), (flat & 63).astype(jnp.float32)]
    rows += [jnp.zeros_like(rows[0])] * (SIDE - len(rows))
    side = jnp.concatenate(rows, axis=0).T.astype(jnp.bfloat16)
    cut = 3 * GROUP_COLS
    for flip, piece_ref in enumerate(piece_refs):
        piece_ref[...] = jnp.zeros_like(piece_ref)
        piece_ref[:, cut : cut + SIDE] = side
        target = quad ^ flip
        for number in range(4):

            @pl.when(target == number)
            def _():
                cols = slice(number * GROUP_COLS, (number + 1) * GROUP_COLS)
                for spot, ref in enumerate((key_ref, value_ref, query_ref)):
                    piece_ref[:, spot * GROUP_COLS : (spot + 1) * GROUP_COLS] = ref[:, cols]


def prepare(tokens, lengths, key, value, query, vectors, up_bias, output, up, down):
    own_rows, width = key.shape
    bulk_rows = own_rows + down.shape[0] * 2
    turn_shape = jax.ShapeDtypeStruct(tokens.shape[1:], jnp.bfloat16)
    piece_shape = jax.ShapeDtypeStruct((own_rows, PACK), jnp.bfloat16)
    return pl.pallas_call(
        prepare_kernel,
        out_shape=[turn_shape] * 2
        + [jax.ShapeDtypeStruct((1, bulk_rows, width), jnp.bfloat16)]
        + [piece_shape] * 4,
        name="prepare",
    )(
        tokens,
        lengths,
        key,
        value,
        query,
        *[item.reshape(1, own_rows) for item in vectors],
        up_bias.reshape(1, up_bias.shape[0]),
        output,
        up,
        down,
    )


def tied(values, *others):
    return lax.optimization_barrier((values, others))[0]


def block_of(values, index, axis):
    return lax.dynamic_index_in_dim(values, index, axis=axis, keepdims=False)


def halves(values, bit, axis):
    return (block_of(values, bit, axis), block_of(values, 1 - bit, axis))


def low_sum(own, arrived):
    return (own.astype(jnp.float32) + arrived.astype(jnp.float32)).astype(jnp.bfloat16)


def sum_parts(own, arrived):
    total = own.astype(jnp.float32)
    for item in arrived:
        total = total + item.astype(jnp.float32)
    return total


def device_table(mapping):
    pairs = []
    for core in range(2):
        for layer_z in range(4):
            for quad in range(4):
                to_core, to_z, to_quad = mapping(core, layer_z, quad)
                pairs.append((core * 16 + layer_z * 4 + quad, to_core * 16 + to_z * 4 + to_quad))
    return pairs


def hop(value, mapping):
    return lax.ppermute(value, BOTH, device_table(mapping))


def hop_quad(value, flip):
    return hop(value, lambda core, layer_z, quad: (core, layer_z, quad ^ flip))


def hop_layer(value, flip):
    return hop(value, lambda core, layer_z, quad: (core, layer_z ^ flip, quad))


def hop_core(value):
    return hop(value, lambda core, layer_z, quad: (1 - core, layer_z, quad))


def to_sequence(value, turn):
    return hop(
        value,
        lambda core, layer_z, quad: (layer_z // 2, 2 * core + (layer_z + turn) % 2, quad),
    )


def to_owner(value, turn):
    return hop(
        value,
        lambda core, layer_z, quad: (layer_z // 2, 2 * core + (layer_z - turn) % 2, quad),
    )


def turned(blocks, quad):
    first, second, third, fourth = blocks
    odd = quad % 2 == 1
    high = quad // 2 == 1
    pairs = (
        jnp.where(odd, second, first),
        jnp.where(odd, first, second),
        jnp.where(odd, fourth, third),
        jnp.where(odd, third, fourth),
    )
    return (
        jnp.where(high, pairs[2], pairs[0]),
        jnp.where(high, pairs[3], pairs[1]),
        jnp.where(high, pairs[0], pairs[2]),
        jnp.where(high, pairs[1], pairs[3]),
    )


def pack_grads(main, vecs):
    coarse = vecs.astype(jnp.bfloat16)
    fine = (vecs - coarse.astype(jnp.float32)).astype(jnp.bfloat16)
    filler = jnp.zeros(main.shape[:-1] + (PACK - main.shape[-1] - 2 * VECS,), jnp.bfloat16)
    return jnp.concatenate([main.astype(jnp.bfloat16), coarse, fine, filler], axis=-1)


def unpack_grads(packed):
    wide = packed.astype(jnp.float32)
    cut = 3 * GROUP_COLS
    return (wide[..., :cut], wide[..., cut : cut + VECS] + wide[..., cut + VECS : cut + 2 * VECS])


def add_packed(own, arrived):
    main, vecs = unpack_grads(own)
    more, more_vecs = unpack_grads(arrived)
    return (main + more, vecs + more_vecs)


def shards_heads(
    tokens,
    doc_lengths,
    query_weight,
    query_bias,
    key_weight,
    value_weight,
    value_bias,
    output_weight,
    output_bias,
    attn_gain,
    attn_shift,
    up_weight,
    up_bias,
    down_weight,
    down_bias,
    ffn_gain,
    ffn_shift,
    cotangent,
):
    groups, stretch, width = tokens.shape
    own_rows = query_weight.shape[0]
    hidden = up_weight.shape[1]
    ratio = hidden // width
    devices = width // own_rows
    bulk_rows = own_rows * (1 + 2 * ratio)
    row_count = groups * stretch
    core = lax.axis_index(BATCH)
    place = lax.axis_index(SEQ)
    layer_z = place // 4
    quad = place % 4
    parity = layer_z % 2
    flips = (1, 2, 3)
    bit_x, bit_y = (quad % 2, quad // 2)
    bit_low, bit_high = (layer_z % 2, layer_z // 2)

    vectors = (
        query_bias,
        value_bias,
        output_bias,
        attn_gain,
        attn_shift,
        down_bias,
        ffn_gain,
        ffn_shift,
    )
    first_turn, second_turn, bulk, *pieces = prepare(
        tokens,
        doc_lengths,
        key_weight,
        value_weight,
        query_weight,
        vectors,
        up_bias,
        output_weight,
        up_weight,
        down_weight,
    )

    own_block = jnp.concatenate(
        [to_sequence(first_turn, 0), to_sequence(second_turn, 1)], axis=0
    )
    token_half = jnp.concatenate(
        [own_block] + [hop_quad(own_block, flip) for flip in flips], axis=0
    )

    quads = turned([pieces[0]] + [hop_quad(pieces[flip], flip) for flip in flips], quad)
    quads = jnp.stack(quads, axis=0)
    layers = [quads] + [hop_layer(quads, flip) for flip in flips]
    layers = jnp.stack(turned(layers, layer_z), axis=0)
    twin = hop_core(layers)
    cores = jnp.stack([jnp.where(core == 0, layers, twin), jnp.where(core == 0, twin, layers)])
    packed = cores.reshape(width, PACK)
    group_weight = packed[:, : 3 * GROUP_COLS]
    side = packed[:, 3 * GROUP_COLS : 3 * GROUP_COLS + SIDE].astype(jnp.float32)
    vector_rows = side[:, :8].T
    up_bias_full = side[:, 8:VECS].reshape(devices, own_rows, ratio)
    up_bias_full = jnp.swapaxes(up_bias_full, 1, 2).reshape(1, hidden)
    (
        qbias_full,
        vbias_full,
        obias_full,
        again_full,
        ashift_full,
        dbias_full,
        fgain_full,
        fshift_full,
    ) = [vector_rows[number] for number in range(8)]
    docs = doc_lengths.shape[1]
    digits = side.reshape(2, width // 2, SIDE)[:, : groups * docs, VECS : VECS + 2]
    lengths_all = (digits[..., 0] * 64 + digits[..., 1]).astype(jnp.int32)
    lengths = lax.dynamic_index_in_dim(
        lengths_all.reshape(2 * groups, docs), layer_z, axis=0, keepdims=False
    )
    doc_ends = jnp.cumsum(lengths)

    def half_segments(which):
        turn_z = jnp.stack([(layer_z - turn) % 2 for turn in (0, 1)]) + 2 * which
        spot = jnp.stack([quad ^ flip for flip in range(4)])
        start = turn_z[None, :] * (4 * stretch) + spot[:, None] * stretch
        positions = start[:, :, None] + jnp.arange(stretch, dtype=jnp.int32)
        positions = positions.reshape(-1)
        return jnp.sum((positions[:, None] >= doc_ends[None, :]).astype(jnp.int32), axis=-1)

    seg_query = half_segments(core)
    seg_key = jnp.concatenate([seg_query, half_segments(1 - core)])
    seg_key = jnp.broadcast_to(seg_key[:, None], (seg_key.shape[0], 128))
    seg_query = seg_query[None, :]

    bulk_all = lax.all_gather(bulk, BOTH, axis=0, tiled=True)

    column_bias = jnp.concatenate(
        [
            jnp.zeros((GROUP_COLS,), jnp.float32),
            lax.dynamic_slice_in_dim(vbias_full, quad * GROUP_COLS, GROUP_COLS),
            lax.dynamic_slice_in_dim(qbias_full, quad * GROUP_COLS, GROUP_COLS),
        ]
    )
    projected = (matmul_plain(token_half, group_weight) + column_bias).astype(jnp.bfloat16)
    own_pair = projected[:, : 2 * GROUP_COLS]
    queries = projected[:, 2 * GROUP_COLS :]
    other_pair = hop_core(own_pair)
    ctx_wide, lse = attend(queries, own_pair, other_pair, seg_key, seg_query)

    ctx_blocks = ctx_wide.astype(jnp.bfloat16).reshape(4, row_count, GROUP_COLS)
    ctx_groups = [ctx_blocks[0]] + [hop_quad(ctx_blocks[flip], flip) for flip in flips]
    ctx_merged = jnp.concatenate(turned(ctx_groups, quad), axis=1)
    ctx_turns = [
        to_owner(ctx_merged[turn * stretch : (turn + 1) * stretch], turn) for turn in (0, 1)
    ]
    context_low = jnp.concatenate(
        [
            jnp.where(parity == 0, ctx_turns[0], ctx_turns[1]),
            jnp.where(parity == 0, ctx_turns[1], ctx_turns[0]),
        ],
        axis=0,
    )

    output_full = bulk_all[:, :own_rows].reshape(width, width)
    up_parts = [
        bulk_all[:, (1 + number) * own_rows : (2 + number) * own_rows].reshape(width, width)
        for number in range(ratio)
    ]
    up_full = jnp.concatenate(up_parts, axis=1)
    down_full = bulk_all[:, (1 + ratio) * own_rows :].reshape(hidden, width)

    token_rows = tokens.reshape(row_count, width)
    res_one = token_rows.astype(jnp.float32) + matmul_plain(context_low, output_full) + obias_full
    normed, pull_one = jax.vjp(norm_apply, res_one, again_full, ashift_full)
    normed_low = normed.astype(jnp.bfloat16)
    up_pre = matmul_plain(normed_low, up_full) + up_bias_full
    activated, pull_gelu = jax.vjp(gelu_exact, up_pre)
    act_low = activated.astype(jnp.bfloat16)
    res_two = normed + matmul_plain(act_low, down_full) + dbias_full
    output_rows, pull_two = jax.vjp(norm_apply, res_two, fgain_full, fshift_full)
    mixed = output_rows.astype(jnp.bfloat16).reshape(tokens.shape)
    grad_out = cotangent.astype(jnp.float32).reshape(row_count, width)
    grad_res_two, grad_ffn_gain, grad_ffn_shift = pull_two(grad_out)
    grad_down_low = grad_res_two.astype(jnp.bfloat16)

    def half_columns(matrix, which):
        half = matrix.shape[1] // 2
        return lax.dynamic_slice_in_dim(matrix, which * half, half, axis=1)

    def down_term(which):
        return matmul_left_t(half_columns(act_low, which), grad_down_low)

    def branch_term(which):
        return jnp.concatenate(
            [
                matmul_left_t(half_columns(normed_low, which), grad_up_low),
                matmul_left_t(half_columns(context_low, which), grad_branch_low),
            ],
            axis=1,
        )

    down_theirs = down_term(1 - core).astype(jnp.bfloat16)
    down_arrived = hop_core(down_theirs)
    (grad_up_pre,) = pull_gelu(matmul_right_t(tied(grad_down_low, down_theirs), down_full))
    grad_up_low = grad_up_pre.astype(jnp.bfloat16)
    grad_normed = grad_res_two + matmul_right_t(grad_up_low, up_full)
    grad_res_one, grad_attn_gain, grad_attn_shift = pull_one(grad_normed)
    grad_branch_low = grad_res_one.astype(jnp.bfloat16)
    grad_context = matmul_right_t(grad_branch_low, output_full).astype(jnp.bfloat16)
    branch_arrived = hop_core(branch_term(1 - core).astype(jnp.bfloat16))

    low_part = grad_context[:stretch]
    high_part = grad_context[stretch:]
    grad_turns = [
        to_sequence(jnp.where((parity + turn) % 2 == 1, high_part, low_part), turn)
        for turn in (0, 1)
    ]
    grad_own = jnp.concatenate(grad_turns, axis=0)
    grad_columns = turned(
        [grad_own[:, n * GROUP_COLS : (n + 1) * GROUP_COLS] for n in range(4)], quad
    )
    grad_ctx = jnp.concatenate(
        [grad_columns[0]] + [hop_quad(grad_columns[flip], flip) for flip in flips], axis=0
    )

    down_total = (down_term(core) + down_arrived.astype(jnp.float32)).astype(jnp.bfloat16)
    down_total = down_total.reshape(2, 2, 2, 2, ratio * own_rows, width)
    branch_total = (branch_term(core) + branch_arrived.astype(jnp.float32)).astype(jnp.bfloat16)
    branch_total = branch_total.reshape(2, 2, 2, 2, own_rows, hidden + width)
    down_own, down_send = tied(halves(down_total, bit_x, 3), grad_ctx)
    branch_own, branch_send = tied(halves(branch_total, bit_y, 2), grad_ctx)
    down_arrived = hop_quad(down_send, 1)
    branch_arrived = hop_quad(branch_send, 2)

    grad_query, grad_own_pair, grad_other_pair = attend_back(
        tied(queries, down_send, branch_send),
        grad_ctx,
        ctx_wide,
        lse,
        own_pair,
        other_pair,
        seg_key,
        seg_query,
    )
    pair_arrived = hop_core(grad_other_pair)
    down_arrived, branch_arrived = tied((down_arrived, branch_arrived), grad_other_pair)
    down_own, down_send = halves(low_sum(down_own, down_arrived), bit_y, 2)
    branch_own, branch_send = halves(low_sum(branch_own, branch_arrived), bit_x, 2)
    down_arrived = hop_quad(down_send, 2)
    branch_arrived = hop_quad(branch_send, 1)
    pair_total = grad_own_pair + tied(pair_arrived, down_send, branch_send).astype(jnp.float32)
    pair_scale = jnp.where(jnp.arange(2 * GROUP_COLS) < GROUP_COLS, SCALE, 1.0)
    grad_projected = jnp.concatenate(
        [(pair_total * pair_scale).astype(jnp.bfloat16), grad_query], axis=1
    )
    grad_half = matmul_right_t(grad_projected, group_weight)
    half_blocks = grad_half.reshape(4, row_count, width)
    low_blocks = half_blocks.astype(jnp.bfloat16)
    low_blocks, down_arrived, branch_arrived = tied((low_blocks, down_arrived, branch_arrived))
    token_arrived = [hop_quad(low_blocks[flip], flip) for flip in flips]
    down_own, down_send = halves(low_sum(down_own, down_arrived), bit_high, 0)
    branch_own, branch_send = halves(low_sum(branch_own, branch_arrived), bit_high, 0)
    down_arrived = hop_layer(down_send, 2)
    up_sums, out_sums, down_sums, again_sums, ashift_sums, fgain_sums, fshift_sums = tied(
        (
            column_sums(grad_up_low),
            column_sums(grad_branch_low),
            column_sums(grad_down_low),
            grad_attn_gain,
            grad_attn_shift,
            grad_ffn_gain,
            grad_ffn_shift,
        ),
        low_blocks,
    )

    grad_group = matmul_left_t(token_half, grad_projected)
    bias_sums = column_sums(grad_projected)
    nothing = jnp.zeros((width,), jnp.float32)
    vec_rows = jnp.stack(
        [
            lax.dynamic_update_slice_in_dim(
                nothing, bias_sums[2 * GROUP_COLS :], quad * GROUP_COLS, 0
            ),
            lax.dynamic_update_slice_in_dim(
                nothing, bias_sums[GROUP_COLS : 2 * GROUP_COLS], quad * GROUP_COLS, 0
            ),
            out_sums,
            again_sums,
            ashift_sums,
            down_sums,
            fgain_sums,
            fshift_sums,
        ],
        axis=0,
    ).T
    up_sums = up_sums.reshape(devices, ratio, own_rows)
    up_sums = jnp.swapaxes(up_sums, 1, 2).reshape(width, ratio)
    vecs = jnp.concatenate([vec_rows, up_sums], axis=1)
    packed_grads = pack_grads(grad_group, vecs).reshape(2, width // 2, PACK)
    mine = jnp.where(core == 0, packed_grads[0], packed_grads[1])
    theirs = jnp.where(core == 0, packed_grads[1], packed_grads[0])
    packed_grads = pack_grads(*add_packed(mine, hop_core(theirs)))
    packed_grads = packed_grads.reshape(2, 2, 4 * own_rows, PACK)
    pack_own, pack_send = halves(packed_grads, bit_high, 0)
    pack_arrived = hop_layer(pack_send, 2)

    token_arrived = tied(token_arrived, down_send, branch_send)
    grad_block = sum_parts(half_blocks[0], token_arrived).astype(jnp.bfloat16)
    grad_block = tied(grad_block, pack_send, down_arrived)
    home = [
        to_owner(grad_block[turn * stretch : (turn + 1) * stretch], turn) for turn in (0, 1)
    ]
    branch_arrived = hop_layer(tied(branch_send, grad_block), 2)
    down_arrived, pack_arrived = tied((down_arrived, pack_arrived), grad_block)
    packed_grads = pack_grads(*add_packed(pack_own, pack_arrived))
    pack_own, pack_send = halves(packed_grads, bit_low, 0)
    pack_arrived = hop_layer(pack_send, 1)
    down_own, down_send = halves(low_sum(down_own, down_arrived), bit_low, 0)
    down_arrived = hop_layer(down_send, 1)
    home = tied(home, pack_send, down_send)
    branch_arrived, pack_arrived = tied((branch_arrived, pack_arrived), home)
    packed_grads = pack_grads(*add_packed(pack_own, pack_arrived)).reshape(4, own_rows, PACK)
    by_quad = turned([packed_grads[number] for number in range(4)], quad)
    main, vecs = unpack_grads(by_quad[0])
    branch_own, branch_send = halves(low_sum(branch_own, branch_arrived), bit_low, 0)
    branch_arrived = hop_layer(branch_send, 1)
    home_rows = jnp.concatenate(
        [
            jnp.where(parity == 0, home[0], home[1]),
            jnp.where(parity == 0, home[1], home[0]),
        ],
        axis=0,
    )
    grad_tokens = (grad_res_one + home_rows.astype(jnp.float32)).reshape(tokens.shape)

    quad_parts = [main]
    for flip in flips:
        more, more_vecs = unpack_grads(hop_quad(by_quad[flip], flip))
        quad_parts.append(more)
        vecs = vecs + more_vecs
    quad_parts = turned(quad_parts, quad)
    sum_key, sum_value, sum_query = [
        jnp.concatenate(
            [part[:, n * GROUP_COLS : (n + 1) * GROUP_COLS] for part in quad_parts], axis=1
        )
        for n in range(3)
    ]
    sum_rows = vecs[:, :8].T
    sum_down = sum_parts(down_own, [down_arrived])
    sum_branch = sum_parts(branch_own, [branch_arrived])
    sum_up = sum_branch[:, :hidden]
    sum_output = sum_branch[:, hidden:]
    return (
        mixed,
        grad_tokens,
        sum_query,
        sum_rows[0],
        sum_key,
        sum_value,
        sum_rows[1],
        sum_output,
        sum_rows[2],
        sum_rows[3],
        sum_rows[4],
        sum_up,
        vecs[:, 8:].T.reshape(up_bias.shape),
        sum_down,
        sum_rows[5],
        sum_rows[6],
        sum_rows[7],
    )


def solution(mesh):
    in_specs = (
        P(BATCH, SEQ, None),
        P(BATCH, None),
        P(BOTH, None),
        P(BOTH),
        P(BOTH, None),
        P(BOTH, None),
        P(BOTH),
        P(BOTH, None),
        P(BOTH),
        P(BOTH),
        P(BOTH),
        P(BOTH, None),
        P(BOTH),
        P(BOTH, None),
        P(BOTH),
        P(BOTH),
        P(BOTH),
        P(BATCH, SEQ, None),
    )
    out_specs = (
        P(BATCH, SEQ, None),
        P(BATCH, SEQ, None),
        P(BOTH, None),
        P(BOTH),
        P(BOTH, None),
        P(BOTH, None),
        P(BOTH),
        P(BOTH, None),
        P(BOTH),
        P(BOTH),
        P(BOTH),
        P(BOTH, None),
        P(BOTH),
        P(BOTH, None),
        P(BOTH),
        P(BOTH),
        P(BOTH),
    )
    fits = mesh.shape[BATCH] == 2 and mesh.shape[SEQ] == 16
    body = shards_heads if fits else shards_general
    return jax.shard_map(body, mesh=mesh, in_specs=in_specs, out_specs=out_specs, check_vma=False)
```

```python
import jax
import jax.numpy as jnp
from jax import lax
from jax.experimental import pallas as pl
from jax.experimental.pallas import tpu as pltpu
from jax.sharding import PartitionSpec as P

BATCH = "batch"
SEQ = "seq"
BOTH = (BATCH, SEQ)
HEADS = 12
HEAD_DIM = 64


SCALE = 0.125
NEG = -1e30
EPS = 1e-12


def norm_apply(hidden, gain_vec, shift_vec):
    center = jnp.mean(hidden, axis=-1, keepdims=True)
    centered = hidden - center
    spread = jnp.mean(centered * centered, axis=-1, keepdims=True)
    return centered * lax.rsqrt(spread + EPS) * gain_vec + shift_vec


def gelu_exact(inputs):
    return jax.nn.gelu(inputs, approximate=False)


def segment_ids(doc_lengths, positions):
    doc_ends = jnp.cumsum(doc_lengths, axis=-1)
    return jnp.sum((positions[None, :, None] >= doc_ends[:, None, :]).astype(jnp.int32), axis=-1)


def matmul_plain(left_op, right_op):
    return jnp.dot(left_op, right_op, preferred_element_type=jnp.float32)


def matmul_right_t(left_op, right_op):
    return lax.dot_general(
        left_op, right_op, (((1,), (1,)), ((), ())), preferred_element_type=jnp.float32
    )


def matmul_left_t(left_op, right_op):
    return lax.dot_general(
        left_op, right_op, (((0,), (0,)), ((), ())), preferred_element_type=jnp.float32
    )


def column_sums(matrix):
    return jnp.sum(matrix.astype(jnp.float32), axis=0)


def head_block(matrix, head_pair):
    pair_width = 2 * HEAD_DIM
    column_block = matrix[..., head_pair * pair_width : (head_pair + 1) * pair_width]
    return column_block.reshape(column_block.shape[:-1] + (2, HEAD_DIM))


def merge_heads(blocks):
    return jnp.concatenate(
        [block_item.reshape(block_item.shape[:2] + (2 * HEAD_DIM,)) for block_item in blocks],
        axis=-1,
    )


def stat_pair(stats, head_pair):
    return stats[:, 2 * head_pair : 2 * head_pair + 2][..., None]


def pair_scores(query_pair, key_pair, same_doc):
    raw_scores = jnp.einsum(
        "sqhd,skhd->shqk", query_pair, key_pair, preferred_element_type=jnp.float32
    )
    return jnp.where(same_doc[:, None], SCALE * raw_scores, NEG)


def attend_forward(queries, key_all, value_all, same_doc):
    outputs, log_sums = ([], [])
    for head_pair in range(HEADS // 2):
        scores = pair_scores(
            head_block(queries, head_pair), head_block(key_all, head_pair), same_doc
        )
        top_score = jnp.max(scores, axis=-1, keepdims=True)
        exponent = jnp.exp(scores - top_score)
        totals = jnp.sum(exponent, axis=-1, keepdims=True)
        probs_low = (exponent / totals).astype(jnp.bfloat16)
        context = jnp.einsum(
            "shqk,skhd->sqhd",
            probs_low,
            head_block(value_all, head_pair),
            preferred_element_type=jnp.float32,
        )
        outputs.append(context)
        log_sums.append((top_score + jnp.log(totals))[..., 0])
    return (merge_heads(outputs), jnp.concatenate(log_sums, axis=1))


def attend_backward(queries, key_all, value_all, same_doc, log_sums, grad_context):
    query_grads, key_grads, value_grads, row_dots = ([], [], [], [])
    for head_pair in range(HEADS // 2):
        query_pair = head_block(queries, head_pair)
        key_pair = head_block(key_all, head_pair)
        grad_pair = head_block(grad_context, head_pair)
        probs = jnp.exp(
            pair_scores(query_pair, key_pair, same_doc) - stat_pair(log_sums, head_pair)
        )
        grad_probs = jnp.einsum(
            "sqhd,skhd->shqk",
            grad_pair,
            head_block(value_all, head_pair),
            preferred_element_type=jnp.float32,
        )
        row_dot = jnp.sum(probs * grad_probs, axis=-1, keepdims=True)
        row_dots.append(row_dot[..., 0])
        grad_scores = (probs * (grad_probs - row_dot)).astype(jnp.bfloat16) * jnp.bfloat16(SCALE)
        query_grads.append(
            jnp.einsum("shqk,skhd->sqhd", grad_scores, key_pair, preferred_element_type=jnp.float32)
        )
    return (merge_heads(query_grads), jnp.concatenate(row_dots, axis=1), None, None)


def key_side_local(query_all, grad_ctx_all, lse_all, rowdot_all, keys_own, values_own, same_doc_t):
    key_grads, value_grads = ([], [])
    for head_pair in range(HEADS // 2):
        query_pair = head_block(query_all, head_pair)
        grad_pair = head_block(grad_ctx_all, head_pair)
        probs = jnp.exp(
            pair_scores(query_pair, head_block(keys_own, head_pair), same_doc_t)
            - stat_pair(lse_all, head_pair)
        )
        grad_probs = jnp.einsum(
            "sqhd,skhd->shqk",
            grad_pair,
            head_block(values_own, head_pair),
            preferred_element_type=jnp.float32,
        )
        grad_scores = (probs * (grad_probs - stat_pair(rowdot_all, head_pair))).astype(
            jnp.bfloat16
        ) * jnp.bfloat16(SCALE)
        key_grads.append(
            jnp.einsum(
                "shqk,sqhd->skhd", grad_scores, query_pair, preferred_element_type=jnp.float32
            )
        )
        value_grads.append(
            jnp.einsum(
                "shqk,sqhd->skhd",
                probs.astype(jnp.bfloat16),
                grad_pair,
                preferred_element_type=jnp.float32,
            )
        )
    return (merge_heads(key_grads), merge_heads(value_grads))


def shards_general(
    tokens,
    doc_lengths,
    query_weight,
    query_bias,
    key_weight,
    value_weight,
    value_bias,
    output_weight,
    output_bias,
    attn_gain,
    attn_shift,
    up_weight,
    up_bias,
    down_weight,
    down_bias,
    ffn_gain,
    ffn_shift,
    cotangent,
):
    gathered = (
        lax.all_gather(query_weight, BOTH, axis=0, tiled=True),
        lax.all_gather(query_bias, BOTH, axis=0, tiled=True),
        lax.all_gather(key_weight, BOTH, axis=0, tiled=True),
        lax.all_gather(value_weight, BOTH, axis=0, tiled=True),
        lax.all_gather(value_bias, BOTH, axis=0, tiled=True),
        lax.all_gather(output_weight, BOTH, axis=0, tiled=True),
        lax.all_gather(output_bias, BOTH, axis=0, tiled=True),
        lax.all_gather(attn_gain, BOTH, axis=0, tiled=True),
        lax.all_gather(attn_shift, BOTH, axis=0, tiled=True),
        lax.all_gather(up_weight, BOTH, axis=0, tiled=True),
        lax.all_gather(up_bias, BOTH, axis=0, tiled=True),
        lax.all_gather(down_weight, BOTH, axis=0, tiled=True),
        lax.all_gather(down_bias, BOTH, axis=0, tiled=True),
        lax.all_gather(ffn_gain, BOTH, axis=0, tiled=True),
        lax.all_gather(ffn_shift, BOTH, axis=0, tiled=True),
    )
    (
        query_full,
        qbias_full,
        key_full,
        value_full,
        vbias_full,
        output_full,
        obias_full,
        again_full,
        ashift_full,
        up_full,
        ubias_full,
        down_full,
        dbias_full,
        fgain_full,
        fshift_full,
    ) = gathered
    seq_groups, stretch_len, width = tokens.shape
    row_count = seq_groups * stretch_len
    token_rows = tokens.reshape(row_count, width)
    positions = lax.axis_index(SEQ) * stretch_len + jnp.arange(stretch_len, dtype=jnp.int32)
    total_len = stretch_len * lax.axis_size(SEQ)
    query_seg = segment_ids(doc_lengths, positions)
    key_seg = segment_ids(doc_lengths, jnp.arange(total_len, dtype=jnp.int32))
    same_doc = query_seg[:, :, None] == key_seg[:, None, :]
    queries = (
        (matmul_plain(token_rows, query_full) + qbias_full)
        .astype(jnp.bfloat16)
        .reshape(tokens.shape)
    )
    keys_local = matmul_plain(token_rows, key_full).astype(jnp.bfloat16).reshape(tokens.shape)
    values_local = (
        (matmul_plain(token_rows, value_full) + vbias_full)
        .astype(jnp.bfloat16)
        .reshape(tokens.shape)
    )
    key_all, value_all = (
        lax.all_gather(keys_local, SEQ, axis=1, tiled=True),
        lax.all_gather(values_local, SEQ, axis=1, tiled=True),
    )
    context, log_sums = attend_forward(queries, key_all, value_all, same_doc)
    context_low = context.reshape(row_count, width).astype(jnp.bfloat16)
    res_one = token_rows.astype(jnp.float32) + matmul_plain(context_low, output_full) + obias_full
    normed, pull_one = jax.vjp(
        norm_apply, res_one, again_full.astype(jnp.float32), ashift_full.astype(jnp.float32)
    )
    normed_low = normed.astype(jnp.bfloat16)
    up_pre = matmul_plain(normed_low, up_full) + ubias_full
    activated, pull_gelu = jax.vjp(gelu_exact, up_pre)
    act_low = activated.astype(jnp.bfloat16)
    res_two = normed + matmul_plain(act_low, down_full) + dbias_full
    output_rows, pull_two = jax.vjp(
        norm_apply, res_two, fgain_full.astype(jnp.float32), fshift_full.astype(jnp.float32)
    )
    mixed = output_rows.astype(jnp.bfloat16).reshape(tokens.shape)
    regathered = (
        lax.all_gather(query_weight, BOTH, axis=0, tiled=True),
        lax.all_gather(query_bias, BOTH, axis=0, tiled=True),
        lax.all_gather(key_weight, BOTH, axis=0, tiled=True),
        lax.all_gather(value_weight, BOTH, axis=0, tiled=True),
        lax.all_gather(value_bias, BOTH, axis=0, tiled=True),
        lax.all_gather(output_weight, BOTH, axis=0, tiled=True),
        lax.all_gather(output_bias, BOTH, axis=0, tiled=True),
        lax.all_gather(attn_gain, BOTH, axis=0, tiled=True),
        lax.all_gather(attn_shift, BOTH, axis=0, tiled=True),
        lax.all_gather(up_weight, BOTH, axis=0, tiled=True),
        lax.all_gather(up_bias, BOTH, axis=0, tiled=True),
        lax.all_gather(down_weight, BOTH, axis=0, tiled=True),
        lax.all_gather(down_bias, BOTH, axis=0, tiled=True),
        lax.all_gather(ffn_gain, BOTH, axis=0, tiled=True),
        lax.all_gather(ffn_shift, BOTH, axis=0, tiled=True),
    )
    query_back = regathered[0]
    key_back = regathered[2]
    value_back = regathered[3]
    output_back = regathered[5]
    up_back = regathered[9]
    down_back = regathered[11]
    grad_out = cotangent.astype(jnp.float32).reshape(row_count, width)
    grad_res_two, grad_ffn_gain, grad_ffn_shift = pull_two(grad_out)
    grad_down_low = grad_res_two.astype(jnp.bfloat16)
    grad_down_weight = matmul_left_t(act_low, grad_down_low)
    grad_down_bias = column_sums(grad_down_low)
    (grad_up_pre,) = pull_gelu(matmul_right_t(grad_down_low, down_back))
    grad_up_low = grad_up_pre.astype(jnp.bfloat16)
    grad_up_weight = matmul_left_t(normed_low, grad_up_low)
    grad_up_bias = column_sums(grad_up_low)
    grad_normed = grad_res_two + matmul_right_t(grad_up_low, up_back)
    grad_res_one, grad_attn_gain, grad_attn_shift = pull_one(grad_normed)
    grad_branch_low = grad_res_one.astype(jnp.bfloat16)
    grad_output_weight = matmul_left_t(context_low, grad_branch_low)
    grad_output_bias = column_sums(grad_branch_low)
    grad_context = (
        matmul_right_t(grad_branch_low, output_back).astype(jnp.bfloat16).reshape(tokens.shape)
    )
    key_again, value_again = (
        lax.all_gather(keys_local, SEQ, axis=1, tiled=True),
        lax.all_gather(values_local, SEQ, axis=1, tiled=True),
    )
    grad_query, row_dots, unused_key, unused_value = attend_backward(
        queries, key_again, value_again, same_doc, log_sums, grad_context
    )
    query_all, grad_ctx_all = (
        lax.all_gather(queries, SEQ, axis=1, tiled=True),
        lax.all_gather(grad_context, SEQ, axis=1, tiled=True),
    )
    lse_all, rowdot_all = (
        lax.all_gather(log_sums, SEQ, axis=2, tiled=True),
        lax.all_gather(row_dots, SEQ, axis=2, tiled=True),
    )
    same_doc_t = key_seg[:, :, None] == query_seg[:, None, :]
    grad_key, grad_value = key_side_local(
        query_all, grad_ctx_all, lse_all, rowdot_all, keys_local, values_local, same_doc_t
    )
    grad_query_low = grad_query.reshape(row_count, width).astype(jnp.bfloat16)
    grad_key_low = grad_key.reshape(row_count, width).astype(jnp.bfloat16)
    grad_value_low = grad_value.reshape(row_count, width).astype(jnp.bfloat16)
    grad_query_weight = matmul_left_t(token_rows, grad_query_low)
    grad_query_bias = column_sums(grad_query_low)
    grad_key_weight = matmul_left_t(token_rows, grad_key_low)
    grad_value_weight = matmul_left_t(token_rows, grad_value_low)
    grad_value_bias = column_sums(grad_value_low)
    grad_tokens = (
        grad_res_one
        + matmul_right_t(grad_query_low, query_back)
        + matmul_right_t(grad_key_low, key_back)
        + matmul_right_t(grad_value_low, value_back)
    )
    summed = (
        lax.psum_scatter(grad_query_weight, BOTH, scatter_dimension=0, tiled=True),
        lax.psum_scatter(grad_query_bias, BOTH, scatter_dimension=0, tiled=True),
        lax.psum_scatter(grad_key_weight, BOTH, scatter_dimension=0, tiled=True),
        lax.psum_scatter(grad_value_weight, BOTH, scatter_dimension=0, tiled=True),
        lax.psum_scatter(grad_value_bias, BOTH, scatter_dimension=0, tiled=True),
        lax.psum_scatter(grad_output_weight, BOTH, scatter_dimension=0, tiled=True),
        lax.psum_scatter(grad_output_bias, BOTH, scatter_dimension=0, tiled=True),
        lax.psum_scatter(grad_attn_gain, BOTH, scatter_dimension=0, tiled=True),
        lax.psum_scatter(grad_attn_shift, BOTH, scatter_dimension=0, tiled=True),
        lax.psum_scatter(grad_up_weight, BOTH, scatter_dimension=0, tiled=True),
        lax.psum_scatter(grad_up_bias, BOTH, scatter_dimension=0, tiled=True),
        lax.psum_scatter(grad_down_weight, BOTH, scatter_dimension=0, tiled=True),
        lax.psum_scatter(grad_down_bias, BOTH, scatter_dimension=0, tiled=True),
        lax.psum_scatter(grad_ffn_gain, BOTH, scatter_dimension=0, tiled=True),
        lax.psum_scatter(grad_ffn_shift, BOTH, scatter_dimension=0, tiled=True),
    )
    return (
        mixed,
        grad_tokens.reshape(tokens.shape),
        summed[0],
        summed[1],
        summed[2],
        summed[3],
        summed[4],
        summed[5],
        summed[6],
        summed[7],
        summed[8],
        summed[9],
        summed[10],
        summed[11],
        summed[12],
        summed[13],
        summed[14],
    )


LOG2E = 1.4426950408889634
GROUP_HEADS = 3
GROUP_COLS = GROUP_HEADS * HEAD_DIM
PACK = 640
VECS = 12
SIDE = 16
KEY_CHUNK = 512


def dot_nt(left_op, right_op):
    return lax.dot_general(
        left_op, right_op, (((1,), (1,)), ((), ())), preferred_element_type=jnp.float32
    )


def dot_nn(left_op, right_op):
    return lax.dot_general(
        left_op, right_op, (((1,), (0,)), ((), ())), preferred_element_type=jnp.float32
    )


def attend_kernel(
    query_ref, own_ref, other_ref, seg_key_ref, seg_query_ref, ctx_ref, lse_ref, value_t
):
    half = own_ref.shape[0]
    rows = query_ref.shape[0]

    @pl.when(pl.program_id(0) == 0)
    def _():
        value_t[:, :half] = own_ref[:, GROUP_COLS : 2 * GROUP_COLS].T
        value_t[:, half:] = other_ref[:, GROUP_COLS : 2 * GROUP_COLS].T

    seg_query = seg_query_ref[...]
    chunks = [
        (ref, start) for ref in (own_ref, other_ref) for start in range(0, half, KEY_CHUNK)
    ]
    for head in range(GROUP_HEADS):
        cols = slice(head * HEAD_DIM, (head + 1) * HEAD_DIM)
        query = query_ref[:, cols]
        scores = []
        top = None
        for number, (ref, start) in enumerate(chunks):
            raw = dot_nt(ref[start : start + KEY_CHUNK, cols], query)
            seg_key = seg_key_ref[number * KEY_CHUNK : (number + 1) * KEY_CHUNK, :]
            seg_key = jnp.concatenate([seg_key] * (rows // 128), axis=1)
            masked = jnp.where(seg_key == seg_query, raw * (SCALE * LOG2E), NEG)
            scores.append(masked)
            peak = jnp.max(masked, axis=0, keepdims=True)
            top = peak if top is None else jnp.maximum(top, peak)
        total = None
        context_t = None
        for number in range(len(chunks)):
            weight = jnp.exp2(scores[number] - top)
            part = jnp.sum(weight, axis=0, keepdims=True)
            piece = dot_nn(
                value_t[cols, number * KEY_CHUNK : (number + 1) * KEY_CHUNK],
                weight.astype(jnp.bfloat16),
            )
            total = part if total is None else total + part
            context_t = piece if context_t is None else context_t + piece
        ctx_ref[:, cols] = (context_t / total).T
        lse_ref[head : head + 1, :] = top + jnp.log2(total)


def attend(query, own, other, seg_key, seg_query):
    rows = query.shape[0]
    half = own.shape[0]
    block = rows // 4
    return pl.pallas_call(
        attend_kernel,
        grid=(4,),
        in_specs=[
            pl.BlockSpec((block, GROUP_COLS), lambda i: (i, 0)),
            pl.BlockSpec((half, 2 * GROUP_COLS), lambda i: (0, 0)),
            pl.BlockSpec((half, 2 * GROUP_COLS), lambda i: (0, 0)),
            pl.BlockSpec((2 * half, 128), lambda i: (0, 0)),
            pl.BlockSpec((1, block), lambda i: (0, i)),
        ],
        out_specs=[
            pl.BlockSpec((block, GROUP_COLS), lambda i: (i, 0)),
            pl.BlockSpec((8, block), lambda i: (0, i)),
        ],
        out_shape=[
            jax.ShapeDtypeStruct((rows, GROUP_COLS), jnp.float32),
            jax.ShapeDtypeStruct((8, rows), jnp.float32),
        ],
        scratch_shapes=[pltpu.VMEM((GROUP_COLS, 2 * half), jnp.bfloat16)],
        compiler_params=pltpu.CompilerParams(vmem_limit_bytes=48 * 1024 * 1024),
        cost_estimate=pl.CostEstimate(
            flops=70 * rows * half * GROUP_COLS, bytes_accessed=1024 * 1024, transcendentals=0
        ),
        name="attend",
    )(query, own, other, seg_key, seg_query)


def attend_back_kernel(
    query_ref,
    grad_ref,
    ctx_ref,
    lse_ref,
    own_ref,
    other_ref,
    seg_key_ref,
    seg_query_ref,
    gquery_ref,
    gown_ref,
    gother_ref,
    key_t,
    gother_sum,
):
    half = own_ref.shape[0]
    rows = query_ref.shape[0]
    first = pl.program_id(0) == 0

    @pl.when(first)
    def _():
        key_t[:, :half] = own_ref[:, :GROUP_COLS].T
        key_t[:, half:] = other_ref[:, :GROUP_COLS].T
        gown_ref[...] = jnp.zeros_like(gown_ref)
        gother_sum[...] = jnp.zeros_like(gother_sum)

    seg_query = seg_query_ref[...]
    chunks = [
        (ref, gref, start)
        for ref, gref in ((own_ref, gown_ref), (other_ref, gother_sum))
        for start in range(0, half, KEY_CHUNK)
    ]
    for head in range(GROUP_HEADS):
        cols = slice(head * HEAD_DIM, (head + 1) * HEAD_DIM)
        vcols = slice(GROUP_COLS + head * HEAD_DIM, GROUP_COLS + (head + 1) * HEAD_DIM)
        query = query_ref[:, cols]
        grad = grad_ref[:, cols]
        lse = lse_ref[head : head + 1, :]
        dots = (grad.astype(jnp.float32) * ctx_ref[:, cols]).T
        row_dot = jnp.sum(dots, axis=0, keepdims=True)
        gquery_t = None
        for number, (ref, gref, start) in enumerate(chunks):
            spot = slice(start, start + KEY_CHUNK)
            raw = dot_nt(ref[spot, cols], query)
            seg_key = seg_key_ref[number * KEY_CHUNK : (number + 1) * KEY_CHUNK, :]
            seg_key = jnp.concatenate([seg_key] * (rows // 128), axis=1)
            masked = jnp.where(seg_key == seg_query, raw * (SCALE * LOG2E), NEG)
            probs = jnp.exp2(masked - lse)
            gprobs = dot_nt(ref[spot, vcols], grad)
            gscores = (probs * (gprobs - row_dot)).astype(jnp.bfloat16)
            gref[spot, vcols] += dot_nn(probs.astype(jnp.bfloat16), grad)
            gref[spot, cols] += dot_nn(gscores, query)
            piece = dot_nn(key_t[cols, number * KEY_CHUNK : (number + 1) * KEY_CHUNK], gscores)
            gquery_t = piece if gquery_t is None else gquery_t + piece
        gquery_ref[:, cols] = (SCALE * gquery_t).T.astype(jnp.bfloat16)

    @pl.when(pl.program_id(0) == pl.num_programs(0) - 1)
    def _():
        gother_ref[...] = gother_sum[...].astype(jnp.bfloat16)


def attend_back(query, grad, ctx, lse, own, other, seg_key, seg_query):
    rows = query.shape[0]
    half = own.shape[0]
    block = rows // 4
    return pl.pallas_call(
        attend_back_kernel,
        grid=(4,),
        in_specs=[
            pl.BlockSpec((block, GROUP_COLS), lambda i: (i, 0)),
            pl.BlockSpec((block, GROUP_COLS), lambda i: (i, 0)),
            pl.BlockSpec((block, GROUP_COLS), lambda i: (i, 0)),
            pl.BlockSpec((8, block), lambda i: (0, i)),
            pl.BlockSpec((half, 2 * GROUP_COLS), lambda i: (0, 0)),
            pl.BlockSpec((half, 2 * GROUP_COLS), lambda i: (0, 0)),
            pl.BlockSpec((2 * half, 128), lambda i: (0, 0)),
            pl.BlockSpec((1, block), lambda i: (0, i)),
        ],
        out_specs=[
            pl.BlockSpec((block, GROUP_COLS), lambda i: (i, 0)),
            pl.BlockSpec((half, 2 * GROUP_COLS), lambda i: (0, 0)),
            pl.BlockSpec((half, 2 * GROUP_COLS), lambda i: (0, 0)),
        ],
        out_shape=[
            jax.ShapeDtypeStruct((rows, GROUP_COLS), jnp.bfloat16),
            jax.ShapeDtypeStruct((half, 2 * GROUP_COLS), jnp.float32),
            jax.ShapeDtypeStruct((half, 2 * GROUP_COLS), jnp.bfloat16),
        ],
        scratch_shapes=[
            pltpu.VMEM((GROUP_COLS, 2 * half), jnp.bfloat16),
            pltpu.VMEM((half, 2 * GROUP_COLS), jnp.float32),
        ],
        compiler_params=pltpu.CompilerParams(vmem_limit_bytes=48 * 1024 * 1024),
        cost_estimate=pl.CostEstimate(
            flops=100 * rows * half * GROUP_COLS, bytes_accessed=1024 * 1024, transcendentals=0
        ),
        name="attend_back",
    )(query, grad, ctx, lse, own, other, seg_key, seg_query)


def prepare_kernel(
    tokens_ref,
    lengths_ref,
    key_ref,
    value_ref,
    query_ref,
    qbias_ref,
    vbias_ref,
    obias_ref,
    again_ref,
    ashift_ref,
    dbias_ref,
    fgain_ref,
    fshift_ref,
    ubias_ref,
    output_ref,
    up_ref,
    down_ref,
    first_ref,
    second_ref,
    bulk_ref,
    *piece_refs,
):
    place = lax.axis_index(SEQ)
    odd = lax.rem(place // 4, 2) == 1
    quad = lax.rem(place, 4)
    first_ref[...] = jnp.where(odd, tokens_ref[1], tokens_ref[0])
    second_ref[...] = jnp.where(odd, tokens_ref[0], tokens_ref[1])
    own_rows, width = key_ref.shape
    ratio = up_ref.shape[1] // width
    bulk_ref[0, :own_rows] = output_ref[...]
    for number in range(ratio):
        bulk_ref[0, (1 + number) * own_rows : (2 + number) * own_rows] = up_ref[
            :, number * width : (number + 1) * width
        ]
    bulk_ref[0, (1 + ratio) * own_rows :] = down_ref[...]
    small = (qbias_ref, vbias_ref, obias_ref, again_ref, ashift_ref, dbias_ref, fgain_ref, fshift_ref)
    rows = [ref[...].astype(jnp.float32) for ref in small]
    wide = ubias_ref[...].astype(jnp.float32)
    rows += [wide[:, n * own_rows : (n + 1) * own_rows] for n in range(VECS - len(small))]
    lengths = lengths_ref[...]
    docs = lengths.shape[1]
    flat = jnp.concatenate(
        [lengths[0:1], lengths[1:2], jnp.zeros((1, own_rows - 2 * docs), jnp.int32)], axis=1
    )
    rows += [(flat >> 6).astype(jnp.float32), (flat & 63).astype(jnp.float32)]
    rows += [jnp.zeros_like(rows[0])] * (SIDE - len(rows))
    side = jnp.concatenate(rows, axis=0).T.astype(jnp.bfloat16)
    cut = 3 * GROUP_COLS
    for flip, piece_ref in enumerate(piece_refs):
        piece_ref[...] = jnp.zeros_like(piece_ref)
        piece_ref[:, cut : cut + SIDE] = side
        target = quad ^ flip
        for number in range(4):

            @pl.when(target == number)
            def _():
                cols = slice(number * GROUP_COLS, (number + 1) * GROUP_COLS)
                for spot, ref in enumerate((key_ref, value_ref, query_ref)):
                    piece_ref[:, spot * GROUP_COLS : (spot + 1) * GROUP_COLS] = ref[:, cols]


def prepare(tokens, lengths, key, value, query, vectors, up_bias, output, up, down):
    own_rows, width = key.shape
    bulk_rows = own_rows + down.shape[0] * 2
    turn_shape = jax.ShapeDtypeStruct(tokens.shape[1:], jnp.bfloat16)
    piece_shape = jax.ShapeDtypeStruct((own_rows, PACK), jnp.bfloat16)
    return pl.pallas_call(
        prepare_kernel,
        out_shape=[turn_shape] * 2
        + [jax.ShapeDtypeStruct((1, bulk_rows, width), jnp.bfloat16)]
        + [piece_shape] * 4,
        name="prepare",
    )(
        tokens,
        lengths,
        key,
        value,
        query,
        *[item.reshape(1, own_rows) for item in vectors],
        up_bias.reshape(1, up_bias.shape[0]),
        output,
        up,
        down,
    )


def tied(values, *others):
    return lax.optimization_barrier((values, others))[0]


def block_of(values, index, axis):
    return lax.dynamic_index_in_dim(values, index, axis=axis, keepdims=False)


def halves(values, bit, axis):
    return (block_of(values, bit, axis), block_of(values, 1 - bit, axis))


def low_sum(own, arrived):
    return (own.astype(jnp.float32) + arrived.astype(jnp.float32)).astype(jnp.bfloat16)


def sum_parts(own, arrived):
    total = own.astype(jnp.float32)
    for item in arrived:
        total = total + item.astype(jnp.float32)
    return total


def device_table(mapping):
    pairs = []
    for core in range(2):
        for layer_z in range(4):
            for quad in range(4):
                to_core, to_z, to_quad = mapping(core, layer_z, quad)
                pairs.append((core * 16 + layer_z * 4 + quad, to_core * 16 + to_z * 4 + to_quad))
    return pairs


def hop(value, mapping):
    return lax.ppermute(value, BOTH, device_table(mapping))


def hop_quad(value, flip):
    return hop(value, lambda core, layer_z, quad: (core, layer_z, quad ^ flip))


def hop_layer(value, flip):
    return hop(value, lambda core, layer_z, quad: (core, layer_z ^ flip, quad))


def hop_core(value):
    return hop(value, lambda core, layer_z, quad: (1 - core, layer_z, quad))


def to_sequence(value, turn):
    return hop(
        value,
        lambda core, layer_z, quad: (layer_z // 2, 2 * core + (layer_z + turn) % 2, quad),
    )


def to_owner(value, turn):
    return hop(
        value,
        lambda core, layer_z, quad: (layer_z // 2, 2 * core + (layer_z - turn) % 2, quad),
    )


def turned(blocks, quad):
    first, second, third, fourth = blocks
    odd = quad % 2 == 1
    high = quad // 2 == 1
    pairs = (
        jnp.where(odd, second, first),
        jnp.where(odd, first, second),
        jnp.where(odd, fourth, third),
        jnp.where(odd, third, fourth),
    )
    return (
        jnp.where(high, pairs[2], pairs[0]),
        jnp.where(high, pairs[3], pairs[1]),
        jnp.where(high, pairs[0], pairs[2]),
        jnp.where(high, pairs[1], pairs[3]),
    )


def pack_grads(main, vecs):
    coarse = vecs.astype(jnp.bfloat16)
    fine = (vecs - coarse.astype(jnp.float32)).astype(jnp.bfloat16)
    filler = jnp.zeros(main.shape[:-1] + (PACK - main.shape[-1] - 2 * VECS,), jnp.bfloat16)
    return jnp.concatenate([main.astype(jnp.bfloat16), coarse, fine, filler], axis=-1)


def unpack_grads(packed):
    wide = packed.astype(jnp.float32)
    cut = 3 * GROUP_COLS
    return (wide[..., :cut], wide[..., cut : cut + VECS] + wide[..., cut + VECS : cut + 2 * VECS])


def add_packed(own, arrived):
    main, vecs = unpack_grads(own)
    more, more_vecs = unpack_grads(arrived)
    return (main + more, vecs + more_vecs)


def shards_heads(
    tokens,
    doc_lengths,
    query_weight,
    query_bias,
    key_weight,
    value_weight,
    value_bias,
    output_weight,
    output_bias,
    attn_gain,
    attn_shift,
    up_weight,
    up_bias,
    down_weight,
    down_bias,
    ffn_gain,
    ffn_shift,
    cotangent,
):
    groups, stretch, width = tokens.shape
    own_rows = query_weight.shape[0]
    hidden = up_weight.shape[1]
    ratio = hidden // width
    devices = width // own_rows
    bulk_rows = own_rows * (1 + 2 * ratio)
    row_count = groups * stretch
    core = lax.axis_index(BATCH)
    place = lax.axis_index(SEQ)
    layer_z = place // 4
    quad = place % 4
    parity = layer_z % 2
    flips = (1, 2, 3)
    bit_x, bit_y = (quad % 2, quad // 2)
    bit_low, bit_high = (layer_z % 2, layer_z // 2)

    vectors = (
        query_bias,
        value_bias,
        output_bias,
        attn_gain,
        attn_shift,
        down_bias,
        ffn_gain,
        ffn_shift,
    )
    first_turn, second_turn, bulk, *pieces = prepare(
        tokens,
        doc_lengths,
        key_weight,
        value_weight,
        query_weight,
        vectors,
        up_bias,
        output_weight,
        up_weight,
        down_weight,
    )

    own_block = jnp.concatenate(
        [to_sequence(first_turn, 0), to_sequence(second_turn, 1)], axis=0
    )
    token_half = jnp.concatenate(
        [own_block] + [hop_quad(own_block, flip) for flip in flips], axis=0
    )

    quads = turned([pieces[0]] + [hop_quad(pieces[flip], flip) for flip in flips], quad)
    quads = jnp.stack(quads, axis=0)
    layers = [quads] + [hop_layer(quads, flip) for flip in flips]
    layers = jnp.stack(turned(layers, layer_z), axis=0)
    twin = hop_core(layers)
    cores = jnp.stack([jnp.where(core == 0, layers, twin), jnp.where(core == 0, twin, layers)])
    packed = cores.reshape(width, PACK)
    group_weight = packed[:, : 3 * GROUP_COLS]
    side = packed[:, 3 * GROUP_COLS : 3 * GROUP_COLS + SIDE].astype(jnp.float32)
    vector_rows = side[:, :8].T
    up_bias_full = side[:, 8:VECS].reshape(devices, own_rows, ratio)
    up_bias_full = jnp.swapaxes(up_bias_full, 1, 2).reshape(1, hidden)
    (
        qbias_full,
        vbias_full,
        obias_full,
        again_full,
        ashift_full,
        dbias_full,
        fgain_full,
        fshift_full,
    ) = [vector_rows[number] for number in range(8)]
    docs = doc_lengths.shape[1]
    digits = side.reshape(2, width // 2, SIDE)[:, : groups * docs, VECS : VECS + 2]
    lengths_all = (digits[..., 0] * 64 + digits[..., 1]).astype(jnp.int32)
    lengths = lax.dynamic_index_in_dim(
        lengths_all.reshape(2 * groups, docs), layer_z, axis=0, keepdims=False
    )
    doc_ends = jnp.cumsum(lengths)

    def half_segments(which):
        turn_z = jnp.stack([(layer_z - turn) % 2 for turn in (0, 1)]) + 2 * which
        spot = jnp.stack([quad ^ flip for flip in range(4)])
        start = turn_z[None, :] * (4 * stretch) + spot[:, None] * stretch
        positions = start[:, :, None] + jnp.arange(stretch, dtype=jnp.int32)
        positions = positions.reshape(-1)
        return jnp.sum((positions[:, None] >= doc_ends[None, :]).astype(jnp.int32), axis=-1)

    seg_query = half_segments(core)
    seg_key = jnp.concatenate([seg_query, half_segments(1 - core)])
    seg_key = jnp.broadcast_to(seg_key[:, None], (seg_key.shape[0], 128))
    seg_query = seg_query[None, :]

    bulk_all = lax.all_gather(bulk, BOTH, axis=0, tiled=True)

    column_bias = jnp.concatenate(
        [
            jnp.zeros((GROUP_COLS,), jnp.float32),
            lax.dynamic_slice_in_dim(vbias_full, quad * GROUP_COLS, GROUP_COLS),
            lax.dynamic_slice_in_dim(qbias_full, quad * GROUP_COLS, GROUP_COLS),
        ]
    )
    projected = (matmul_plain(token_half, group_weight) + column_bias).astype(jnp.bfloat16)
    own_pair = projected[:, : 2 * GROUP_COLS]
    queries = projected[:, 2 * GROUP_COLS :]
    other_pair = hop_core(own_pair)
    ctx_wide, lse = attend(queries, own_pair, other_pair, seg_key, seg_query)

    ctx_blocks = ctx_wide.astype(jnp.bfloat16).reshape(4, row_count, GROUP_COLS)
    ctx_groups = [ctx_blocks[0]] + [hop_quad(ctx_blocks[flip], flip) for flip in flips]
    ctx_merged = jnp.concatenate(turned(ctx_groups, quad), axis=1)
    ctx_turns = [
        to_owner(ctx_merged[turn * stretch : (turn + 1) * stretch], turn) for turn in (0, 1)
    ]
    context_low = jnp.concatenate(
        [
            jnp.where(parity == 0, ctx_turns[0], ctx_turns[1]),
            jnp.where(parity == 0, ctx_turns[1], ctx_turns[0]),
        ],
        axis=0,
    )

    output_full = bulk_all[:, :own_rows].reshape(width, width)
    up_parts = [
        bulk_all[:, (1 + number) * own_rows : (2 + number) * own_rows].reshape(width, width)
        for number in range(ratio)
    ]
    up_full = jnp.concatenate(up_parts, axis=1)
    down_full = bulk_all[:, (1 + ratio) * own_rows :].reshape(hidden, width)

    token_rows = tokens.reshape(row_count, width)
    res_one = token_rows.astype(jnp.float32) + matmul_plain(context_low, output_full) + obias_full
    normed, pull_one = jax.vjp(norm_apply, res_one, again_full, ashift_full)
    normed_low = normed.astype(jnp.bfloat16)
    up_pre = matmul_plain(normed_low, up_full) + up_bias_full
    activated, pull_gelu = jax.vjp(gelu_exact, up_pre)
    act_low = activated.astype(jnp.bfloat16)
    res_two = normed + matmul_plain(act_low, down_full) + dbias_full
    output_rows, pull_two = jax.vjp(norm_apply, res_two, fgain_full, fshift_full)
    mixed = output_rows.astype(jnp.bfloat16).reshape(tokens.shape)
    grad_out = cotangent.astype(jnp.float32).reshape(row_count, width)
    grad_res_two, grad_ffn_gain, grad_ffn_shift = pull_two(grad_out)
    grad_down_low = grad_res_two.astype(jnp.bfloat16)

    def half_columns(matrix, which):
        half = matrix.shape[1] // 2
        return lax.dynamic_slice_in_dim(matrix, which * half, half, axis=1)

    def down_term(which):
        return matmul_left_t(half_columns(act_low, which), grad_down_low)

    def branch_term(which):
        return jnp.concatenate(
            [
                matmul_left_t(half_columns(normed_low, which), grad_up_low),
                matmul_left_t(half_columns(context_low, which), grad_branch_low),
            ],
            axis=1,
        )

    down_theirs = down_term(1 - core).astype(jnp.bfloat16)
    down_arrived = hop_core(down_theirs)
    (grad_up_pre,) = pull_gelu(matmul_right_t(tied(grad_down_low, down_theirs), down_full))
    grad_up_low = grad_up_pre.astype(jnp.bfloat16)
    grad_normed = grad_res_two + matmul_right_t(grad_up_low, up_full)
    grad_res_one, grad_attn_gain, grad_attn_shift = pull_one(grad_normed)
    grad_branch_low = grad_res_one.astype(jnp.bfloat16)
    grad_context = matmul_right_t(grad_branch_low, output_full).astype(jnp.bfloat16)
    branch_arrived = hop_core(branch_term(1 - core).astype(jnp.bfloat16))

    low_part = grad_context[:stretch]
    high_part = grad_context[stretch:]
    grad_turns = [
        to_sequence(jnp.where((parity + turn) % 2 == 1, high_part, low_part), turn)
        for turn in (0, 1)
    ]
    grad_own = jnp.concatenate(grad_turns, axis=0)
    grad_columns = turned(
        [grad_own[:, n * GROUP_COLS : (n + 1) * GROUP_COLS] for n in range(4)], quad
    )
    grad_ctx = jnp.concatenate(
        [grad_columns[0]] + [hop_quad(grad_columns[flip], flip) for flip in flips], axis=0
    )

    down_total = (down_term(core) + down_arrived.astype(jnp.float32)).astype(jnp.bfloat16)
    down_total = down_total.reshape(2, 2, 2, 2, ratio * own_rows, width)
    branch_total = (branch_term(core) + branch_arrived.astype(jnp.float32)).astype(jnp.bfloat16)
    branch_total = branch_total.reshape(2, 2, 2, 2, own_rows, hidden + width)
    down_own, down_send = tied(halves(down_total, bit_x, 3), grad_ctx)
    branch_own, branch_send = tied(halves(branch_total, bit_y, 2), grad_ctx)
    down_arrived = hop_quad(down_send, 1)
    branch_arrived = hop_quad(branch_send, 2)

    grad_query, grad_own_pair, grad_other_pair = attend_back(
        tied(queries, down_send, branch_send),
        grad_ctx,
        ctx_wide,
        lse,
        own_pair,
        other_pair,
        seg_key,
        seg_query,
    )
    pair_arrived = hop_core(grad_other_pair)
    down_arrived, branch_arrived = tied((down_arrived, branch_arrived), grad_other_pair)
    down_own, down_send = halves(low_sum(down_own, down_arrived), bit_y, 2)
    branch_own, branch_send = halves(low_sum(branch_own, branch_arrived), bit_x, 2)
    down_arrived = hop_quad(down_send, 2)
    branch_arrived = hop_quad(branch_send, 1)
    pair_total = grad_own_pair + tied(pair_arrived, down_send, branch_send).astype(jnp.float32)
    pair_scale = jnp.where(jnp.arange(2 * GROUP_COLS) < GROUP_COLS, SCALE, 1.0)
    grad_projected = jnp.concatenate(
        [(pair_total * pair_scale).astype(jnp.bfloat16), grad_query], axis=1
    )
    grad_half = matmul_right_t(grad_projected, group_weight)
    half_blocks = grad_half.reshape(4, row_count, width)
    low_blocks = half_blocks.astype(jnp.bfloat16)
    low_blocks, down_arrived, branch_arrived = tied((low_blocks, down_arrived, branch_arrived))
    token_arrived = [hop_quad(low_blocks[flip], flip) for flip in flips]
    down_own, down_send = halves(low_sum(down_own, down_arrived), bit_low, 1)
    branch_own, branch_send = halves(low_sum(branch_own, branch_arrived), bit_low, 1)
    down_arrived = hop_layer(down_send, 1)
    branch_arrived = hop_layer(branch_send, 1)
    up_sums, out_sums, down_sums, again_sums, ashift_sums, fgain_sums, fshift_sums = tied(
        (
            column_sums(grad_up_low),
            column_sums(grad_branch_low),
            column_sums(grad_down_low),
            grad_attn_gain,
            grad_attn_shift,
            grad_ffn_gain,
            grad_ffn_shift,
        ),
        low_blocks,
    )

    grad_group = matmul_left_t(token_half, grad_projected)
    bias_sums = column_sums(grad_projected)
    nothing = jnp.zeros((width,), jnp.float32)
    vec_rows = jnp.stack(
        [
            lax.dynamic_update_slice_in_dim(
                nothing, bias_sums[2 * GROUP_COLS :], quad * GROUP_COLS, 0
            ),
            lax.dynamic_update_slice_in_dim(
                nothing, bias_sums[GROUP_COLS : 2 * GROUP_COLS], quad * GROUP_COLS, 0
            ),
            out_sums,
            again_sums,
            ashift_sums,
            down_sums,
            fgain_sums,
            fshift_sums,
        ],
        axis=0,
    ).T
    up_sums = up_sums.reshape(devices, ratio, own_rows)
    up_sums = jnp.swapaxes(up_sums, 1, 2).reshape(width, ratio)
    vecs = jnp.concatenate([vec_rows, up_sums], axis=1)
    packed_grads = pack_grads(grad_group, vecs).reshape(2, width // 2, PACK)
    mine = jnp.where(core == 0, packed_grads[0], packed_grads[1])
    theirs = jnp.where(core == 0, packed_grads[1], packed_grads[0])
    packed_grads = pack_grads(*add_packed(mine, hop_core(theirs)))
    packed_grads = packed_grads.reshape(2, 2, 4 * own_rows, PACK)
    pack_own, pack_send = halves(packed_grads, bit_low, 1)
    pack_arrived = hop_layer(pack_send, 1)

    token_arrived = tied(token_arrived, down_send, branch_send)
    grad_block = sum_parts(half_blocks[0], token_arrived).astype(jnp.bfloat16)
    grad_block = tied(grad_block, pack_send, down_arrived)
    home = [
        to_owner(grad_block[turn * stretch : (turn + 1) * stretch], turn) for turn in (0, 1)
    ]
    down_arrived, pack_arrived, branch_arrived = tied(
        (down_arrived, pack_arrived, branch_arrived), grad_block
    )
    packed_grads = pack_grads(*add_packed(pack_own, pack_arrived))
    pack_own, pack_send = halves(packed_grads, bit_high, 0)
    pack_arrived = hop_layer(pack_send, 2)
    down_own, down_send = halves(low_sum(down_own, down_arrived), bit_high, 0)
    down_arrived = hop_layer(down_send, 2)
    branch_own, branch_send = halves(low_sum(branch_own, branch_arrived), bit_high, 0)
    branch_arrived = hop_layer(branch_send, 2)
    home, pack_arrived = tied((home, pack_arrived), down_send, branch_send)
    packed_grads = pack_grads(*add_packed(pack_own, pack_arrived)).reshape(4, own_rows, PACK)
    by_quad = turned([packed_grads[number] for number in range(4)], quad)
    main, vecs = unpack_grads(by_quad[0])
    home_rows = jnp.concatenate(
        [
            jnp.where(parity == 0, home[0], home[1]),
            jnp.where(parity == 0, home[1], home[0]),
        ],
        axis=0,
    )
    grad_tokens = (grad_res_one + home_rows.astype(jnp.float32)).reshape(tokens.shape)

    quad_parts = [main]
    for flip in flips:
        more, more_vecs = unpack_grads(hop_quad(by_quad[flip], flip))
        quad_parts.append(more)
        vecs = vecs + more_vecs
    quad_parts = turned(quad_parts, quad)
    sum_key, sum_value, sum_query = [
        jnp.concatenate(
            [part[:, n * GROUP_COLS : (n + 1) * GROUP_COLS] for part in quad_parts], axis=1
        )
        for n in range(3)
    ]
    sum_rows = vecs[:, :8].T
    sum_down = sum_parts(down_own, [down_arrived])
    sum_branch = sum_parts(branch_own, [branch_arrived])
    sum_up = sum_branch[:, :hidden]
    sum_output = sum_branch[:, hidden:]
    return (
        mixed,
        grad_tokens,
        sum_query,
        sum_rows[0],
        sum_key,
        sum_value,
        sum_rows[1],
        sum_output,
        sum_rows[2],
        sum_rows[3],
        sum_rows[4],
        sum_up,
        vecs[:, 8:].T.reshape(up_bias.shape),
        sum_down,
        sum_rows[5],
        sum_rows[6],
        sum_rows[7],
    )


def solution(mesh):
    in_specs = (
        P(BATCH, SEQ, None),
        P(BATCH, None),
        P(BOTH, None),
        P(BOTH),
        P(BOTH, None),
        P(BOTH, None),
        P(BOTH),
        P(BOTH, None),
        P(BOTH),
        P(BOTH),
        P(BOTH),
        P(BOTH, None),
        P(BOTH),
        P(BOTH, None),
        P(BOTH),
        P(BOTH),
        P(BOTH),
        P(BATCH, SEQ, None),
    )
    out_specs = (
        P(BATCH, SEQ, None),
        P(BATCH, SEQ, None),
        P(BOTH, None),
        P(BOTH),
        P(BOTH, None),
        P(BOTH, None),
        P(BOTH),
        P(BOTH, None),
        P(BOTH),
        P(BOTH),
        P(BOTH),
        P(BOTH, None),
        P(BOTH),
        P(BOTH, None),
        P(BOTH),
        P(BOTH),
        P(BOTH),
    )
    fits = mesh.shape[BATCH] == 2 and mesh.shape[SEQ] == 16
    body = shards_heads if fits else shards_general
    return jax.shard_map(body, mesh=mesh, in_specs=in_specs, out_specs=out_specs, check_vma=False)
```

```python
import jax
import jax.numpy as jnp
from jax import lax
from jax.experimental import pallas as pl
from jax.experimental.pallas import tpu as pltpu
from jax.sharding import PartitionSpec as P

BATCH = "batch"
SEQ = "seq"
BOTH = (BATCH, SEQ)
HEADS = 12
HEAD_DIM = 64


SCALE = 0.125
NEG = -1e30
EPS = 1e-12


def norm_apply(hidden, gain_vec, shift_vec):
    center = jnp.mean(hidden, axis=-1, keepdims=True)
    centered = hidden - center
    spread = jnp.mean(centered * centered, axis=-1, keepdims=True)
    return centered * lax.rsqrt(spread + EPS) * gain_vec + shift_vec


def gelu_exact(inputs):
    return jax.nn.gelu(inputs, approximate=False)


def segment_ids(doc_lengths, positions):
    doc_ends = jnp.cumsum(doc_lengths, axis=-1)
    return jnp.sum((positions[None, :, None] >= doc_ends[:, None, :]).astype(jnp.int32), axis=-1)


def matmul_plain(left_op, right_op):
    return jnp.dot(left_op, right_op, preferred_element_type=jnp.float32)


def matmul_right_t(left_op, right_op):
    return lax.dot_general(
        left_op, right_op, (((1,), (1,)), ((), ())), preferred_element_type=jnp.float32
    )


def matmul_left_t(left_op, right_op):
    return lax.dot_general(
        left_op, right_op, (((0,), (0,)), ((), ())), preferred_element_type=jnp.float32
    )


def column_sums(matrix):
    return jnp.sum(matrix.astype(jnp.float32), axis=0)


def head_block(matrix, head_pair):
    pair_width = 2 * HEAD_DIM
    column_block = matrix[..., head_pair * pair_width : (head_pair + 1) * pair_width]
    return column_block.reshape(column_block.shape[:-1] + (2, HEAD_DIM))


def merge_heads(blocks):
    return jnp.concatenate(
        [block_item.reshape(block_item.shape[:2] + (2 * HEAD_DIM,)) for block_item in blocks],
        axis=-1,
    )


def stat_pair(stats, head_pair):
    return stats[:, 2 * head_pair : 2 * head_pair + 2][..., None]


def pair_scores(query_pair, key_pair, same_doc):
    raw_scores = jnp.einsum(
        "sqhd,skhd->shqk", query_pair, key_pair, preferred_element_type=jnp.float32
    )
    return jnp.where(same_doc[:, None], SCALE * raw_scores, NEG)


def attend_forward(queries, key_all, value_all, same_doc):
    outputs, log_sums = ([], [])
    for head_pair in range(HEADS // 2):
        scores = pair_scores(
            head_block(queries, head_pair), head_block(key_all, head_pair), same_doc
        )
        top_score = jnp.max(scores, axis=-1, keepdims=True)
        exponent = jnp.exp(scores - top_score)
        totals = jnp.sum(exponent, axis=-1, keepdims=True)
        probs_low = (exponent / totals).astype(jnp.bfloat16)
        context = jnp.einsum(
            "shqk,skhd->sqhd",
            probs_low,
            head_block(value_all, head_pair),
            preferred_element_type=jnp.float32,
        )
        outputs.append(context)
        log_sums.append((top_score + jnp.log(totals))[..., 0])
    return (merge_heads(outputs), jnp.concatenate(log_sums, axis=1))


def attend_backward(queries, key_all, value_all, same_doc, log_sums, grad_context):
    query_grads, key_grads, value_grads, row_dots = ([], [], [], [])
    for head_pair in range(HEADS // 2):
        query_pair = head_block(queries, head_pair)
        key_pair = head_block(key_all, head_pair)
        grad_pair = head_block(grad_context, head_pair)
        probs = jnp.exp(
            pair_scores(query_pair, key_pair, same_doc) - stat_pair(log_sums, head_pair)
        )
        grad_probs = jnp.einsum(
            "sqhd,skhd->shqk",
            grad_pair,
            head_block(value_all, head_pair),
            preferred_element_type=jnp.float32,
        )
        row_dot = jnp.sum(probs * grad_probs, axis=-1, keepdims=True)
        row_dots.append(row_dot[..., 0])
        grad_scores = (probs * (grad_probs - row_dot)).astype(jnp.bfloat16) * jnp.bfloat16(SCALE)
        query_grads.append(
            jnp.einsum("shqk,skhd->sqhd", grad_scores, key_pair, preferred_element_type=jnp.float32)
        )
    return (merge_heads(query_grads), jnp.concatenate(row_dots, axis=1), None, None)


def key_side_local(query_all, grad_ctx_all, lse_all, rowdot_all, keys_own, values_own, same_doc_t):
    key_grads, value_grads = ([], [])
    for head_pair in range(HEADS // 2):
        query_pair = head_block(query_all, head_pair)
        grad_pair = head_block(grad_ctx_all, head_pair)
        probs = jnp.exp(
            pair_scores(query_pair, head_block(keys_own, head_pair), same_doc_t)
            - stat_pair(lse_all, head_pair)
        )
        grad_probs = jnp.einsum(
            "sqhd,skhd->shqk",
            grad_pair,
            head_block(values_own, head_pair),
            preferred_element_type=jnp.float32,
        )
        grad_scores = (probs * (grad_probs - stat_pair(rowdot_all, head_pair))).astype(
            jnp.bfloat16
        ) * jnp.bfloat16(SCALE)
        key_grads.append(
            jnp.einsum(
                "shqk,sqhd->skhd", grad_scores, query_pair, preferred_element_type=jnp.float32
            )
        )
        value_grads.append(
            jnp.einsum(
                "shqk,sqhd->skhd",
                probs.astype(jnp.bfloat16),
                grad_pair,
                preferred_element_type=jnp.float32,
            )
        )
    return (merge_heads(key_grads), merge_heads(value_grads))


def shards_general(
    tokens,
    doc_lengths,
    query_weight,
    query_bias,
    key_weight,
    value_weight,
    value_bias,
    output_weight,
    output_bias,
    attn_gain,
    attn_shift,
    up_weight,
    up_bias,
    down_weight,
    down_bias,
    ffn_gain,
    ffn_shift,
    cotangent,
):
    gathered = (
        lax.all_gather(query_weight, BOTH, axis=0, tiled=True),
        lax.all_gather(query_bias, BOTH, axis=0, tiled=True),
        lax.all_gather(key_weight, BOTH, axis=0, tiled=True),
        lax.all_gather(value_weight, BOTH, axis=0, tiled=True),
        lax.all_gather(value_bias, BOTH, axis=0, tiled=True),
        lax.all_gather(output_weight, BOTH, axis=0, tiled=True),
        lax.all_gather(output_bias, BOTH, axis=0, tiled=True),
        lax.all_gather(attn_gain, BOTH, axis=0, tiled=True),
        lax.all_gather(attn_shift, BOTH, axis=0, tiled=True),
        lax.all_gather(up_weight, BOTH, axis=0, tiled=True),
        lax.all_gather(up_bias, BOTH, axis=0, tiled=True),
        lax.all_gather(down_weight, BOTH, axis=0, tiled=True),
        lax.all_gather(down_bias, BOTH, axis=0, tiled=True),
        lax.all_gather(ffn_gain, BOTH, axis=0, tiled=True),
        lax.all_gather(ffn_shift, BOTH, axis=0, tiled=True),
    )
    (
        query_full,
        qbias_full,
        key_full,
        value_full,
        vbias_full,
        output_full,
        obias_full,
        again_full,
        ashift_full,
        up_full,
        ubias_full,
        down_full,
        dbias_full,
        fgain_full,
        fshift_full,
    ) = gathered
    seq_groups, stretch_len, width = tokens.shape
    row_count = seq_groups * stretch_len
    token_rows = tokens.reshape(row_count, width)
    positions = lax.axis_index(SEQ) * stretch_len + jnp.arange(stretch_len, dtype=jnp.int32)
    total_len = stretch_len * lax.axis_size(SEQ)
    query_seg = segment_ids(doc_lengths, positions)
    key_seg = segment_ids(doc_lengths, jnp.arange(total_len, dtype=jnp.int32))
    same_doc = query_seg[:, :, None] == key_seg[:, None, :]
    queries = (
        (matmul_plain(token_rows, query_full) + qbias_full)
        .astype(jnp.bfloat16)
        .reshape(tokens.shape)
    )
    keys_local = matmul_plain(token_rows, key_full).astype(jnp.bfloat16).reshape(tokens.shape)
    values_local = (
        (matmul_plain(token_rows, value_full) + vbias_full)
        .astype(jnp.bfloat16)
        .reshape(tokens.shape)
    )
    key_all, value_all = (
        lax.all_gather(keys_local, SEQ, axis=1, tiled=True),
        lax.all_gather(values_local, SEQ, axis=1, tiled=True),
    )
    context, log_sums = attend_forward(queries, key_all, value_all, same_doc)
    context_low = context.reshape(row_count, width).astype(jnp.bfloat16)
    res_one = token_rows.astype(jnp.float32) + matmul_plain(context_low, output_full) + obias_full
    normed, pull_one = jax.vjp(
        norm_apply, res_one, again_full.astype(jnp.float32), ashift_full.astype(jnp.float32)
    )
    normed_low = normed.astype(jnp.bfloat16)
    up_pre = matmul_plain(normed_low, up_full) + ubias_full
    activated, pull_gelu = jax.vjp(gelu_exact, up_pre)
    act_low = activated.astype(jnp.bfloat16)
    res_two = normed + matmul_plain(act_low, down_full) + dbias_full
    output_rows, pull_two = jax.vjp(
        norm_apply, res_two, fgain_full.astype(jnp.float32), fshift_full.astype(jnp.float32)
    )
    mixed = output_rows.astype(jnp.bfloat16).reshape(tokens.shape)
    regathered = (
        lax.all_gather(query_weight, BOTH, axis=0, tiled=True),
        lax.all_gather(query_bias, BOTH, axis=0, tiled=True),
        lax.all_gather(key_weight, BOTH, axis=0, tiled=True),
        lax.all_gather(value_weight, BOTH, axis=0, tiled=True),
        lax.all_gather(value_bias, BOTH, axis=0, tiled=True),
        lax.all_gather(output_weight, BOTH, axis=0, tiled=True),
        lax.all_gather(output_bias, BOTH, axis=0, tiled=True),
        lax.all_gather(attn_gain, BOTH, axis=0, tiled=True),
        lax.all_gather(attn_shift, BOTH, axis=0, tiled=True),
        lax.all_gather(up_weight, BOTH, axis=0, tiled=True),
        lax.all_gather(up_bias, BOTH, axis=0, tiled=True),
        lax.all_gather(down_weight, BOTH, axis=0, tiled=True),
        lax.all_gather(down_bias, BOTH, axis=0, tiled=True),
        lax.all_gather(ffn_gain, BOTH, axis=0, tiled=True),
        lax.all_gather(ffn_shift, BOTH, axis=0, tiled=True),
    )
    query_back = regathered[0]
    key_back = regathered[2]
    value_back = regathered[3]
    output_back = regathered[5]
    up_back = regathered[9]
    down_back = regathered[11]
    grad_out = cotangent.astype(jnp.float32).reshape(row_count, width)
    grad_res_two, grad_ffn_gain, grad_ffn_shift = pull_two(grad_out)
    grad_down_low = grad_res_two.astype(jnp.bfloat16)
    grad_down_weight = matmul_left_t(act_low, grad_down_low)
    grad_down_bias = column_sums(grad_down_low)
    (grad_up_pre,) = pull_gelu(matmul_right_t(grad_down_low, down_back))
    grad_up_low = grad_up_pre.astype(jnp.bfloat16)
    grad_up_weight = matmul_left_t(normed_low, grad_up_low)
    grad_up_bias = column_sums(grad_up_low)
    grad_normed = grad_res_two + matmul_right_t(grad_up_low, up_back)
    grad_res_one, grad_attn_gain, grad_attn_shift = pull_one(grad_normed)
    grad_branch_low = grad_res_one.astype(jnp.bfloat16)
    grad_output_weight = matmul_left_t(context_low, grad_branch_low)
    grad_output_bias = column_sums(grad_branch_low)
    grad_context = (
        matmul_right_t(grad_branch_low, output_back).astype(jnp.bfloat16).reshape(tokens.shape)
    )
    key_again, value_again = (
        lax.all_gather(keys_local, SEQ, axis=1, tiled=True),
        lax.all_gather(values_local, SEQ, axis=1, tiled=True),
    )
    grad_query, row_dots, unused_key, unused_value = attend_backward(
        queries, key_again, value_again, same_doc, log_sums, grad_context
    )
    query_all, grad_ctx_all = (
        lax.all_gather(queries, SEQ, axis=1, tiled=True),
        lax.all_gather(grad_context, SEQ, axis=1, tiled=True),
    )
    lse_all, rowdot_all = (
        lax.all_gather(log_sums, SEQ, axis=2, tiled=True),
        lax.all_gather(row_dots, SEQ, axis=2, tiled=True),
    )
    same_doc_t = key_seg[:, :, None] == query_seg[:, None, :]
    grad_key, grad_value = key_side_local(
        query_all, grad_ctx_all, lse_all, rowdot_all, keys_local, values_local, same_doc_t
    )
    grad_query_low = grad_query.reshape(row_count, width).astype(jnp.bfloat16)
    grad_key_low = grad_key.reshape(row_count, width).astype(jnp.bfloat16)
    grad_value_low = grad_value.reshape(row_count, width).astype(jnp.bfloat16)
    grad_query_weight = matmul_left_t(token_rows, grad_query_low)
    grad_query_bias = column_sums(grad_query_low)
    grad_key_weight = matmul_left_t(token_rows, grad_key_low)
    grad_value_weight = matmul_left_t(token_rows, grad_value_low)
    grad_value_bias = column_sums(grad_value_low)
    grad_tokens = (
        grad_res_one
        + matmul_right_t(grad_query_low, query_back)
        + matmul_right_t(grad_key_low, key_back)
        + matmul_right_t(grad_value_low, value_back)
    )
    summed = (
        lax.psum_scatter(grad_query_weight, BOTH, scatter_dimension=0, tiled=True),
        lax.psum_scatter(grad_query_bias, BOTH, scatter_dimension=0, tiled=True),
        lax.psum_scatter(grad_key_weight, BOTH, scatter_dimension=0, tiled=True),
        lax.psum_scatter(grad_value_weight, BOTH, scatter_dimension=0, tiled=True),
        lax.psum_scatter(grad_value_bias, BOTH, scatter_dimension=0, tiled=True),
        lax.psum_scatter(grad_output_weight, BOTH, scatter_dimension=0, tiled=True),
        lax.psum_scatter(grad_output_bias, BOTH, scatter_dimension=0, tiled=True),
        lax.psum_scatter(grad_attn_gain, BOTH, scatter_dimension=0, tiled=True),
        lax.psum_scatter(grad_attn_shift, BOTH, scatter_dimension=0, tiled=True),
        lax.psum_scatter(grad_up_weight, BOTH, scatter_dimension=0, tiled=True),
        lax.psum_scatter(grad_up_bias, BOTH, scatter_dimension=0, tiled=True),
        lax.psum_scatter(grad_down_weight, BOTH, scatter_dimension=0, tiled=True),
        lax.psum_scatter(grad_down_bias, BOTH, scatter_dimension=0, tiled=True),
        lax.psum_scatter(grad_ffn_gain, BOTH, scatter_dimension=0, tiled=True),
        lax.psum_scatter(grad_ffn_shift, BOTH, scatter_dimension=0, tiled=True),
    )
    return (
        mixed,
        grad_tokens.reshape(tokens.shape),
        summed[0],
        summed[1],
        summed[2],
        summed[3],
        summed[4],
        summed[5],
        summed[6],
        summed[7],
        summed[8],
        summed[9],
        summed[10],
        summed[11],
        summed[12],
        summed[13],
        summed[14],
    )


LOG2E = 1.4426950408889634
GROUP_HEADS = 3
GROUP_COLS = GROUP_HEADS * HEAD_DIM
PACK = 640
VECS = 12
SIDE = 16
KEY_CHUNK = 512


def dot_nt(left_op, right_op):
    return lax.dot_general(
        left_op, right_op, (((1,), (1,)), ((), ())), preferred_element_type=jnp.float32
    )


def dot_nn(left_op, right_op):
    return lax.dot_general(
        left_op, right_op, (((1,), (0,)), ((), ())), preferred_element_type=jnp.float32
    )


def attend_kernel(
    query_ref, own_ref, other_ref, seg_key_ref, seg_query_ref, ctx_ref, lse_ref, value_t
):
    half = own_ref.shape[0]
    rows = query_ref.shape[0]

    @pl.when(pl.program_id(0) == 0)
    def _():
        value_t[:, :half] = own_ref[:, GROUP_COLS : 2 * GROUP_COLS].T
        value_t[:, half:] = other_ref[:, GROUP_COLS : 2 * GROUP_COLS].T

    seg_query = seg_query_ref[...]
    chunks = [
        (ref, start) for ref in (own_ref, other_ref) for start in range(0, half, KEY_CHUNK)
    ]
    for head in range(GROUP_HEADS):
        cols = slice(head * HEAD_DIM, (head + 1) * HEAD_DIM)
        query = query_ref[:, cols]
        scores = []
        top = None
        for number, (ref, start) in enumerate(chunks):
            raw = dot_nt(ref[start : start + KEY_CHUNK, cols], query)
            seg_key = seg_key_ref[number * KEY_CHUNK : (number + 1) * KEY_CHUNK, :]
            seg_key = jnp.concatenate([seg_key] * (rows // 128), axis=1)
            masked = jnp.where(seg_key == seg_query, raw * (SCALE * LOG2E), NEG)
            scores.append(masked)
            peak = jnp.max(masked, axis=0, keepdims=True)
            top = peak if top is None else jnp.maximum(top, peak)
        total = None
        context_t = None
        for number in range(len(chunks)):
            weight = jnp.exp2(scores[number] - top)
            part = jnp.sum(weight, axis=0, keepdims=True)
            piece = dot_nn(
                value_t[cols, number * KEY_CHUNK : (number + 1) * KEY_CHUNK],
                weight.astype(jnp.bfloat16),
            )
            total = part if total is None else total + part
            context_t = piece if context_t is None else context_t + piece
        ctx_ref[:, cols] = (context_t / total).T
        lse_ref[head : head + 1, :] = top + jnp.log2(total)


def attend(query, own, other, seg_key, seg_query):
    rows = query.shape[0]
    half = own.shape[0]
    block = rows // 4
    return pl.pallas_call(
        attend_kernel,
        grid=(4,),
        in_specs=[
            pl.BlockSpec((block, GROUP_COLS), lambda i: (i, 0)),
            pl.BlockSpec((half, 2 * GROUP_COLS), lambda i: (0, 0)),
            pl.BlockSpec((half, 2 * GROUP_COLS), lambda i: (0, 0)),
            pl.BlockSpec((2 * half, 128), lambda i: (0, 0)),
            pl.BlockSpec((1, block), lambda i: (0, i)),
        ],
        out_specs=[
            pl.BlockSpec((block, GROUP_COLS), lambda i: (i, 0)),
            pl.BlockSpec((8, block), lambda i: (0, i)),
        ],
        out_shape=[
            jax.ShapeDtypeStruct((rows, GROUP_COLS), jnp.float32),
            jax.ShapeDtypeStruct((8, rows), jnp.float32),
        ],
        scratch_shapes=[pltpu.VMEM((GROUP_COLS, 2 * half), jnp.bfloat16)],
        compiler_params=pltpu.CompilerParams(vmem_limit_bytes=48 * 1024 * 1024),
        cost_estimate=pl.CostEstimate(
            flops=70 * rows * half * GROUP_COLS, bytes_accessed=1024 * 1024, transcendentals=0
        ),
        name="attend",
    )(query, own, other, seg_key, seg_query)


def attend_back_kernel(
    query_ref,
    grad_ref,
    ctx_ref,
    lse_ref,
    own_ref,
    other_ref,
    seg_key_ref,
    seg_query_ref,
    gquery_ref,
    gown_ref,
    gother_ref,
    key_t,
    gother_sum,
):
    half = own_ref.shape[0]
    rows = query_ref.shape[0]
    first = pl.program_id(0) == 0

    @pl.when(first)
    def _():
        key_t[:, :half] = own_ref[:, :GROUP_COLS].T
        key_t[:, half:] = other_ref[:, :GROUP_COLS].T
        gown_ref[...] = jnp.zeros_like(gown_ref)
        gother_sum[...] = jnp.zeros_like(gother_sum)

    seg_query = seg_query_ref[...]
    chunks = [
        (ref, gref, start)
        for ref, gref in ((own_ref, gown_ref), (other_ref, gother_sum))
        for start in range(0, half, KEY_CHUNK)
    ]
    for head in range(GROUP_HEADS):
        cols = slice(head * HEAD_DIM, (head + 1) * HEAD_DIM)
        vcols = slice(GROUP_COLS + head * HEAD_DIM, GROUP_COLS + (head + 1) * HEAD_DIM)
        query = query_ref[:, cols]
        grad = grad_ref[:, cols]
        lse = lse_ref[head : head + 1, :]
        dots = (grad.astype(jnp.float32) * ctx_ref[:, cols]).T
        row_dot = jnp.sum(dots, axis=0, keepdims=True)
        gquery_t = None
        for number, (ref, gref, start) in enumerate(chunks):
            spot = slice(start, start + KEY_CHUNK)
            raw = dot_nt(ref[spot, cols], query)
            seg_key = seg_key_ref[number * KEY_CHUNK : (number + 1) * KEY_CHUNK, :]
            seg_key = jnp.concatenate([seg_key] * (rows // 128), axis=1)
            masked = jnp.where(seg_key == seg_query, raw * (SCALE * LOG2E), NEG)
            probs = jnp.exp2(masked - lse)
            gprobs = dot_nt(ref[spot, vcols], grad)
            gscores = (probs * (gprobs - row_dot)).astype(jnp.bfloat16)
            gref[spot, vcols] += dot_nn(probs.astype(jnp.bfloat16), grad)
            gref[spot, cols] += dot_nn(gscores, query)
            piece = dot_nn(key_t[cols, number * KEY_CHUNK : (number + 1) * KEY_CHUNK], gscores)
            gquery_t = piece if gquery_t is None else gquery_t + piece
        gquery_ref[:, cols] = (SCALE * gquery_t).T.astype(jnp.bfloat16)

    @pl.when(pl.program_id(0) == pl.num_programs(0) - 1)
    def _():
        gother_ref[...] = gother_sum[...].astype(jnp.bfloat16)


def attend_back(query, grad, ctx, lse, own, other, seg_key, seg_query):
    rows = query.shape[0]
    half = own.shape[0]
    block = rows // 4
    return pl.pallas_call(
        attend_back_kernel,
        grid=(4,),
        in_specs=[
            pl.BlockSpec((block, GROUP_COLS), lambda i: (i, 0)),
            pl.BlockSpec((block, GROUP_COLS), lambda i: (i, 0)),
            pl.BlockSpec((block, GROUP_COLS), lambda i: (i, 0)),
            pl.BlockSpec((8, block), lambda i: (0, i)),
            pl.BlockSpec((half, 2 * GROUP_COLS), lambda i: (0, 0)),
            pl.BlockSpec((half, 2 * GROUP_COLS), lambda i: (0, 0)),
            pl.BlockSpec((2 * half, 128), lambda i: (0, 0)),
            pl.BlockSpec((1, block), lambda i: (0, i)),
        ],
        out_specs=[
            pl.BlockSpec((block, GROUP_COLS), lambda i: (i, 0)),
            pl.BlockSpec((half, 2 * GROUP_COLS), lambda i: (0, 0)),
            pl.BlockSpec((half, 2 * GROUP_COLS), lambda i: (0, 0)),
        ],
        out_shape=[
            jax.ShapeDtypeStruct((rows, GROUP_COLS), jnp.bfloat16),
            jax.ShapeDtypeStruct((half, 2 * GROUP_COLS), jnp.float32),
            jax.ShapeDtypeStruct((half, 2 * GROUP_COLS), jnp.bfloat16),
        ],
        scratch_shapes=[
            pltpu.VMEM((GROUP_COLS, 2 * half), jnp.bfloat16),
            pltpu.VMEM((half, 2 * GROUP_COLS), jnp.float32),
        ],
        compiler_params=pltpu.CompilerParams(vmem_limit_bytes=48 * 1024 * 1024),
        cost_estimate=pl.CostEstimate(
            flops=100 * rows * half * GROUP_COLS, bytes_accessed=1024 * 1024, transcendentals=0
        ),
        name="attend_back",
    )(query, grad, ctx, lse, own, other, seg_key, seg_query)


def prepare_kernel(
    tokens_ref,
    lengths_ref,
    key_ref,
    value_ref,
    query_ref,
    qbias_ref,
    vbias_ref,
    obias_ref,
    again_ref,
    ashift_ref,
    dbias_ref,
    fgain_ref,
    fshift_ref,
    ubias_ref,
    output_ref,
    up_ref,
    down_ref,
    first_ref,
    second_ref,
    bulk_ref,
    *piece_refs,
):
    place = lax.axis_index(SEQ)
    odd = lax.rem(place // 4, 2) == 1
    quad = lax.rem(place, 4)
    first_ref[...] = jnp.where(odd, tokens_ref[1], tokens_ref[0])
    second_ref[...] = jnp.where(odd, tokens_ref[0], tokens_ref[1])
    own_rows, width = key_ref.shape
    ratio = up_ref.shape[1] // width
    bulk_ref[0, :own_rows] = output_ref[...]
    for number in range(ratio):
        bulk_ref[0, (1 + number) * own_rows : (2 + number) * own_rows] = up_ref[
            :, number * width : (number + 1) * width
        ]
    bulk_ref[0, (1 + ratio) * own_rows :] = down_ref[...]
    small = (qbias_ref, vbias_ref, obias_ref, again_ref, ashift_ref, dbias_ref, fgain_ref, fshift_ref)
    rows = [ref[...].astype(jnp.float32) for ref in small]
    wide = ubias_ref[...].astype(jnp.float32)
    rows += [wide[:, n * own_rows : (n + 1) * own_rows] for n in range(VECS - len(small))]
    lengths = lengths_ref[...]
    docs = lengths.shape[1]
    flat = jnp.concatenate(
        [lengths[0:1], lengths[1:2], jnp.zeros((1, own_rows - 2 * docs), jnp.int32)], axis=1
    )
    rows += [(flat >> 6).astype(jnp.float32), (flat & 63).astype(jnp.float32)]
    rows += [jnp.zeros_like(rows[0])] * (SIDE - len(rows))
    side = jnp.concatenate(rows, axis=0).T.astype(jnp.bfloat16)
    cut = 3 * GROUP_COLS
    for flip, piece_ref in enumerate(piece_refs):
        piece_ref[...] = jnp.zeros_like(piece_ref)
        piece_ref[:, cut : cut + SIDE] = side
        target = quad ^ flip
        for number in range(4):

            @pl.when(target == number)
            def _():
                cols = slice(number * GROUP_COLS, (number + 1) * GROUP_COLS)
                for spot, ref in enumerate((key_ref, value_ref, query_ref)):
                    piece_ref[:, spot * GROUP_COLS : (spot + 1) * GROUP_COLS] = ref[:, cols]


def prepare(tokens, lengths, key, value, query, vectors, up_bias, output, up, down):
    own_rows, width = key.shape
    bulk_rows = own_rows + down.shape[0] * 2
    turn_shape = jax.ShapeDtypeStruct(tokens.shape[1:], jnp.bfloat16)
    piece_shape = jax.ShapeDtypeStruct((own_rows, PACK), jnp.bfloat16)
    return pl.pallas_call(
        prepare_kernel,
        out_shape=[turn_shape] * 2
        + [jax.ShapeDtypeStruct((1, bulk_rows, width), jnp.bfloat16)]
        + [piece_shape] * 4,
        name="prepare",
    )(
        tokens,
        lengths,
        key,
        value,
        query,
        *[item.reshape(1, own_rows) for item in vectors],
        up_bias.reshape(1, up_bias.shape[0]),
        output,
        up,
        down,
    )


def tied(values, *others):
    return lax.optimization_barrier((values, others))[0]


def block_of(values, index, axis):
    return lax.dynamic_index_in_dim(values, index, axis=axis, keepdims=False)


def halves(values, bit, axis):
    return (block_of(values, bit, axis), block_of(values, 1 - bit, axis))


def low_sum(own, arrived):
    return (own.astype(jnp.float32) + arrived.astype(jnp.float32)).astype(jnp.bfloat16)


def sum_parts(own, arrived):
    total = own.astype(jnp.float32)
    for item in arrived:
        total = total + item.astype(jnp.float32)
    return total


def device_table(mapping):
    pairs = []
    for core in range(2):
        for layer_z in range(4):
            for quad in range(4):
                to_core, to_z, to_quad = mapping(core, layer_z, quad)
                pairs.append((core * 16 + layer_z * 4 + quad, to_core * 16 + to_z * 4 + to_quad))
    return pairs


def hop(value, mapping):
    return lax.ppermute(value, BOTH, device_table(mapping))


def hop_quad(value, flip):
    return hop(value, lambda core, layer_z, quad: (core, layer_z, quad ^ flip))


def hop_layer(value, flip):
    return hop(value, lambda core, layer_z, quad: (core, layer_z ^ flip, quad))


def hop_core(value):
    return hop(value, lambda core, layer_z, quad: (1 - core, layer_z, quad))


def to_sequence(value, turn):
    return hop(
        value,
        lambda core, layer_z, quad: (layer_z // 2, 2 * core + (layer_z + turn) % 2, quad),
    )


def to_owner(value, turn):
    return hop(
        value,
        lambda core, layer_z, quad: (layer_z // 2, 2 * core + (layer_z - turn) % 2, quad),
    )


def turned(blocks, quad):
    first, second, third, fourth = blocks
    odd = quad % 2 == 1
    high = quad // 2 == 1
    pairs = (
        jnp.where(odd, second, first),
        jnp.where(odd, first, second),
        jnp.where(odd, fourth, third),
        jnp.where(odd, third, fourth),
    )
    return (
        jnp.where(high, pairs[2], pairs[0]),
        jnp.where(high, pairs[3], pairs[1]),
        jnp.where(high, pairs[0], pairs[2]),
        jnp.where(high, pairs[1], pairs[3]),
    )


def pack_grads(main, vecs):
    coarse = vecs.astype(jnp.bfloat16)
    fine = (vecs - coarse.astype(jnp.float32)).astype(jnp.bfloat16)
    filler = jnp.zeros(main.shape[:-1] + (PACK - main.shape[-1] - 2 * VECS,), jnp.bfloat16)
    return jnp.concatenate([main.astype(jnp.bfloat16), coarse, fine, filler], axis=-1)


def unpack_grads(packed):
    wide = packed.astype(jnp.float32)
    cut = 3 * GROUP_COLS
    return (wide[..., :cut], wide[..., cut : cut + VECS] + wide[..., cut + VECS : cut + 2 * VECS])


def add_packed(own, arrived):
    main, vecs = unpack_grads(own)
    more, more_vecs = unpack_grads(arrived)
    return (main + more, vecs + more_vecs)


def shards_heads(
    tokens,
    doc_lengths,
    query_weight,
    query_bias,
    key_weight,
    value_weight,
    value_bias,
    output_weight,
    output_bias,
    attn_gain,
    attn_shift,
    up_weight,
    up_bias,
    down_weight,
    down_bias,
    ffn_gain,
    ffn_shift,
    cotangent,
):
    groups, stretch, width = tokens.shape
    own_rows = query_weight.shape[0]
    hidden = up_weight.shape[1]
    ratio = hidden // width
    devices = width // own_rows
    bulk_rows = own_rows * (1 + 2 * ratio)
    row_count = groups * stretch
    core = lax.axis_index(BATCH)
    place = lax.axis_index(SEQ)
    layer_z = place // 4
    quad = place % 4
    parity = layer_z % 2
    flips = (1, 2, 3)
    bit_x, bit_y = (quad % 2, quad // 2)
    bit_low, bit_high = (layer_z % 2, layer_z // 2)

    vectors = (
        query_bias,
        value_bias,
        output_bias,
        attn_gain,
        attn_shift,
        down_bias,
        ffn_gain,
        ffn_shift,
    )
    first_turn, second_turn, bulk, *pieces = prepare(
        tokens,
        doc_lengths,
        key_weight,
        value_weight,
        query_weight,
        vectors,
        up_bias,
        output_weight,
        up_weight,
        down_weight,
    )

    own_block = jnp.concatenate(
        [to_sequence(first_turn, 0), to_sequence(second_turn, 1)], axis=0
    )
    token_half = jnp.concatenate(
        [own_block] + [hop_quad(own_block, flip) for flip in flips], axis=0
    )

    quads = turned([pieces[0]] + [hop_quad(pieces[flip], flip) for flip in flips], quad)
    quads = jnp.stack(quads, axis=0)
    layers = [quads] + [hop_layer(quads, flip) for flip in flips]
    layers = jnp.stack(turned(layers, layer_z), axis=0)
    twin = hop_core(layers)
    cores = jnp.stack([jnp.where(core == 0, layers, twin), jnp.where(core == 0, twin, layers)])
    packed = cores.reshape(width, PACK)
    group_weight = packed[:, : 3 * GROUP_COLS]
    side = packed[:, 3 * GROUP_COLS : 3 * GROUP_COLS + SIDE].astype(jnp.float32)
    vector_rows = side[:, :8].T
    up_bias_full = side[:, 8:VECS].reshape(devices, own_rows, ratio)
    up_bias_full = jnp.swapaxes(up_bias_full, 1, 2).reshape(1, hidden)
    (
        qbias_full,
        vbias_full,
        obias_full,
        again_full,
        ashift_full,
        dbias_full,
        fgain_full,
        fshift_full,
    ) = [vector_rows[number] for number in range(8)]
    docs = doc_lengths.shape[1]
    digits = side.reshape(2, width // 2, SIDE)[:, : groups * docs, VECS : VECS + 2]
    lengths_all = (digits[..., 0] * 64 + digits[..., 1]).astype(jnp.int32)
    lengths = lax.dynamic_index_in_dim(
        lengths_all.reshape(2 * groups, docs), layer_z, axis=0, keepdims=False
    )
    doc_ends = jnp.cumsum(lengths)

    def half_segments(which):
        turn_z = jnp.stack([(layer_z - turn) % 2 for turn in (0, 1)]) + 2 * which
        spot = jnp.stack([quad ^ flip for flip in range(4)])
        start = turn_z[None, :] * (4 * stretch) + spot[:, None] * stretch
        positions = start[:, :, None] + jnp.arange(stretch, dtype=jnp.int32)
        positions = positions.reshape(-1)
        return jnp.sum((positions[:, None] >= doc_ends[None, :]).astype(jnp.int32), axis=-1)

    seg_query = half_segments(core)
    seg_key = jnp.concatenate([seg_query, half_segments(1 - core)])
    seg_key = jnp.broadcast_to(seg_key[:, None], (seg_key.shape[0], 128))
    seg_query = seg_query[None, :]

    bulk_all = lax.all_gather(bulk, BOTH, axis=0, tiled=True)

    column_bias = jnp.concatenate(
        [
            jnp.zeros((GROUP_COLS,), jnp.float32),
            lax.dynamic_slice_in_dim(vbias_full, quad * GROUP_COLS, GROUP_COLS),
            lax.dynamic_slice_in_dim(qbias_full, quad * GROUP_COLS, GROUP_COLS),
        ]
    )
    projected = (matmul_plain(token_half, group_weight) + column_bias).astype(jnp.bfloat16)
    own_pair = projected[:, : 2 * GROUP_COLS]
    queries = projected[:, 2 * GROUP_COLS :]
    other_pair = hop_core(own_pair)
    ctx_wide, lse = attend(queries, own_pair, other_pair, seg_key, seg_query)

    ctx_blocks = ctx_wide.astype(jnp.bfloat16).reshape(4, row_count, GROUP_COLS)
    ctx_groups = [ctx_blocks[0]] + [hop_quad(ctx_blocks[flip], flip) for flip in flips]
    ctx_merged = jnp.concatenate(turned(ctx_groups, quad), axis=1)
    ctx_turns = [
        to_owner(ctx_merged[turn * stretch : (turn + 1) * stretch], turn) for turn in (0, 1)
    ]
    context_low = jnp.concatenate(
        [
            jnp.where(parity == 0, ctx_turns[0], ctx_turns[1]),
            jnp.where(parity == 0, ctx_turns[1], ctx_turns[0]),
        ],
        axis=0,
    )

    output_full = bulk_all[:, :own_rows].reshape(width, width)
    up_parts = [
        bulk_all[:, (1 + number) * own_rows : (2 + number) * own_rows].reshape(width, width)
        for number in range(ratio)
    ]
    up_full = jnp.concatenate(up_parts, axis=1)
    down_full = bulk_all[:, (1 + ratio) * own_rows :].reshape(hidden, width)

    token_rows = tokens.reshape(row_count, width)
    res_one = token_rows.astype(jnp.float32) + matmul_plain(context_low, output_full) + obias_full
    normed, pull_one = jax.vjp(norm_apply, res_one, again_full, ashift_full)
    normed_low = normed.astype(jnp.bfloat16)
    up_pre = matmul_plain(normed_low, up_full) + up_bias_full
    activated, pull_gelu = jax.vjp(gelu_exact, up_pre)
    act_low = activated.astype(jnp.bfloat16)
    res_two = normed + matmul_plain(act_low, down_full) + dbias_full
    output_rows, pull_two = jax.vjp(norm_apply, res_two, fgain_full, fshift_full)
    mixed = output_rows.astype(jnp.bfloat16).reshape(tokens.shape)
    grad_out = cotangent.astype(jnp.float32).reshape(row_count, width)
    grad_res_two, grad_ffn_gain, grad_ffn_shift = pull_two(grad_out)
    grad_down_low = grad_res_two.astype(jnp.bfloat16)

    def half_columns(matrix, which):
        half = matrix.shape[1] // 2
        return lax.dynamic_slice_in_dim(matrix, which * half, half, axis=1)

    def down_term(which):
        return matmul_left_t(half_columns(act_low, which), grad_down_low)

    def branch_term(which):
        return jnp.concatenate(
            [
                matmul_left_t(half_columns(normed_low, which), grad_up_low),
                matmul_left_t(half_columns(context_low, which), grad_branch_low),
            ],
            axis=1,
        )

    down_theirs = down_term(1 - core).astype(jnp.bfloat16)
    down_arrived = hop_core(down_theirs)
    (grad_up_pre,) = pull_gelu(matmul_right_t(tied(grad_down_low, down_theirs), down_full))
    grad_up_low = grad_up_pre.astype(jnp.bfloat16)
    grad_normed = grad_res_two + matmul_right_t(grad_up_low, up_full)
    grad_res_one, grad_attn_gain, grad_attn_shift = pull_one(grad_normed)
    grad_branch_low = grad_res_one.astype(jnp.bfloat16)
    grad_context = matmul_right_t(grad_branch_low, output_full).astype(jnp.bfloat16)
    branch_arrived = hop_core(branch_term(1 - core).astype(jnp.bfloat16))

    low_part = grad_context[:stretch]
    high_part = grad_context[stretch:]
    grad_turns = [
        to_sequence(jnp.where((parity + turn) % 2 == 1, high_part, low_part), turn)
        for turn in (0, 1)
    ]
    down_total = (down_term(core) + down_arrived.astype(jnp.float32)).astype(jnp.bfloat16)
    down_total = down_total.reshape(2, 2, 2, 2, ratio * own_rows, width)
    branch_total = (branch_term(core) + branch_arrived.astype(jnp.float32)).astype(jnp.bfloat16)
    branch_total = branch_total.reshape(2, 2, 2, 2, own_rows, hidden + width)
    grad_turns = tied(grad_turns, down_total, branch_total)
    grad_own = jnp.concatenate(grad_turns, axis=0)
    grad_columns = turned(
        [grad_own[:, n * GROUP_COLS : (n + 1) * GROUP_COLS] for n in range(4)], quad
    )
    grad_ctx = jnp.concatenate(
        [grad_columns[0]] + [hop_quad(grad_columns[flip], flip) for flip in flips], axis=0
    )

    down_own, down_send = tied(halves(down_total, bit_x, 3), grad_ctx)
    branch_own, branch_send = tied(halves(branch_total, bit_y, 2), grad_ctx)
    down_arrived = hop_quad(down_send, 1)
    branch_arrived = hop_quad(branch_send, 2)

    grad_query, grad_own_pair, grad_other_pair = attend_back(
        tied(queries, down_send, branch_send),
        grad_ctx,
        ctx_wide,
        lse,
        own_pair,
        other_pair,
        seg_key,
        seg_query,
    )
    pair_arrived = hop_core(grad_other_pair)
    down_arrived, branch_arrived = tied((down_arrived, branch_arrived), grad_other_pair)
    down_own, down_send = halves(low_sum(down_own, down_arrived), bit_y, 2)
    branch_own, branch_send = halves(low_sum(branch_own, branch_arrived), bit_x, 2)
    down_arrived = hop_quad(down_send, 2)
    branch_arrived = hop_quad(branch_send, 1)
    pair_total = grad_own_pair + tied(pair_arrived, down_send, branch_send).astype(jnp.float32)
    pair_scale = jnp.where(jnp.arange(2 * GROUP_COLS) < GROUP_COLS, SCALE, 1.0)
    grad_projected = jnp.concatenate(
        [(pair_total * pair_scale).astype(jnp.bfloat16), grad_query], axis=1
    )
    grad_half = matmul_right_t(grad_projected, group_weight)
    half_blocks = grad_half.reshape(4, row_count, width)
    low_blocks = half_blocks.astype(jnp.bfloat16)
    low_blocks, down_arrived, branch_arrived = tied((low_blocks, down_arrived, branch_arrived))
    token_arrived = [hop_quad(low_blocks[flip], flip) for flip in flips]
    down_own, down_send = halves(low_sum(down_own, down_arrived), bit_low, 1)
    branch_own, branch_send = halves(low_sum(branch_own, branch_arrived), bit_low, 1)
    down_arrived = hop_layer(down_send, 1)
    up_sums, out_sums, down_sums, again_sums, ashift_sums, fgain_sums, fshift_sums = tied(
        (
            column_sums(grad_up_low),
            column_sums(grad_branch_low),
            column_sums(grad_down_low),
            grad_attn_gain,
            grad_attn_shift,
            grad_ffn_gain,
            grad_ffn_shift,
        ),
        low_blocks,
    )

    grad_group = matmul_left_t(token_half, grad_projected)
    bias_sums = column_sums(grad_projected)
    nothing = jnp.zeros((width,), jnp.float32)
    vec_rows = jnp.stack(
        [
            lax.dynamic_update_slice_in_dim(
                nothing, bias_sums[2 * GROUP_COLS :], quad * GROUP_COLS, 0
            ),
            lax.dynamic_update_slice_in_dim(
                nothing, bias_sums[GROUP_COLS : 2 * GROUP_COLS], quad * GROUP_COLS, 0
            ),
            out_sums,
            again_sums,
            ashift_sums,
            down_sums,
            fgain_sums,
            fshift_sums,
        ],
        axis=0,
    ).T
    up_sums = up_sums.reshape(devices, ratio, own_rows)
    up_sums = jnp.swapaxes(up_sums, 1, 2).reshape(width, ratio)
    vecs = jnp.concatenate([vec_rows, up_sums], axis=1)
    packed_grads = pack_grads(grad_group, vecs).reshape(2, width // 2, PACK)
    mine = jnp.where(core == 0, packed_grads[0], packed_grads[1])
    theirs = jnp.where(core == 0, packed_grads[1], packed_grads[0])
    pack_arrived = hop_core(theirs)
    packed_grads = pack_grads(*add_packed(mine, pack_arrived))
    branch_arrived = hop_layer(tied(branch_send, pack_arrived), 1)
    packed_grads = packed_grads.reshape(2, 2, 4 * own_rows, PACK)
    pack_own, pack_send = halves(packed_grads, bit_low, 1)
    pack_arrived = hop_layer(pack_send, 1)

    down_own, down_send = halves(low_sum(down_own, down_arrived), bit_high, 0)
    down_arrived = hop_layer(down_send, 2)
    token_arrived = tied(token_arrived, down_send, pack_send)
    grad_block = sum_parts(half_blocks[0], token_arrived).astype(jnp.bfloat16)
    home = [
        to_owner(grad_block[turn * stretch : (turn + 1) * stretch], turn) for turn in (0, 1)
    ]
    pack_arrived, branch_arrived, down_arrived = tied(
        (pack_arrived, branch_arrived, down_arrived), grad_block
    )
    packed_grads = pack_grads(*add_packed(pack_own, pack_arrived))
    pack_own, pack_send = halves(packed_grads, bit_high, 0)
    pack_arrived = hop_layer(pack_send, 2)
    branch_own, branch_send = halves(low_sum(branch_own, branch_arrived), bit_high, 0)
    branch_arrived = hop_layer(branch_send, 2)
    home, pack_arrived = tied((home, pack_arrived), branch_send)
    packed_grads = pack_grads(*add_packed(pack_own, pack_arrived)).reshape(4, own_rows, PACK)
    by_quad = turned([packed_grads[number] for number in range(4)], quad)
    main, vecs = unpack_grads(by_quad[0])
    home_rows = jnp.concatenate(
        [
            jnp.where(parity == 0, home[0], home[1]),
            jnp.where(parity == 0, home[1], home[0]),
        ],
        axis=0,
    )
    grad_tokens = (grad_res_one + home_rows.astype(jnp.float32)).reshape(tokens.shape)

    quad_parts = [main]
    for flip in flips:
        more, more_vecs = unpack_grads(hop_quad(by_quad[flip], flip))
        quad_parts.append(more)
        vecs = vecs + more_vecs
    quad_parts = turned(quad_parts, quad)
    sum_key, sum_value, sum_query = [
        jnp.concatenate(
            [part[:, n * GROUP_COLS : (n + 1) * GROUP_COLS] for part in quad_parts], axis=1
        )
        for n in range(3)
    ]
    sum_rows = vecs[:, :8].T
    sum_down = sum_parts(down_own, [down_arrived])
    sum_branch = sum_parts(branch_own, [branch_arrived])
    sum_up = sum_branch[:, :hidden]
    sum_output = sum_branch[:, hidden:]
    return (
        mixed,
        grad_tokens,
        sum_query,
        sum_rows[0],
        sum_key,
        sum_value,
        sum_rows[1],
        sum_output,
        sum_rows[2],
        sum_rows[3],
        sum_rows[4],
        sum_up,
        vecs[:, 8:].T.reshape(up_bias.shape),
        sum_down,
        sum_rows[5],
        sum_rows[6],
        sum_rows[7],
    )


def solution(mesh):
    in_specs = (
        P(BATCH, SEQ, None),
        P(BATCH, None),
        P(BOTH, None),
        P(BOTH),
        P(BOTH, None),
        P(BOTH, None),
        P(BOTH),
        P(BOTH, None),
        P(BOTH),
        P(BOTH),
        P(BOTH),
        P(BOTH, None),
        P(BOTH),
        P(BOTH, None),
        P(BOTH),
        P(BOTH),
        P(BOTH),
        P(BATCH, SEQ, None),
    )
    out_specs = (
        P(BATCH, SEQ, None),
        P(BATCH, SEQ, None),
        P(BOTH, None),
        P(BOTH),
        P(BOTH, None),
        P(BOTH, None),
        P(BOTH),
        P(BOTH, None),
        P(BOTH),
        P(BOTH),
        P(BOTH),
        P(BOTH, None),
        P(BOTH),
        P(BOTH, None),
        P(BOTH),
        P(BOTH),
        P(BOTH),
    )
    fits = mesh.shape[BATCH] == 2 and mesh.shape[SEQ] == 16
    body = shards_heads if fits else shards_general
    return jax.shard_map(body, mesh=mesh, in_specs=in_specs, out_specs=out_specs, check_vma=False)
```

```python
import jax
import jax.numpy as jnp
from jax import lax
from jax.experimental import pallas as pl
from jax.experimental.pallas import tpu as pltpu
from jax.sharding import PartitionSpec as P

BATCH = "batch"
SEQ = "seq"
BOTH = (BATCH, SEQ)
HEADS = 12
HEAD_DIM = 64


SCALE = 0.125
NEG = -1e30
EPS = 1e-12


def norm_apply(hidden, gain_vec, shift_vec):
    center = jnp.mean(hidden, axis=-1, keepdims=True)
    centered = hidden - center
    spread = jnp.mean(centered * centered, axis=-1, keepdims=True)
    return centered * lax.rsqrt(spread + EPS) * gain_vec + shift_vec


def gelu_exact(inputs):
    return jax.nn.gelu(inputs, approximate=False)


def segment_ids(doc_lengths, positions):
    doc_ends = jnp.cumsum(doc_lengths, axis=-1)
    return jnp.sum((positions[None, :, None] >= doc_ends[:, None, :]).astype(jnp.int32), axis=-1)


def matmul_plain(left_op, right_op):
    return jnp.dot(left_op, right_op, preferred_element_type=jnp.float32)


def matmul_right_t(left_op, right_op):
    return lax.dot_general(
        left_op, right_op, (((1,), (1,)), ((), ())), preferred_element_type=jnp.float32
    )


def matmul_left_t(left_op, right_op):
    return lax.dot_general(
        left_op, right_op, (((0,), (0,)), ((), ())), preferred_element_type=jnp.float32
    )


def column_sums(matrix):
    return jnp.sum(matrix.astype(jnp.float32), axis=0)


def head_block(matrix, head_pair):
    pair_width = 2 * HEAD_DIM
    column_block = matrix[..., head_pair * pair_width : (head_pair + 1) * pair_width]
    return column_block.reshape(column_block.shape[:-1] + (2, HEAD_DIM))


def merge_heads(blocks):
    return jnp.concatenate(
        [block_item.reshape(block_item.shape[:2] + (2 * HEAD_DIM,)) for block_item in blocks],
        axis=-1,
    )


def stat_pair(stats, head_pair):
    return stats[:, 2 * head_pair : 2 * head_pair + 2][..., None]


def pair_scores(query_pair, key_pair, same_doc):
    raw_scores = jnp.einsum(
        "sqhd,skhd->shqk", query_pair, key_pair, preferred_element_type=jnp.float32
    )
    return jnp.where(same_doc[:, None], SCALE * raw_scores, NEG)


def attend_forward(queries, key_all, value_all, same_doc):
    outputs, log_sums = ([], [])
    for head_pair in range(HEADS // 2):
        scores = pair_scores(
            head_block(queries, head_pair), head_block(key_all, head_pair), same_doc
        )
        top_score = jnp.max(scores, axis=-1, keepdims=True)
        exponent = jnp.exp(scores - top_score)
        totals = jnp.sum(exponent, axis=-1, keepdims=True)
        probs_low = (exponent / totals).astype(jnp.bfloat16)
        context = jnp.einsum(
            "shqk,skhd->sqhd",
            probs_low,
            head_block(value_all, head_pair),
            preferred_element_type=jnp.float32,
        )
        outputs.append(context)
        log_sums.append((top_score + jnp.log(totals))[..., 0])
    return (merge_heads(outputs), jnp.concatenate(log_sums, axis=1))


def attend_backward(queries, key_all, value_all, same_doc, log_sums, grad_context):
    query_grads, key_grads, value_grads, row_dots = ([], [], [], [])
    for head_pair in range(HEADS // 2):
        query_pair = head_block(queries, head_pair)
        key_pair = head_block(key_all, head_pair)
        grad_pair = head_block(grad_context, head_pair)
        probs = jnp.exp(
            pair_scores(query_pair, key_pair, same_doc) - stat_pair(log_sums, head_pair)
        )
        grad_probs = jnp.einsum(
            "sqhd,skhd->shqk",
            grad_pair,
            head_block(value_all, head_pair),
            preferred_element_type=jnp.float32,
        )
        row_dot = jnp.sum(probs * grad_probs, axis=-1, keepdims=True)
        row_dots.append(row_dot[..., 0])
        grad_scores = (probs * (grad_probs - row_dot)).astype(jnp.bfloat16) * jnp.bfloat16(SCALE)
        query_grads.append(
            jnp.einsum("shqk,skhd->sqhd", grad_scores, key_pair, preferred_element_type=jnp.float32)
        )
    return (merge_heads(query_grads), jnp.concatenate(row_dots, axis=1), None, None)


def key_side_local(query_all, grad_ctx_all, lse_all, rowdot_all, keys_own, values_own, same_doc_t):
    key_grads, value_grads = ([], [])
    for head_pair in range(HEADS // 2):
        query_pair = head_block(query_all, head_pair)
        grad_pair = head_block(grad_ctx_all, head_pair)
        probs = jnp.exp(
            pair_scores(query_pair, head_block(keys_own, head_pair), same_doc_t)
            - stat_pair(lse_all, head_pair)
        )
        grad_probs = jnp.einsum(
            "sqhd,skhd->shqk",
            grad_pair,
            head_block(values_own, head_pair),
            preferred_element_type=jnp.float32,
        )
        grad_scores = (probs * (grad_probs - stat_pair(rowdot_all, head_pair))).astype(
            jnp.bfloat16
        ) * jnp.bfloat16(SCALE)
        key_grads.append(
            jnp.einsum(
                "shqk,sqhd->skhd", grad_scores, query_pair, preferred_element_type=jnp.float32
            )
        )
        value_grads.append(
            jnp.einsum(
                "shqk,sqhd->skhd",
                probs.astype(jnp.bfloat16),
                grad_pair,
                preferred_element_type=jnp.float32,
            )
        )
    return (merge_heads(key_grads), merge_heads(value_grads))


def shards_general(
    tokens,
    doc_lengths,
    query_weight,
    query_bias,
    key_weight,
    value_weight,
    value_bias,
    output_weight,
    output_bias,
    attn_gain,
    attn_shift,
    up_weight,
    up_bias,
    down_weight,
    down_bias,
    ffn_gain,
    ffn_shift,
    cotangent,
):
    gathered = (
        lax.all_gather(query_weight, BOTH, axis=0, tiled=True),
        lax.all_gather(query_bias, BOTH, axis=0, tiled=True),
        lax.all_gather(key_weight, BOTH, axis=0, tiled=True),
        lax.all_gather(value_weight, BOTH, axis=0, tiled=True),
        lax.all_gather(value_bias, BOTH, axis=0, tiled=True),
        lax.all_gather(output_weight, BOTH, axis=0, tiled=True),
        lax.all_gather(output_bias, BOTH, axis=0, tiled=True),
        lax.all_gather(attn_gain, BOTH, axis=0, tiled=True),
        lax.all_gather(attn_shift, BOTH, axis=0, tiled=True),
        lax.all_gather(up_weight, BOTH, axis=0, tiled=True),
        lax.all_gather(up_bias, BOTH, axis=0, tiled=True),
        lax.all_gather(down_weight, BOTH, axis=0, tiled=True),
        lax.all_gather(down_bias, BOTH, axis=0, tiled=True),
        lax.all_gather(ffn_gain, BOTH, axis=0, tiled=True),
        lax.all_gather(ffn_shift, BOTH, axis=0, tiled=True),
    )
    (
        query_full,
        qbias_full,
        key_full,
        value_full,
        vbias_full,
        output_full,
        obias_full,
        again_full,
        ashift_full,
        up_full,
        ubias_full,
        down_full,
        dbias_full,
        fgain_full,
        fshift_full,
    ) = gathered
    seq_groups, stretch_len, width = tokens.shape
    row_count = seq_groups * stretch_len
    token_rows = tokens.reshape(row_count, width)
    positions = lax.axis_index(SEQ) * stretch_len + jnp.arange(stretch_len, dtype=jnp.int32)
    total_len = stretch_len * lax.axis_size(SEQ)
    query_seg = segment_ids(doc_lengths, positions)
    key_seg = segment_ids(doc_lengths, jnp.arange(total_len, dtype=jnp.int32))
    same_doc = query_seg[:, :, None] == key_seg[:, None, :]
    queries = (
        (matmul_plain(token_rows, query_full) + qbias_full)
        .astype(jnp.bfloat16)
        .reshape(tokens.shape)
    )
    keys_local = matmul_plain(token_rows, key_full).astype(jnp.bfloat16).reshape(tokens.shape)
    values_local = (
        (matmul_plain(token_rows, value_full) + vbias_full)
        .astype(jnp.bfloat16)
        .reshape(tokens.shape)
    )
    key_all, value_all = (
        lax.all_gather(keys_local, SEQ, axis=1, tiled=True),
        lax.all_gather(values_local, SEQ, axis=1, tiled=True),
    )
    context, log_sums = attend_forward(queries, key_all, value_all, same_doc)
    context_low = context.reshape(row_count, width).astype(jnp.bfloat16)
    res_one = token_rows.astype(jnp.float32) + matmul_plain(context_low, output_full) + obias_full
    normed, pull_one = jax.vjp(
        norm_apply, res_one, again_full.astype(jnp.float32), ashift_full.astype(jnp.float32)
    )
    normed_low = normed.astype(jnp.bfloat16)
    up_pre = matmul_plain(normed_low, up_full) + ubias_full
    activated, pull_gelu = jax.vjp(gelu_exact, up_pre)
    act_low = activated.astype(jnp.bfloat16)
    res_two = normed + matmul_plain(act_low, down_full) + dbias_full
    output_rows, pull_two = jax.vjp(
        norm_apply, res_two, fgain_full.astype(jnp.float32), fshift_full.astype(jnp.float32)
    )
    mixed = output_rows.astype(jnp.bfloat16).reshape(tokens.shape)
    regathered = (
        lax.all_gather(query_weight, BOTH, axis=0, tiled=True),
        lax.all_gather(query_bias, BOTH, axis=0, tiled=True),
        lax.all_gather(key_weight, BOTH, axis=0, tiled=True),
        lax.all_gather(value_weight, BOTH, axis=0, tiled=True),
        lax.all_gather(value_bias, BOTH, axis=0, tiled=True),
        lax.all_gather(output_weight, BOTH, axis=0, tiled=True),
        lax.all_gather(output_bias, BOTH, axis=0, tiled=True),
        lax.all_gather(attn_gain, BOTH, axis=0, tiled=True),
        lax.all_gather(attn_shift, BOTH, axis=0, tiled=True),
        lax.all_gather(up_weight, BOTH, axis=0, tiled=True),
        lax.all_gather(up_bias, BOTH, axis=0, tiled=True),
        lax.all_gather(down_weight, BOTH, axis=0, tiled=True),
        lax.all_gather(down_bias, BOTH, axis=0, tiled=True),
        lax.all_gather(ffn_gain, BOTH, axis=0, tiled=True),
        lax.all_gather(ffn_shift, BOTH, axis=0, tiled=True),
    )
    query_back = regathered[0]
    key_back = regathered[2]
    value_back = regathered[3]
    output_back = regathered[5]
    up_back = regathered[9]
    down_back = regathered[11]
    grad_out = cotangent.astype(jnp.float32).reshape(row_count, width)
    grad_res_two, grad_ffn_gain, grad_ffn_shift = pull_two(grad_out)
    grad_down_low = grad_res_two.astype(jnp.bfloat16)
    grad_down_weight = matmul_left_t(act_low, grad_down_low)
    grad_down_bias = column_sums(grad_down_low)
    (grad_up_pre,) = pull_gelu(matmul_right_t(grad_down_low, down_back))
    grad_up_low = grad_up_pre.astype(jnp.bfloat16)
    grad_up_weight = matmul_left_t(normed_low, grad_up_low)
    grad_up_bias = column_sums(grad_up_low)
    grad_normed = grad_res_two + matmul_right_t(grad_up_low, up_back)
    grad_res_one, grad_attn_gain, grad_attn_shift = pull_one(grad_normed)
    grad_branch_low = grad_res_one.astype(jnp.bfloat16)
    grad_output_weight = matmul_left_t(context_low, grad_branch_low)
    grad_output_bias = column_sums(grad_branch_low)
    grad_context = (
        matmul_right_t(grad_branch_low, output_back).astype(jnp.bfloat16).reshape(tokens.shape)
    )
    key_again, value_again = (
        lax.all_gather(keys_local, SEQ, axis=1, tiled=True),
        lax.all_gather(values_local, SEQ, axis=1, tiled=True),
    )
    grad_query, row_dots, unused_key, unused_value = attend_backward(
        queries, key_again, value_again, same_doc, log_sums, grad_context
    )
    query_all, grad_ctx_all = (
        lax.all_gather(queries, SEQ, axis=1, tiled=True),
        lax.all_gather(grad_context, SEQ, axis=1, tiled=True),
    )
    lse_all, rowdot_all = (
        lax.all_gather(log_sums, SEQ, axis=2, tiled=True),
        lax.all_gather(row_dots, SEQ, axis=2, tiled=True),
    )
    same_doc_t = key_seg[:, :, None] == query_seg[:, None, :]
    grad_key, grad_value = key_side_local(
        query_all, grad_ctx_all, lse_all, rowdot_all, keys_local, values_local, same_doc_t
    )
    grad_query_low = grad_query.reshape(row_count, width).astype(jnp.bfloat16)
    grad_key_low = grad_key.reshape(row_count, width).astype(jnp.bfloat16)
    grad_value_low = grad_value.reshape(row_count, width).astype(jnp.bfloat16)
    grad_query_weight = matmul_left_t(token_rows, grad_query_low)
    grad_query_bias = column_sums(grad_query_low)
    grad_key_weight = matmul_left_t(token_rows, grad_key_low)
    grad_value_weight = matmul_left_t(token_rows, grad_value_low)
    grad_value_bias = column_sums(grad_value_low)
    grad_tokens = (
        grad_res_one
        + matmul_right_t(grad_query_low, query_back)
        + matmul_right_t(grad_key_low, key_back)
        + matmul_right_t(grad_value_low, value_back)
    )
    summed = (
        lax.psum_scatter(grad_query_weight, BOTH, scatter_dimension=0, tiled=True),
        lax.psum_scatter(grad_query_bias, BOTH, scatter_dimension=0, tiled=True),
        lax.psum_scatter(grad_key_weight, BOTH, scatter_dimension=0, tiled=True),
        lax.psum_scatter(grad_value_weight, BOTH, scatter_dimension=0, tiled=True),
        lax.psum_scatter(grad_value_bias, BOTH, scatter_dimension=0, tiled=True),
        lax.psum_scatter(grad_output_weight, BOTH, scatter_dimension=0, tiled=True),
        lax.psum_scatter(grad_output_bias, BOTH, scatter_dimension=0, tiled=True),
        lax.psum_scatter(grad_attn_gain, BOTH, scatter_dimension=0, tiled=True),
        lax.psum_scatter(grad_attn_shift, BOTH, scatter_dimension=0, tiled=True),
        lax.psum_scatter(grad_up_weight, BOTH, scatter_dimension=0, tiled=True),
        lax.psum_scatter(grad_up_bias, BOTH, scatter_dimension=0, tiled=True),
        lax.psum_scatter(grad_down_weight, BOTH, scatter_dimension=0, tiled=True),
        lax.psum_scatter(grad_down_bias, BOTH, scatter_dimension=0, tiled=True),
        lax.psum_scatter(grad_ffn_gain, BOTH, scatter_dimension=0, tiled=True),
        lax.psum_scatter(grad_ffn_shift, BOTH, scatter_dimension=0, tiled=True),
    )
    return (
        mixed,
        grad_tokens.reshape(tokens.shape),
        summed[0],
        summed[1],
        summed[2],
        summed[3],
        summed[4],
        summed[5],
        summed[6],
        summed[7],
        summed[8],
        summed[9],
        summed[10],
        summed[11],
        summed[12],
        summed[13],
        summed[14],
    )


LOG2E = 1.4426950408889634
GROUP_HEADS = 3
GROUP_COLS = GROUP_HEADS * HEAD_DIM
PACK = 640
VECS = 12
SIDE = 16
KEY_CHUNK = 512


def dot_nt(left_op, right_op):
    return lax.dot_general(
        left_op, right_op, (((1,), (1,)), ((), ())), preferred_element_type=jnp.float32
    )


def dot_nn(left_op, right_op):
    return lax.dot_general(
        left_op, right_op, (((1,), (0,)), ((), ())), preferred_element_type=jnp.float32
    )


def attend_kernel(
    query_ref, own_ref, other_ref, seg_key_ref, seg_query_ref, ctx_ref, lse_ref, value_t
):
    half = own_ref.shape[0]
    rows = query_ref.shape[0]

    @pl.when(pl.program_id(0) == 0)
    def _():
        value_t[:, :half] = own_ref[:, GROUP_COLS : 2 * GROUP_COLS].T
        value_t[:, half:] = other_ref[:, GROUP_COLS : 2 * GROUP_COLS].T

    seg_query = seg_query_ref[...]
    chunks = [
        (ref, start) for ref in (own_ref, other_ref) for start in range(0, half, KEY_CHUNK)
    ]
    for head in range(GROUP_HEADS):
        cols = slice(head * HEAD_DIM, (head + 1) * HEAD_DIM)
        query = query_ref[:, cols]
        scores = []
        top = None
        for number, (ref, start) in enumerate(chunks):
            raw = dot_nt(ref[start : start + KEY_CHUNK, cols], query)
            seg_key = seg_key_ref[number * KEY_CHUNK : (number + 1) * KEY_CHUNK, :]
            seg_key = jnp.concatenate([seg_key] * (rows // 128), axis=1)
            masked = jnp.where(seg_key == seg_query, raw * (SCALE * LOG2E), NEG)
            scores.append(masked)
            peak = jnp.max(masked, axis=0, keepdims=True)
            top = peak if top is None else jnp.maximum(top, peak)
        total = None
        context_t = None
        for number in range(len(chunks)):
            weight = jnp.exp2(scores[number] - top)
            part = jnp.sum(weight, axis=0, keepdims=True)
            piece = dot_nn(
                value_t[cols, number * KEY_CHUNK : (number + 1) * KEY_CHUNK],
                weight.astype(jnp.bfloat16),
            )
            total = part if total is None else total + part
            context_t = piece if context_t is None else context_t + piece
        ctx_ref[:, cols] = (context_t / total).T
        lse_ref[head : head + 1, :] = top + jnp.log2(total)


def attend(query, own, other, seg_key, seg_query):
    rows = query.shape[0]
    half = own.shape[0]
    block = rows // 4
    return pl.pallas_call(
        attend_kernel,
        grid=(4,),
        in_specs=[
            pl.BlockSpec((block, GROUP_COLS), lambda i: (i, 0)),
            pl.BlockSpec((half, 2 * GROUP_COLS), lambda i: (0, 0)),
            pl.BlockSpec((half, 2 * GROUP_COLS), lambda i: (0, 0)),
            pl.BlockSpec((2 * half, 128), lambda i: (0, 0)),
            pl.BlockSpec((1, block), lambda i: (0, i)),
        ],
        out_specs=[
            pl.BlockSpec((block, GROUP_COLS), lambda i: (i, 0)),
            pl.BlockSpec((8, block), lambda i: (0, i)),
        ],
        out_shape=[
            jax.ShapeDtypeStruct((rows, GROUP_COLS), jnp.float32),
            jax.ShapeDtypeStruct((8, rows), jnp.float32),
        ],
        scratch_shapes=[pltpu.VMEM((GROUP_COLS, 2 * half), jnp.bfloat16)],
        compiler_params=pltpu.CompilerParams(vmem_limit_bytes=48 * 1024 * 1024),
        cost_estimate=pl.CostEstimate(
            flops=70 * rows * half * GROUP_COLS, bytes_accessed=1024 * 1024, transcendentals=0
        ),
        name="attend",
    )(query, own, other, seg_key, seg_query)


def attend_back_kernel(
    query_ref,
    grad_ref,
    ctx_ref,
    lse_ref,
    own_ref,
    other_ref,
    seg_key_ref,
    seg_query_ref,
    gquery_ref,
    gown_ref,
    gother_ref,
    key_t,
    gother_sum,
):
    half = own_ref.shape[0]
    rows = query_ref.shape[0]
    first = pl.program_id(0) == 0

    @pl.when(first)
    def _():
        key_t[:, :half] = own_ref[:, :GROUP_COLS].T
        key_t[:, half:] = other_ref[:, :GROUP_COLS].T
        gown_ref[...] = jnp.zeros_like(gown_ref)
        gother_sum[...] = jnp.zeros_like(gother_sum)

    seg_query = seg_query_ref[...]
    chunks = [
        (ref, gref, start)
        for ref, gref in ((own_ref, gown_ref), (other_ref, gother_sum))
        for start in range(0, half, KEY_CHUNK)
    ]
    for head in range(GROUP_HEADS):
        cols = slice(head * HEAD_DIM, (head + 1) * HEAD_DIM)
        vcols = slice(GROUP_COLS + head * HEAD_DIM, GROUP_COLS + (head + 1) * HEAD_DIM)
        query = query_ref[:, cols]
        grad = grad_ref[:, cols]
        lse = lse_ref[head : head + 1, :]
        dots = (grad.astype(jnp.float32) * ctx_ref[:, cols]).T
        row_dot = jnp.sum(dots, axis=0, keepdims=True)
        gquery_t = None
        for number, (ref, gref, start) in enumerate(chunks):
            spot = slice(start, start + KEY_CHUNK)
            raw = dot_nt(ref[spot, cols], query)
            seg_key = seg_key_ref[number * KEY_CHUNK : (number + 1) * KEY_CHUNK, :]
            seg_key = jnp.concatenate([seg_key] * (rows // 128), axis=1)
            masked = jnp.where(seg_key == seg_query, raw * (SCALE * LOG2E), NEG)
            probs = jnp.exp2(masked - lse)
            gprobs = dot_nt(ref[spot, vcols], grad)
            gscores = (probs * (gprobs - row_dot)).astype(jnp.bfloat16)
            gref[spot, vcols] += dot_nn(probs.astype(jnp.bfloat16), grad)
            gref[spot, cols] += dot_nn(gscores, query)
            piece = dot_nn(key_t[cols, number * KEY_CHUNK : (number + 1) * KEY_CHUNK], gscores)
            gquery_t = piece if gquery_t is None else gquery_t + piece
        gquery_ref[:, cols] = (SCALE * gquery_t).T.astype(jnp.bfloat16)

    @pl.when(pl.program_id(0) == pl.num_programs(0) - 1)
    def _():
        gother_ref[...] = gother_sum[...].astype(jnp.bfloat16)


def attend_back(query, grad, ctx, lse, own, other, seg_key, seg_query):
    rows = query.shape[0]
    half = own.shape[0]
    block = rows // 4
    return pl.pallas_call(
        attend_back_kernel,
        grid=(4,),
        in_specs=[
            pl.BlockSpec((block, GROUP_COLS), lambda i: (i, 0)),
            pl.BlockSpec((block, GROUP_COLS), lambda i: (i, 0)),
            pl.BlockSpec((block, GROUP_COLS), lambda i: (i, 0)),
            pl.BlockSpec((8, block), lambda i: (0, i)),
            pl.BlockSpec((half, 2 * GROUP_COLS), lambda i: (0, 0)),
            pl.BlockSpec((half, 2 * GROUP_COLS), lambda i: (0, 0)),
            pl.BlockSpec((2 * half, 128), lambda i: (0, 0)),
            pl.BlockSpec((1, block), lambda i: (0, i)),
        ],
        out_specs=[
            pl.BlockSpec((block, GROUP_COLS), lambda i: (i, 0)),
            pl.BlockSpec((half, 2 * GROUP_COLS), lambda i: (0, 0)),
            pl.BlockSpec((half, 2 * GROUP_COLS), lambda i: (0, 0)),
        ],
        out_shape=[
            jax.ShapeDtypeStruct((rows, GROUP_COLS), jnp.bfloat16),
            jax.ShapeDtypeStruct((half, 2 * GROUP_COLS), jnp.float32),
            jax.ShapeDtypeStruct((half, 2 * GROUP_COLS), jnp.bfloat16),
        ],
        scratch_shapes=[
            pltpu.VMEM((GROUP_COLS, 2 * half), jnp.bfloat16),
            pltpu.VMEM((half, 2 * GROUP_COLS), jnp.float32),
        ],
        compiler_params=pltpu.CompilerParams(vmem_limit_bytes=48 * 1024 * 1024),
        cost_estimate=pl.CostEstimate(
            flops=100 * rows * half * GROUP_COLS, bytes_accessed=1024 * 1024, transcendentals=0
        ),
        name="attend_back",
    )(query, grad, ctx, lse, own, other, seg_key, seg_query)


def prepare_kernel(
    tokens_ref,
    lengths_ref,
    key_ref,
    value_ref,
    query_ref,
    qbias_ref,
    vbias_ref,
    obias_ref,
    again_ref,
    ashift_ref,
    dbias_ref,
    fgain_ref,
    fshift_ref,
    ubias_ref,
    output_ref,
    up_ref,
    down_ref,
    first_ref,
    second_ref,
    bulk_ref,
    *piece_refs,
):
    place = lax.axis_index(SEQ)
    odd = lax.rem(place // 4, 2) == 1
    quad = lax.rem(place, 4)
    first_ref[...] = jnp.where(odd, tokens_ref[1], tokens_ref[0])
    second_ref[...] = jnp.where(odd, tokens_ref[0], tokens_ref[1])
    own_rows, width = key_ref.shape
    ratio = up_ref.shape[1] // width
    bulk_ref[0, :own_rows] = output_ref[...]
    for number in range(ratio):
        bulk_ref[0, (1 + number) * own_rows : (2 + number) * own_rows] = up_ref[
            :, number * width : (number + 1) * width
        ]
    bulk_ref[0, (1 + ratio) * own_rows :] = down_ref[...]
    small = (qbias_ref, vbias_ref, obias_ref, again_ref, ashift_ref, dbias_ref, fgain_ref, fshift_ref)
    rows = [ref[...].astype(jnp.float32) for ref in small]
    wide = ubias_ref[...].astype(jnp.float32)
    rows += [wide[:, n * own_rows : (n + 1) * own_rows] for n in range(VECS - len(small))]
    lengths = lengths_ref[...]
    docs = lengths.shape[1]
    flat = jnp.concatenate(
        [lengths[0:1], lengths[1:2], jnp.zeros((1, own_rows - 2 * docs), jnp.int32)], axis=1
    )
    rows += [(flat >> 6).astype(jnp.float32), (flat & 63).astype(jnp.float32)]
    rows += [jnp.zeros_like(rows[0])] * (SIDE - len(rows))
    side = jnp.concatenate(rows, axis=0).T.astype(jnp.bfloat16)
    cut = 3 * GROUP_COLS
    for flip, piece_ref in enumerate(piece_refs):
        piece_ref[...] = jnp.zeros_like(piece_ref)
        piece_ref[:, cut : cut + SIDE] = side
        target = quad ^ flip
        for number in range(4):

            @pl.when(target == number)
            def _():
                cols = slice(number * GROUP_COLS, (number + 1) * GROUP_COLS)
                for spot, ref in enumerate((key_ref, value_ref, query_ref)):
                    piece_ref[:, spot * GROUP_COLS : (spot + 1) * GROUP_COLS] = ref[:, cols]


def prepare(tokens, lengths, key, value, query, vectors, up_bias, output, up, down):
    own_rows, width = key.shape
    bulk_rows = own_rows + down.shape[0] * 2
    turn_shape = jax.ShapeDtypeStruct(tokens.shape[1:], jnp.bfloat16)
    piece_shape = jax.ShapeDtypeStruct((own_rows, PACK), jnp.bfloat16)
    return pl.pallas_call(
        prepare_kernel,
        out_shape=[turn_shape] * 2
        + [jax.ShapeDtypeStruct((1, bulk_rows, width), jnp.bfloat16)]
        + [piece_shape] * 4,
        name="prepare",
    )(
        tokens,
        lengths,
        key,
        value,
        query,
        *[item.reshape(1, own_rows) for item in vectors],
        up_bias.reshape(1, up_bias.shape[0]),
        output,
        up,
        down,
    )


def tied(values, *others):
    return lax.optimization_barrier((values, others))[0]


def block_of(values, index, axis):
    return lax.dynamic_index_in_dim(values, index, axis=axis, keepdims=False)


def halves(values, bit, axis):
    return (block_of(values, bit, axis), block_of(values, 1 - bit, axis))


def low_sum(own, arrived):
    return (own.astype(jnp.float32) + arrived.astype(jnp.float32)).astype(jnp.bfloat16)


def sum_parts(own, arrived):
    total = own.astype(jnp.float32)
    for item in arrived:
        total = total + item.astype(jnp.float32)
    return total


def device_table(mapping):
    pairs = []
    for core in range(2):
        for layer_z in range(4):
            for quad in range(4):
                to_core, to_z, to_quad = mapping(core, layer_z, quad)
                pairs.append((core * 16 + layer_z * 4 + quad, to_core * 16 + to_z * 4 + to_quad))
    return pairs


def hop(value, mapping):
    return lax.ppermute(value, BOTH, device_table(mapping))


def hop_quad(value, flip):
    return hop(value, lambda core, layer_z, quad: (core, layer_z, quad ^ flip))


def hop_layer(value, flip):
    return hop(value, lambda core, layer_z, quad: (core, layer_z ^ flip, quad))


def hop_core(value):
    return hop(value, lambda core, layer_z, quad: (1 - core, layer_z, quad))


def to_sequence(value, turn):
    return hop(
        value,
        lambda core, layer_z, quad: (layer_z // 2, 2 * core + (layer_z + turn) % 2, quad),
    )


def to_owner(value, turn):
    return hop(
        value,
        lambda core, layer_z, quad: (layer_z // 2, 2 * core + (layer_z - turn) % 2, quad),
    )


def turned(blocks, quad):
    first, second, third, fourth = blocks
    odd = quad % 2 == 1
    high = quad // 2 == 1
    pairs = (
        jnp.where(odd, second, first),
        jnp.where(odd, first, second),
        jnp.where(odd, fourth, third),
        jnp.where(odd, third, fourth),
    )
    return (
        jnp.where(high, pairs[2], pairs[0]),
        jnp.where(high, pairs[3], pairs[1]),
        jnp.where(high, pairs[0], pairs[2]),
        jnp.where(high, pairs[1], pairs[3]),
    )


def pack_grads(main, vecs):
    coarse = vecs.astype(jnp.bfloat16)
    fine = (vecs - coarse.astype(jnp.float32)).astype(jnp.bfloat16)
    filler = jnp.zeros(main.shape[:-1] + (PACK - main.shape[-1] - 2 * VECS,), jnp.bfloat16)
    return jnp.concatenate([main.astype(jnp.bfloat16), coarse, fine, filler], axis=-1)


def unpack_grads(packed):
    wide = packed.astype(jnp.float32)
    cut = 3 * GROUP_COLS
    return (wide[..., :cut], wide[..., cut : cut + VECS] + wide[..., cut + VECS : cut + 2 * VECS])


def add_packed(own, arrived):
    main, vecs = unpack_grads(own)
    more, more_vecs = unpack_grads(arrived)
    return (main + more, vecs + more_vecs)


def shards_heads(
    tokens,
    doc_lengths,
    query_weight,
    query_bias,
    key_weight,
    value_weight,
    value_bias,
    output_weight,
    output_bias,
    attn_gain,
    attn_shift,
    up_weight,
    up_bias,
    down_weight,
    down_bias,
    ffn_gain,
    ffn_shift,
    cotangent,
):
    groups, stretch, width = tokens.shape
    own_rows = query_weight.shape[0]
    hidden = up_weight.shape[1]
    ratio = hidden // width
    devices = width // own_rows
    bulk_rows = own_rows * (1 + 2 * ratio)
    row_count = groups * stretch
    core = lax.axis_index(BATCH)
    place = lax.axis_index(SEQ)
    layer_z = place // 4
    quad = place % 4
    parity = layer_z % 2
    flips = (1, 2, 3)
    bit_x, bit_y = (quad % 2, quad // 2)
    bit_low, bit_high = (layer_z % 2, layer_z // 2)

    vectors = (
        query_bias,
        value_bias,
        output_bias,
        attn_gain,
        attn_shift,
        down_bias,
        ffn_gain,
        ffn_shift,
    )
    first_turn, second_turn, bulk, *pieces = prepare(
        tokens,
        doc_lengths,
        key_weight,
        value_weight,
        query_weight,
        vectors,
        up_bias,
        output_weight,
        up_weight,
        down_weight,
    )

    own_block = jnp.concatenate(
        [to_sequence(first_turn, 0), to_sequence(second_turn, 1)], axis=0
    )
    token_half = jnp.concatenate(
        [own_block] + [hop_quad(own_block, flip) for flip in flips], axis=0
    )

    quads = turned([pieces[0]] + [hop_quad(pieces[flip], flip) for flip in flips], quad)
    quads = jnp.stack(quads, axis=0)
    layers = [quads] + [hop_layer(quads, flip) for flip in flips]
    layers = jnp.stack(turned(layers, layer_z), axis=0)
    twin = hop_core(layers)
    cores = jnp.stack([jnp.where(core == 0, layers, twin), jnp.where(core == 0, twin, layers)])
    packed = cores.reshape(width, PACK)
    group_weight = packed[:, : 3 * GROUP_COLS]
    side = packed[:, 3 * GROUP_COLS : 3 * GROUP_COLS + SIDE].astype(jnp.float32)
    vector_rows = side[:, :8].T
    up_bias_full = side[:, 8:VECS].reshape(devices, own_rows, ratio)
    up_bias_full = jnp.swapaxes(up_bias_full, 1, 2).reshape(1, hidden)
    (
        qbias_full,
        vbias_full,
        obias_full,
        again_full,
        ashift_full,
        dbias_full,
        fgain_full,
        fshift_full,
    ) = [vector_rows[number] for number in range(8)]
    docs = doc_lengths.shape[1]
    digits = side.reshape(2, width // 2, SIDE)[:, : groups * docs, VECS : VECS + 2]
    lengths_all = (digits[..., 0] * 64 + digits[..., 1]).astype(jnp.int32)
    lengths = lax.dynamic_index_in_dim(
        lengths_all.reshape(2 * groups, docs), layer_z, axis=0, keepdims=False
    )
    doc_ends = jnp.cumsum(lengths)

    def half_segments(which):
        turn_z = jnp.stack([(layer_z - turn) % 2 for turn in (0, 1)]) + 2 * which
        spot = jnp.stack([quad ^ flip for flip in range(4)])
        start = turn_z[None, :] * (4 * stretch) + spot[:, None] * stretch
        positions = start[:, :, None] + jnp.arange(stretch, dtype=jnp.int32)
        positions = positions.reshape(-1)
        return jnp.sum((positions[:, None] >= doc_ends[None, :]).astype(jnp.int32), axis=-1)

    seg_query = half_segments(core)
    seg_key = jnp.concatenate([seg_query, half_segments(1 - core)])
    seg_key = jnp.broadcast_to(seg_key[:, None], (seg_key.shape[0], 128))
    seg_query = seg_query[None, :]

    bulk_all = lax.all_gather(bulk, BOTH, axis=0, tiled=True)

    column_bias = jnp.concatenate(
        [
            jnp.zeros((GROUP_COLS,), jnp.float32),
            lax.dynamic_slice_in_dim(vbias_full, quad * GROUP_COLS, GROUP_COLS),
            lax.dynamic_slice_in_dim(qbias_full, quad * GROUP_COLS, GROUP_COLS),
        ]
    )
    projected = (matmul_plain(token_half, group_weight) + column_bias).astype(jnp.bfloat16)
    own_pair = projected[:, : 2 * GROUP_COLS]
    queries = projected[:, 2 * GROUP_COLS :]
    other_pair = hop_core(own_pair)
    ctx_wide, lse = attend(queries, own_pair, other_pair, seg_key, seg_query)

    ctx_blocks = ctx_wide.astype(jnp.bfloat16).reshape(4, row_count, GROUP_COLS)
    ctx_groups = [ctx_blocks[0]] + [hop_quad(ctx_blocks[flip], flip) for flip in flips]
    ctx_merged = jnp.concatenate(turned(ctx_groups, quad), axis=1)
    ctx_turns = [
        to_owner(ctx_merged[turn * stretch : (turn + 1) * stretch], turn) for turn in (0, 1)
    ]
    context_low = jnp.concatenate(
        [
            jnp.where(parity == 0, ctx_turns[0], ctx_turns[1]),
            jnp.where(parity == 0, ctx_turns[1], ctx_turns[0]),
        ],
        axis=0,
    )

    output_full = bulk_all[:, :own_rows].reshape(width, width)
    up_parts = [
        bulk_all[:, (1 + number) * own_rows : (2 + number) * own_rows].reshape(width, width)
        for number in range(ratio)
    ]
    up_full = jnp.concatenate(up_parts, axis=1)
    down_full = bulk_all[:, (1 + ratio) * own_rows :].reshape(hidden, width)

    token_rows = tokens.reshape(row_count, width)
    res_one = token_rows.astype(jnp.float32) + matmul_plain(context_low, output_full) + obias_full
    normed, pull_one = jax.vjp(norm_apply, res_one, again_full, ashift_full)
    normed_low = normed.astype(jnp.bfloat16)
    up_pre = matmul_plain(normed_low, up_full) + up_bias_full
    activated, pull_gelu = jax.vjp(gelu_exact, up_pre)
    act_low = activated.astype(jnp.bfloat16)
    res_two = normed + matmul_plain(act_low, down_full) + dbias_full
    output_rows, pull_two = jax.vjp(norm_apply, res_two, fgain_full, fshift_full)
    mixed = output_rows.astype(jnp.bfloat16).reshape(tokens.shape)
    grad_out = cotangent.astype(jnp.float32).reshape(row_count, width)
    grad_res_two, grad_ffn_gain, grad_ffn_shift = pull_two(grad_out)
    grad_down_low = grad_res_two.astype(jnp.bfloat16)

    def half_columns(matrix, which):
        half = matrix.shape[1] // 2
        return lax.dynamic_slice_in_dim(matrix, which * half, half, axis=1)

    def down_term(which):
        return matmul_left_t(half_columns(act_low, which), grad_down_low)

    def branch_term(which):
        return matmul_left_t(half_columns(normed_low, which), grad_up_low)

    def out_term(which):
        return matmul_left_t(half_columns(context_low, which), grad_branch_low)

    down_theirs = down_term(1 - core).astype(jnp.bfloat16)
    down_arrived = hop_core(down_theirs)
    (grad_up_pre,) = pull_gelu(matmul_right_t(tied(grad_down_low, down_theirs), down_full))
    grad_up_low = grad_up_pre.astype(jnp.bfloat16)
    grad_normed = grad_res_two + matmul_right_t(grad_up_low, up_full)
    grad_res_one, grad_attn_gain, grad_attn_shift = pull_one(grad_normed)
    grad_branch_low = grad_res_one.astype(jnp.bfloat16)
    grad_context = matmul_right_t(grad_branch_low, output_full).astype(jnp.bfloat16)
    branch_arrived = hop_core(branch_term(1 - core).astype(jnp.bfloat16))
    out_arrived = hop_core(out_term(1 - core).astype(jnp.bfloat16))

    low_part = grad_context[:stretch]
    high_part = grad_context[stretch:]
    grad_turns = [
        to_sequence(jnp.where((parity + turn) % 2 == 1, high_part, low_part), turn)
        for turn in (0, 1)
    ]
    down_total = (down_term(core) + down_arrived.astype(jnp.float32)).astype(jnp.bfloat16)
    down_total = down_total.reshape(2, 2, 2, 2, ratio * own_rows, width)
    branch_total = (branch_term(core) + branch_arrived.astype(jnp.float32)).astype(jnp.bfloat16)
    branch_total = branch_total.reshape(2, 2, 2, 2, own_rows, hidden)
    out_total = low_sum(out_term(core), out_arrived).reshape(2, 2, 2, 2, own_rows, width)
    grad_turns = tied(grad_turns, down_total, branch_total, out_total)
    grad_own = jnp.concatenate(grad_turns, axis=0)
    grad_columns = turned(
        [grad_own[:, n * GROUP_COLS : (n + 1) * GROUP_COLS] for n in range(4)], quad
    )
    grad_ctx = jnp.concatenate(
        [grad_columns[0]] + [hop_quad(grad_columns[flip], flip) for flip in flips], axis=0
    )

    down_own, down_send = tied(halves(down_total, bit_x, 3), grad_ctx)
    branch_own, branch_send = tied(halves(branch_total, bit_y, 2), grad_ctx)
    down_arrived = hop_quad(down_send, 1)
    branch_arrived = hop_quad(branch_send, 2)
    out_own, out_send = tied(halves(out_total, bit_low, 1), grad_ctx)
    out_arrived = hop_layer(out_send, 1)

    grad_query, grad_own_pair, grad_other_pair = attend_back(
        tied(queries, down_send, branch_send, out_send),
        grad_ctx,
        ctx_wide,
        lse,
        own_pair,
        other_pair,
        seg_key,
        seg_query,
    )
    pair_arrived = hop_core(grad_other_pair)
    down_arrived, branch_arrived, out_arrived = tied(
        (down_arrived, branch_arrived, out_arrived), grad_other_pair
    )
    out_own, out_send = halves(low_sum(out_own, out_arrived), bit_high, 0)
    out_arrived = hop_layer(out_send, 2)
    down_own, down_send = halves(low_sum(down_own, down_arrived), bit_y, 2)
    branch_own, branch_send = halves(low_sum(branch_own, branch_arrived), bit_x, 2)
    down_arrived = hop_quad(down_send, 2)
    branch_arrived = hop_quad(branch_send, 1)
    pair_total = grad_own_pair + tied(pair_arrived, down_send, branch_send, out_send).astype(
        jnp.float32
    )
    pair_scale = jnp.where(jnp.arange(2 * GROUP_COLS) < GROUP_COLS, SCALE, 1.0)
    grad_projected = jnp.concatenate(
        [(pair_total * pair_scale).astype(jnp.bfloat16), grad_query], axis=1
    )
    grad_half = matmul_right_t(grad_projected, group_weight)
    half_blocks = grad_half.reshape(4, row_count, width)
    low_blocks = half_blocks.astype(jnp.bfloat16)
    low_blocks, down_arrived, branch_arrived, out_arrived = tied(
        (low_blocks, down_arrived, branch_arrived, out_arrived)
    )
    token_arrived = [hop_quad(low_blocks[flip], flip) for flip in flips]
    down_own, down_send = halves(low_sum(down_own, down_arrived), bit_low, 1)
    branch_own, branch_send = halves(low_sum(branch_own, branch_arrived), bit_low, 1)
    down_arrived = hop_layer(down_send, 1)
    out_own, out_send = halves(low_sum(out_own, out_arrived), bit_x, 1)
    up_sums, out_sums, down_sums, again_sums, ashift_sums, fgain_sums, fshift_sums = tied(
        (
            column_sums(grad_up_low),
            column_sums(grad_branch_low),
            column_sums(grad_down_low),
            grad_attn_gain,
            grad_attn_shift,
            grad_ffn_gain,
            grad_ffn_shift,
        ),
        low_blocks,
    )

    grad_projected = tied(grad_projected, low_blocks)
    grad_group = matmul_left_t(token_half, grad_projected)
    bias_sums = column_sums(grad_projected)
    nothing = jnp.zeros((width,), jnp.float32)
    vec_rows = jnp.stack(
        [
            lax.dynamic_update_slice_in_dim(
                nothing, bias_sums[2 * GROUP_COLS :], quad * GROUP_COLS, 0
            ),
            lax.dynamic_update_slice_in_dim(
                nothing, bias_sums[GROUP_COLS : 2 * GROUP_COLS], quad * GROUP_COLS, 0
            ),
            out_sums,
            again_sums,
            ashift_sums,
            down_sums,
            fgain_sums,
            fshift_sums,
        ],
        axis=0,
    ).T
    up_sums = up_sums.reshape(devices, ratio, own_rows)
    up_sums = jnp.swapaxes(up_sums, 1, 2).reshape(width, ratio)
    vecs = jnp.concatenate([vec_rows, up_sums], axis=1)
    packed_grads = pack_grads(grad_group, vecs).reshape(2, width // 2, PACK)
    mine = jnp.where(core == 0, packed_grads[0], packed_grads[1])
    theirs = jnp.where(core == 0, packed_grads[1], packed_grads[0])
    pack_arrived = hop_core(theirs)
    packed_grads = pack_grads(*add_packed(mine, pack_arrived))
    branch_arrived = hop_layer(tied(branch_send, pack_arrived), 1)
    packed_grads = packed_grads.reshape(2, 2, 4 * own_rows, PACK)
    pack_own, pack_send = halves(packed_grads, bit_low, 1)
    pack_arrived = hop_layer(pack_send, 1)

    down_own, down_send = halves(low_sum(down_own, down_arrived), bit_high, 0)
    down_arrived = hop_layer(down_send, 2)
    branch_own, branch_send = halves(low_sum(branch_own, branch_arrived), bit_high, 0)
    branch_arrived = hop_layer(branch_send, 2)
    token_arrived = tied(token_arrived, down_send, branch_send, pack_send)
    grad_block = sum_parts(half_blocks[0], token_arrived).astype(jnp.bfloat16)
    home = [
        to_owner(grad_block[turn * stretch : (turn + 1) * stretch], turn) for turn in (0, 1)
    ]
    pack_arrived, down_arrived = tied((pack_arrived, down_arrived), grad_block)
    packed_grads = pack_grads(*add_packed(pack_own, pack_arrived))
    pack_own, pack_send = halves(packed_grads, bit_high, 0)
    pack_arrived = hop_layer(pack_send, 2)
    out_arrived = hop_quad(tied(out_send, pack_send), 1)
    home, pack_arrived, out_arrived = tied((home, pack_arrived, out_arrived))
    out_own, out_send = halves(low_sum(out_own, out_arrived), bit_y, 0)
    out_arrived = hop_quad(out_send, 2)
    packed_grads = pack_grads(*add_packed(pack_own, pack_arrived)).reshape(4, own_rows, PACK)
    by_quad = turned([packed_grads[number] for number in range(4)], quad)
    main, vecs = unpack_grads(by_quad[0])
    home_rows = jnp.concatenate(
        [
            jnp.where(parity == 0, home[0], home[1]),
            jnp.where(parity == 0, home[1], home[0]),
        ],
        axis=0,
    )
    grad_tokens = (grad_res_one + home_rows.astype(jnp.float32)).reshape(tokens.shape)

    quad_parts = [main]
    for flip in flips:
        more, more_vecs = unpack_grads(hop_quad(by_quad[flip], flip))
        quad_parts.append(more)
        vecs = vecs + more_vecs
    quad_parts = turned(quad_parts, quad)
    sum_key, sum_value, sum_query = [
        jnp.concatenate(
            [part[:, n * GROUP_COLS : (n + 1) * GROUP_COLS] for part in quad_parts], axis=1
        )
        for n in range(3)
    ]
    sum_rows = vecs[:, :8].T
    sum_down = sum_parts(down_own, [down_arrived])
    sum_up = sum_parts(branch_own, [branch_arrived])
    sum_output = sum_parts(out_own, [out_arrived])
    return (
        mixed,
        grad_tokens,
        sum_query,
        sum_rows[0],
        sum_key,
        sum_value,
        sum_rows[1],
        sum_output,
        sum_rows[2],
        sum_rows[3],
        sum_rows[4],
        sum_up,
        vecs[:, 8:].T.reshape(up_bias.shape),
        sum_down,
        sum_rows[5],
        sum_rows[6],
        sum_rows[7],
    )


def solution(mesh):
    in_specs = (
        P(BATCH, SEQ, None),
        P(BATCH, None),
        P(BOTH, None),
        P(BOTH),
        P(BOTH, None),
        P(BOTH, None),
        P(BOTH),
        P(BOTH, None),
        P(BOTH),
        P(BOTH),
        P(BOTH),
        P(BOTH, None),
        P(BOTH),
        P(BOTH, None),
        P(BOTH),
        P(BOTH),
        P(BOTH),
        P(BATCH, SEQ, None),
    )
    out_specs = (
        P(BATCH, SEQ, None),
        P(BATCH, SEQ, None),
        P(BOTH, None),
        P(BOTH),
        P(BOTH, None),
        P(BOTH, None),
        P(BOTH),
        P(BOTH, None),
        P(BOTH),
        P(BOTH),
        P(BOTH),
        P(BOTH, None),
        P(BOTH),
        P(BOTH, None),
        P(BOTH),
        P(BOTH),
        P(BOTH),
    )
    fits = mesh.shape[BATCH] == 2 and mesh.shape[SEQ] == 16
    body = shards_heads if fits else shards_general
    return jax.shard_map(body, mesh=mesh, in_specs=in_specs, out_specs=out_specs, check_vma=False)
```
